32 devices in a mesh: slab: 8 (over y, x, core), sub: 4 (over z).
Axes of the slice: x: 2, y: 2, z: 4, core: 2. Of those that a mesh axis runs over, the one named last changes fastest.
Arguments:
- positions: float32 [3, 32768], P(None, 'slab'), may hold values from 0 to 33, as said below
- velocity: float32 [3, 32768], P(None, 'slab'), may hold values from -6 to 6
- density: float32 [32768], P('slab'), may hold values from 0.1 to 10
- pressure: float32 [32768], P('slab'), may hold values from 0.1 to 10
- counts: int32 [256], P('slab'), may hold values from 8 to 128, as said below
- pair_list: int32 [3, 1280], P(None, ('slab', 'sub')), may hold values from -32 to 255, as said below
Outputs:
- rates: float32 [5, 32768], P(None, 'slab')
The draws below stay inside these ranges and needn't reach their ends.
Inputs may be any that keep to these rules, and one draw needn't show every extreme that they name: `positions`: particle k of leaf g lies in slab floor(g / 32) along x (x minus that index in [0, 1)), in column g mod 32 along y (likewise), and z in [0, 1). `counts`: at least 8 live particles a leaf; some leaf holds 128. `pair_list`: row 0 is a slot's home leaf, a leaf of this device's part of its slab (columns 8 * i to 8 * i + 7 on the device of index i along sub), or -1 for an empty slot. Row 1 is the other leaf, -1 for an empty slot: the home leaf itself, the leaf of the next column cyclically in the same slab, or a leaf of the next slab cyclically whose column is the home column - 1, + 0 or + 1 plus w, modulo 32; w is 0 for home leaves outside the last slab and one shift common to all pairs headed in the last slab. Row 2 is the image offset along y in units of cell width, 0 for an empty slot and for a pair of a leaf with itself; for a pair into the next slab, minus row 2 modulo 32 equals w. A leaf heads at most 5 pairs, each device holds at most 40 live slots, and some device holds exactly that many.
All inputs are finite; a program needn't handle non-finite values.
Results may differ from the reference program's by a relative error of at most 0.0003.
Values sent between devices are 32-bit elements; how exact they have to be, the bound alone decides.
No kernel may reach another device: no remote copies, remote signals or barrier semaphores. Data moves between devices by JAX's collectives and lax.ppermute only.
A program may use at most 64 MiB of HBM per device.

```python
import math
import jax
import jax.numpy as jnp
from jax import lax

LEAF = 128
CAND = 5
LEAF_SUB = 8
SLAB_LEAVES = 32
LEAVES = 256
PARTICLES = 32768
PAIR_SUB = 40
PAIRS = 1280


def draw_positions(key, part):
    particle = jnp.arange(PARTICLES, dtype=jnp.int32)
    leaf_index = particle // LEAF
    slab_coord = (leaf_index // SLAB_LEAVES).astype(jnp.float32)
    column = (leaf_index % SLAB_LEAVES).astype(jnp.float32)
    spread = jax.random.uniform(key, (3, PARTICLES), jnp.float32)
    return jnp.stack([slab_coord + spread[0], column + spread[1], spread[2]]).astype(jnp.float32)


def draw_counts(key, part):
    groups = LEAVES // LEAF_SUB
    level_key, count_key, peak_key = jax.random.split(jax.random.fold_in(key, 11), 3)
    levels = jax.random.randint(level_key, (groups,), 0, 3)
    floors = jnp.array([8, 48, 112], jnp.int32)[levels]
    floors = jnp.repeat(floors, LEAF_SUB)
    drawn_counts = jax.random.randint(count_key, (LEAVES,), floors, LEAF + 1)
    peak_leaf = jax.random.randint(peak_key, (), 0, LEAVES)
    return jnp.where(jnp.arange(LEAVES, dtype=jnp.int32) == peak_leaf, LEAF, drawn_counts).astype(jnp.int32)


def draw_pair_list(key, part):
    devices = LEAVES // LEAF_SUB
    slab_total = LEAVES // SLAB_LEAVES
    core_total = SLAB_LEAVES // LEAF_SUB
    shear_key, level_key, keep_key, full_key, order_key = jax.random.split(jax.random.fold_in(key, 23), 5)
    shear_cells = jax.random.randint(shear_key, (), LEAF_SUB, SLAB_LEAVES)
    device = jnp.arange(devices, dtype=jnp.int32)[:, None, None]
    local_leaf = jnp.arange(LEAF_SUB, dtype=jnp.int32)[None, :, None]
    candidate = jnp.arange(CAND, dtype=jnp.int32)[None, None, :]
    slab_of = device // core_total
    column = device % core_total * LEAF_SUB + local_leaf
    home_leaf = slab_of * SLAB_LEAVES + column
    same_column = (column + 1) % SLAB_LEAVES
    same_other = slab_of * SLAB_LEAVES + same_column
    same_offset = column + 1 - same_column
    next_slab = (slab_of + 1) % slab_total
    wrapped = (slab_of == slab_total - 1).astype(jnp.int32)
    target = column + candidate - 3
    next_column = (target + wrapped * shear_cells) % SLAB_LEAVES
    next_other = next_slab * SLAB_LEAVES + next_column
    next_offset = target - next_column
    other_leaf = jnp.where(candidate == 0, home_leaf, jnp.where(candidate == 1, same_other, next_other))
    offset = jnp.where(candidate == 0, 0, jnp.where(candidate == 1, same_offset, next_offset))
    levels = jax.random.randint(level_key, (devices, 1, 1), 0, 5)
    full_device = jax.random.randint(full_key, (), 0, devices)
    levels = jnp.where(device == full_device, 4, levels)
    kept_pair = (jax.random.randint(keep_key, (devices, LEAF_SUB, CAND), 0, 4) < levels) | (candidate < 2)
    shape = (devices, LEAF_SUB, CAND)
    pair_rows = jnp.stack([jnp.where(kept_pair, jnp.broadcast_to(home_leaf, shape), -1), jnp.where(kept_pair, jnp.broadcast_to(other_leaf, shape), -1), jnp.where(kept_pair, jnp.broadcast_to(offset, shape), 0)])
    flattened = pair_rows.reshape(3, devices, LEAF_SUB * CAND)
    order_keys = jax.random.split(order_key, devices)
    shuffles = jax.vmap(lambda one_key: jax.random.permutation(one_key, LEAF_SUB * CAND))(order_keys)
    shuffled = jnp.take_along_axis(flattened, shuffles[None].astype(jnp.int32), axis=2)
    return shuffled.reshape(3, devices * LEAF_SUB * CAND).astype(jnp.int32)


def shard_levels(own_key, dims, cuts, smallest, largest):
    def one(dim, shards_of):
        draws = jax.random.uniform(jax.random.fold_in(jax.random.fold_in(own_key, 6), dim), (shards_of,), jnp.float32, smallest / len(cuts), largest / len(cuts))
        return jnp.repeat(jnp.exp(draws), dims[dim] // shards_of).reshape((-1,) + (1,) * (len(dims) - dim - 1))

    level = one(*cuts[0])
    for cut in cuts[1:]:
        level = level * one(*cut)
    return level


def centred(stream_key, extent, width, most, cuts=(), held_as=jnp.bfloat16):
    entries = jax.random.normal(stream_key, extent, jnp.float32) * width
    if len(cuts) > 0:
        entries = shard_levels(stream_key, extent, cuts, -0.22, 0.18) * entries
    return jnp.clip(entries, min=-most, max=most).astype(held_as)


def setup_inputs(seed: int = 0) -> dict:
    arg_keys = jax.random.split(jax.random.key(seed), 7)
    positions = draw_positions(jax.random.fold_in(arg_keys[6], 71), 0)
    velocity = centred(arg_keys[1], (3, PARTICLES), 1.0, 6.0, ((1, 8),), jnp.float32)
    density = jnp.clip(jnp.exp(math.log(10.0) - 4.6051702 * jax.random.uniform(arg_keys[2], (PARTICLES,), jnp.float32) ** shard_levels(arg_keys[2], (PARTICLES,), ((0, 8),), -0.2, 0.2)), 0.1, 10.0)
    pressure = jnp.clip(jnp.exp(math.log(10.0) - 4.6051702 * jax.random.uniform(arg_keys[3], (PARTICLES,), jnp.float32) ** shard_levels(arg_keys[3], (PARTICLES,), ((0, 8),), -0.2, 0.2)), 0.1, 10.0)
    counts = draw_counts(jax.random.fold_in(arg_keys[6], 71), 0)
    pair_list = draw_pair_list(jax.random.fold_in(arg_keys[6], 71), 0)
    return {"positions": positions, "velocity": velocity, "density": density, "pressure": pressure, "counts": counts, "pair_list": pair_list}


GAMMA = 5.0 / 3.0
SUPPORT = 1.5
KERNEL_NORM = 21.0 / (2.0 * math.pi * SUPPORT ** 3)
MOMENT_REG = 0.05
SHEAR_SPEED = 1.0
AREA_FLOOR = 0.0001
SYM_PAIRS = ((0, 0), (0, 1), (0, 2), (1, 1), (1, 2), (2, 2))
UNIT_DIAG = (1.0, 0.0, 0.0, 1.0, 0.0, 1.0)

def kernel(dist_sq):
    scaled = jnp.sqrt(dist_sq) / SUPPORT
    inside = jnp.maximum(1.0 - scaled, 0.0)
    return KERNEL_NORM * inside ** 4 * (1.0 + 4.0 * scaled)

def image_rows(tile, wrapped, offset, box_length):
    zero_row = jnp.zeros_like(offset)
    displace = jnp.stack([wrapped * box_length, offset, zero_row, zero_row, -SHEAR_SPEED * wrapped, zero_row, zero_row, zero_row])
    return tile + displace[:, :, None]

def sym_apply(matrix, vector):
    comp_x = matrix[0] * vector[0] + matrix[1] * vector[1] + matrix[2] * vector[2]
    comp_y = matrix[1] * vector[0] + matrix[3] * vector[1] + matrix[4] * vector[2]
    comp_z = matrix[2] * vector[0] + matrix[4] * vector[1] + matrix[5] * vector[2]
    return [comp_x, comp_y, comp_z]

def sym_inverse(matrix):
    entry_xx, entry_xy, entry_xz, entry_yy, entry_yz, entry_zz = matrix
    minor_xx = entry_yy * entry_zz - entry_yz * entry_yz
    minor_xy = entry_xz * entry_yz - entry_xy * entry_zz
    minor_xz = entry_xy * entry_yz - entry_xz * entry_yy
    minor_yy = entry_xx * entry_zz - entry_xz * entry_xz
    minor_yz = entry_xy * entry_xz - entry_xx * entry_yz
    minor_zz = entry_xx * entry_yy - entry_xy * entry_xy
    determinant = entry_xx * minor_xx + entry_xy * minor_xy + entry_xz * minor_xz
    return [minor / determinant for minor in (minor_xx, minor_xy, minor_xz, minor_yy, minor_yz, minor_zz)]

def moment_tile(near_tile, far_tile, mask_near, mask_far, weight):
    separation = [far_tile[direction][:, None, :] - near_tile[direction][:, :, None] for direction in range(3)]
    dist_sq = separation[0] * separation[0] + separation[1] * separation[1] + separation[2] * separation[2]
    smoothing = kernel(dist_sq) * mask_near[:, :, None] * mask_far[:, None, :] * weight[:, None, None]
    summands = [smoothing] + [smoothing * separation[left_axis] * separation[right_axis] for left_axis, right_axis in SYM_PAIRS]
    for quantity in range(5):
        weighted = smoothing * (far_tile[3 + quantity][:, None, :] - near_tile[3 + quantity][:, :, None])
        summands = summands + [weighted * separation[direction] for direction in range(3)]
    row_sums = jnp.stack([lax.optimization_barrier(jnp.sum(summand, axis=2)) for summand in summands])
    col_sums = jnp.stack([lax.optimization_barrier(jnp.sum(summand, axis=1)) for summand in summands])
    return (row_sums, col_sums)

def finish_moments(moments, live_mask):
    number_density = moments[0] + 1.0 - live_mask
    inverse_density = 1.0 / number_density
    second = [moments[1 + position] * inverse_density + MOMENT_REG * UNIT_DIAG[position] for position in range(6)]
    inverse = sym_inverse(second)
    slopes = []
    for quantity in range(5):
        numerator = [moments[7 + 3 * quantity + direction] * inverse_density for direction in range(3)]
        slopes = slopes + sym_apply(inverse, numerator)
    return jnp.stack([number_density] + inverse + slopes)

def side_flux(density_side, velocity_side, pressure_side, normal, normal_speed, lag_speed, wave_speed, contact):
    energy = pressure_side / (GAMMA - 1.0) + 0.5 * density_side * (velocity_side[0] ** 2 + velocity_side[1] ** 2 + velocity_side[2] ** 2)
    plain_flux = [density_side * normal_speed]
    plain_flux = plain_flux + [density_side * velocity_side[direction] * normal_speed + pressure_side * normal[direction] for direction in range(3)]
    plain_flux = plain_flux + [(energy + pressure_side) * normal_speed]
    conserved = [density_side] + [density_side * velocity_side[direction] for direction in range(3)] + [energy]
    factor = density_side * lag_speed / (wave_speed - contact)
    speed_gap = contact - normal_speed
    star_state = [factor] + [factor * (velocity_side[direction] + speed_gap * normal[direction]) for direction in range(3)]
    star_state = star_state + [factor * (energy / density_side + speed_gap * (contact + pressure_side / (density_side * lag_speed)))]
    starred = [plain_flux[component] + wave_speed * (star_state[component] - conserved[component]) for component in range(5)]
    return (plain_flux, starred)

def hllc_flux(left_state, right_state, normal, face_vel):
    left_vel = [left_state[direction] - face_vel[direction] for direction in range(3)]
    right_vel = [right_state[direction] - face_vel[direction] for direction in range(3)]
    left_density, left_pressure = (left_state[3], left_state[4])
    right_density, right_pressure = (right_state[3], right_state[4])
    left_normal = left_vel[0] * normal[0] + left_vel[1] * normal[1] + left_vel[2] * normal[2]
    right_normal = right_vel[0] * normal[0] + right_vel[1] * normal[1] + right_vel[2] * normal[2]
    left_sound = jnp.sqrt(GAMMA * left_pressure / left_density)
    right_sound = jnp.sqrt(GAMMA * right_pressure / right_density)
    speed_left = jnp.minimum(left_normal - left_sound, right_normal - right_sound)
    speed_right = jnp.maximum(left_normal + left_sound, right_normal + right_sound)
    lag_left = speed_left - left_normal
    lag_right = speed_right - right_normal
    contact = (right_pressure - left_pressure + left_density * left_normal * lag_left - right_density * right_normal * lag_right) / (left_density * lag_left - right_density * lag_right)
    flux_left, star_left = side_flux(left_density, left_vel, left_pressure, normal, left_normal, lag_left, speed_left, contact)
    flux_right, star_right = side_flux(right_density, right_vel, right_pressure, normal, right_normal, lag_right, speed_right, contact)
    moving = [jnp.where(speed_left >= 0.0, flux_left[component], jnp.where(contact >= 0.0, star_left[component], jnp.where(speed_right >= 0.0, star_right[component], flux_right[component]))) for component in range(5)]
    mass_flux = moving[0]
    momentum = [moving[1 + direction] + face_vel[direction] * mass_flux for direction in range(3)]
    face_sq = face_vel[0] ** 2 + face_vel[1] ** 2 + face_vel[2] ** 2
    energy_flux = moving[4] + face_vel[0] * moving[1] + face_vel[1] * moving[2] + face_vel[2] * moving[3] + 0.5 * face_sq * mass_flux
    return [mass_flux] + momentum + [energy_flux]

def flux_tile(near_tile, far_tile, near_pay, far_pay, mask_near, mask_far, weight):
    separation = [far_tile[direction][:, None, :] - near_tile[direction][:, :, None] for direction in range(3)]
    dist_sq = separation[0] * separation[0] + separation[1] * separation[1] + separation[2] * separation[2]
    smoothing = kernel(dist_sq) * mask_near[:, :, None] * mask_far[:, None, :]
    near_density = near_pay[0][:, :, None]
    far_density = far_pay[0][:, None, :]
    near_matrix = [near_pay[1 + position][:, :, None] for position in range(6)]
    far_matrix = [far_pay[1 + position][:, None, :] for position in range(6)]
    toward_near = sym_apply(near_matrix, separation)
    toward_far = sym_apply(far_matrix, separation)
    near_scale = smoothing / (near_density * near_density)
    far_scale = smoothing / (far_density * far_density)
    area = [near_scale * toward_near[direction] + far_scale * toward_far[direction] for direction in range(3)]
    magnitude = jnp.sqrt(area[0] * area[0] + area[1] * area[1] + area[2] * area[2])
    clamp_scale = 1.0 / jnp.maximum(magnitude, AREA_FLOOR)
    normal = [area[direction] * clamp_scale for direction in range(3)]
    left_state = []
    right_state = []
    for quantity in range(5):
        near_value = near_tile[3 + quantity][:, :, None]
        far_value = far_tile[3 + quantity][:, None, :]
        near_change = 0.5 * (near_pay[7 + 3 * quantity][:, :, None] * separation[0] + near_pay[8 + 3 * quantity][:, :, None] * separation[1] + near_pay[9 + 3 * quantity][:, :, None] * separation[2])
        far_change = 0.5 * (far_pay[7 + 3 * quantity][:, None, :] * separation[0] + far_pay[8 + 3 * quantity][:, None, :] * separation[1] + far_pay[9 + 3 * quantity][:, None, :] * separation[2])
        low_bound = jnp.minimum(near_value, far_value)
        high_bound = jnp.maximum(near_value, far_value)
        left_state.append(jnp.clip(near_value + near_change, low_bound, high_bound))
        right_state.append(jnp.clip(far_value - far_change, low_bound, high_bound))
    face_vel = [0.5 * (near_tile[3 + direction][:, :, None] + far_tile[3 + direction][:, None, :]) for direction in range(3)]
    fluxes = hllc_flux(left_state, right_state, normal, face_vel)
    pair_scale = magnitude * weight[:, None, None]
    row_sums = jnp.stack([-lax.optimization_barrier(jnp.sum(pair_scale * face_flux, axis=2)) for face_flux in fluxes])
    col_sums = jnp.stack([lax.optimization_barrier(jnp.sum(pair_scale * face_flux, axis=1)) for face_flux in fluxes])
    return (row_sums, col_sums)

def reference(positions, velocity, density, pressure, counts, pair_list):
    primitive = jnp.concatenate([positions, velocity, density[None], pressure[None]], axis=0).reshape(8, LEAVES, LEAF)
    live_mask = (jnp.arange(LEAF, dtype=jnp.int32)[None, :] < counts[:, None]).astype(jnp.float32)
    box_length = jnp.asarray(LEAVES // SLAB_LEAVES, jnp.float32)
    occupied = pair_list[0] >= 0
    home_leaf = jnp.where(occupied, pair_list[0], 0).astype(jnp.int32)
    other_leaf = jnp.where(occupied, pair_list[1], 0).astype(jnp.int32)
    wrapped = (other_leaf // SLAB_LEAVES < home_leaf // SLAB_LEAVES).astype(jnp.float32)
    offset = pair_list[2].astype(jnp.float32)
    weight = jnp.where(occupied, jnp.where(home_leaf == other_leaf, 0.5, 1.0), 0.0).astype(jnp.float32)
    block_count = PAIRS // PAIR_SUB
    blocked = tuple((column_data.reshape(block_count, PAIR_SUB) for column_data in (home_leaf, other_leaf, wrapped, offset, weight)))

    def moment_step(running, block_data):
        home_part, other_part, wrap_part, offset_part, weight_part = block_data
        near_tile = primitive[:, home_part]
        far_tile = image_rows(primitive[:, other_part], wrap_part, offset_part, box_length)
        row_sums, col_sums = moment_tile(near_tile, far_tile, live_mask[home_part], live_mask[other_part], weight_part)
        running = running.at[:, home_part].add(row_sums).at[:, other_part].add(col_sums)
        return (running, None)
    moments = lax.scan(moment_step, jnp.zeros((22, LEAVES, LEAF), jnp.float32), blocked)[0]
    payload = finish_moments(moments, live_mask)

    def flux_step(running, block_data):
        home_part, other_part, wrap_part, offset_part, weight_part = block_data
        near_tile = primitive[:, home_part]
        far_tile = image_rows(primitive[:, other_part], wrap_part, offset_part, box_length)
        row_sums, col_sums = flux_tile(near_tile, far_tile, payload[:, home_part], payload[:, other_part], live_mask[home_part], live_mask[other_part], weight_part)
        running = running.at[:, home_part].add(row_sums).at[:, other_part].add(col_sums)
        return (running, None)
    flux_sum = lax.scan(flux_step, jnp.zeros((5, LEAVES, LEAF), jnp.float32), blocked)[0]
    return (payload[0][None] * flux_sum).reshape(5, PARTICLES)
```

```python
import functools
import math

import jax
import jax.numpy as jnp
from jax import lax
from jax.experimental import pallas as pl
from jax.experimental.pallas import tpu as pltpu
from jax.sharding import PartitionSpec as P

LEAF = 128
CAND = 5

GAMMA = 5.0 / 3.0
SUPPORT = 1.5
KERNEL_NORM = 21.0 / (2.0 * math.pi * SUPPORT**3)
MOMENT_REG = 0.05
AREA_FLOOR = 0.0001
AWAY = 64.0
UNROLL = 4
F32 = jnp.float32
BF16 = jnp.bfloat16


def shifted(shard, axis, by):
    peers = lax.axis_size(axis)
    return lax.ppermute(shard, axis, [(i, (i + by) % peers) for i in range(peers)])


def swapped(shard, axis, mask):
    peers = lax.axis_size(axis)
    return lax.ppermute(shard, axis, [(i, i ^ mask) for i in range(peers)])


def reciprocal(value):
    guess = pl.reciprocal(value, approx=True)
    return guess * (2.0 - value * guess)


def smoothing_of(dist_sq, scale):
    safe = jnp.maximum(dist_sq, 1e-12)
    radius = safe * lax.rsqrt(safe)
    inside = jnp.maximum(1.0 - radius * (1.0 / SUPPORT), 0.0)
    square = inside * inside
    return (square * square) * (scale + (scale * (4.0 / SUPPORT)) * radius)


def split_three(value):
    high = value.astype(BF16).astype(F32)
    rest = value - high
    middle = rest.astype(BF16).astype(F32)
    return high, middle, rest - middle


def bilinear(near_rows, far_rows):
    near_high, near_mid, near_low = split_three(near_rows)
    far_high, far_mid, far_low = split_three(far_rows)
    near_stack = jnp.concatenate(
        [near_high, near_high, near_high, near_mid, near_mid, near_low], axis=0
    ).astype(BF16)
    far_stack = jnp.concatenate(
        [far_high, far_mid, far_low, far_high, far_mid, far_high], axis=0
    ).astype(BF16)
    return lax.dot_general(
        near_stack, far_stack, (((0,), (0,)), ((), ())), preferred_element_type=F32
    )


def moment_features(tile):
    row = lax.broadcasted_iota(jnp.int32, tile.shape, 0)
    by_x = tile * tile[0:1]
    by_y = jnp.where(row == 0, 1.0, tile * tile[1:2])
    by_z = tile * tile[2:3]
    whole = jnp.concatenate([tile, by_x, by_y, by_z], axis=0)
    high = whole.astype(BF16)
    low = (whole - high.astype(F32)).astype(BF16)
    both = jnp.concatenate([high, low], axis=0)
    return jnp.concatenate([both, both], axis=1)


def displacement(step_x, step_y, wrap):
    row = lax.broadcasted_iota(jnp.int32, (8, LEAF), 0)
    zero = jnp.zeros((8, LEAF), F32)
    out = jnp.where(row == 0, step_x, zero)
    out = jnp.where(row == 1, step_y, out)
    return jnp.where(row == 4, -wrap, out)


def finish_leaf(raw, tile):
    pos = [tile[k : k + 1] for k in range(3)]
    live = pos[0] < 0.5 * AWAY
    total = raw[16:17]
    first = [raw[k : k + 1] - pos[k] * total for k in range(3)]

    def second(left, right):
        lead = raw[8 + 8 * left + right : 9 + 8 * left + right]
        return lead - pos[left] * raw[right : right + 1] - pos[right] * first[left]

    density = jnp.where(live, total, 1.0)
    inverse_density = 1.0 / density

    def scaled(value):
        return jnp.where(live, value * inverse_density, 0.0)

    exx = scaled(second(0, 0)) + MOMENT_REG
    exy = scaled(second(0, 1))
    exz = scaled(second(0, 2))
    eyy = scaled(second(1, 1)) + MOMENT_REG
    eyz = scaled(second(1, 2))
    ezz = scaled(second(2, 2)) + MOMENT_REG
    mxx = eyy * ezz - eyz * eyz
    mxy = exz * eyz - exy * ezz
    mxz = exy * eyz - exz * eyy
    myy = exx * ezz - exz * exz
    myz = exy * exz - exx * eyz
    mzz = exx * eyy - exy * exy
    scale = 1.0 / (exx * mxx + exy * mxy + exz * mxz)
    inverse = [entry * scale for entry in (mxx, mxy, mxz, myy, myz, mzz)]
    square = inverse_density * inverse_density
    rows = [density] + [entry * square for entry in inverse]
    for quantity in range(3, 8):
        value = tile[quantity : quantity + 1]
        along = [
            scaled(
                raw[8 + 8 * k + quantity : 9 + 8 * k + quantity]
                - pos[k] * raw[quantity : quantity + 1]
                - value * first[k]
            )
            for k in range(3)
        ]
        half = [0.5 * term for term in along]
        rows.append(inverse[0] * half[0] + inverse[1] * half[1] + inverse[2] * half[2])
        rows.append(inverse[1] * half[0] + inverse[3] * half[1] + inverse[4] * half[2])
        rows.append(inverse[2] * half[0] + inverse[4] * half[1] + inverse[5] * half[2])
    rows.append(jnp.zeros((2, LEAF), F32))
    return jnp.concatenate(rows, axis=0)


def dot3(left, right):
    return left[0] * right[0] + left[1] * right[1] + left[2] * right[2]


def apply_sym(matrix, vector):
    return [
        dot3((matrix[0], matrix[1], matrix[2]), vector),
        dot3((matrix[1], matrix[3], matrix[4]), vector),
        dot3((matrix[2], matrix[4], matrix[5]), vector),
    ]


def limited(value, low, high):
    return jnp.minimum(jnp.maximum(value, low), high)


def face_fluxes(near, far, weight):
    sep = [far[k] - near[k] for k in range(3)]
    smooth = smoothing_of(dot3(sep, sep), KERNEL_NORM)
    toward = apply_sym([near[8 + k] + far[8 + k] for k in range(6)], sep)
    length_sq = jnp.maximum(dot3(toward, toward), 1e-30)
    inverse_length = lax.rsqrt(length_sq)
    magnitude = smooth * (length_sq * inverse_length)
    scale = jnp.minimum(inverse_length, smooth * (1.0 / AREA_FLOOR))
    normal = [entry * scale for entry in toward]
    left_vel, right_vel, face_vel = [], [], []
    for k in range(3):
        face_vel.append(0.5 * (near[3 + k] + far[3 + k]))
        half_gap = 0.5 * (far[3 + k] - near[3 + k])
        high = jnp.abs(half_gap)
        low = -high
        left_vel.append(limited(dot3(near[14 + 3 * k : 17 + 3 * k], sep) - half_gap, low, high))
        right_vel.append(limited(half_gap - dot3(far[14 + 3 * k : 17 + 3 * k], sep), low, high))
    thermo = []
    for k in (3, 4):
        low = jnp.minimum(near[3 + k], far[3 + k])
        high = jnp.maximum(near[3 + k], far[3 + k])
        thermo.append(
            limited(near[3 + k] + dot3(near[14 + 3 * k : 17 + 3 * k], sep), low, high)
        )
        thermo.append(
            limited(far[3 + k] - dot3(far[14 + 3 * k : 17 + 3 * k], sep), low, high)
        )
    left_rho, right_rho, left_p, right_p = thermo
    left_u = dot3(left_vel, normal)
    right_u = dot3(right_vel, normal)
    left_gp = GAMMA * left_p
    right_gp = GAMMA * right_p
    left_c = left_gp * lax.rsqrt(left_gp * left_rho)
    right_c = right_gp * lax.rsqrt(right_gp * right_rho)
    slow = jnp.minimum(left_u - left_c, right_u - right_c)
    fast = jnp.maximum(left_u + left_c, right_u + right_c)
    left_m = left_rho * (slow - left_u)
    right_m = right_rho * (fast - right_u)
    contact = (right_p - left_p + left_m * left_u - right_m * right_u) * reciprocal(
        left_m - right_m
    )
    is_left = contact >= 0.0
    speed = jnp.where(is_left, jnp.minimum(slow, 0.0), jnp.maximum(fast, 0.0))
    rho = jnp.where(is_left, left_rho, right_rho)
    press = jnp.where(is_left, left_p, right_p)
    normal_speed = jnp.where(is_left, left_u, right_u)
    vel = [jnp.where(is_left, left_vel[k], right_vel[k]) for k in range(3)]
    lag = speed - normal_speed
    ratio = lag * reciprocal(speed - contact)
    through = ratio * contact
    gain = speed * ratio - speed
    push = (rho * lag) * gain
    area = magnitude * weight
    mass = (rho * through) * area
    total_p = (press + push) * area
    mom = [mass * vel[k] + total_p * normal[k] for k in range(3)]
    energy = (press * (through * (1.0 / (GAMMA - 1.0)) + normal_speed + gain) + push * contact) * area
    energy = energy + (0.5 * dot3(vel, vel)) * mass
    energy = energy + dot3(face_vel, mom) + (0.5 * dot3(face_vel, face_vel)) * mass
    return [mass] + [mom[k] + face_vel[k] * mass for k in range(3)] + [energy]


def step_kernel(
    width,
    leaf_sub,
    slot_count,
    own_first,
    own_slots,
    rec,
    info,
    lower_ref,
    own_ref,
    upper_ref,
    beyond_ref,
    own_out,
    next_out,
    order,
    local,
    raw,
    pay,
    near_cols,
    far_rows,
    col_sum,
    row_sum,
):
    whole = 4 * width

    def load_leaf(column, carry):
        lanes = pl.ds(pl.multiple_of(column * LEAF, LEAF), LEAF)
        local[column] = lower_ref[:, lanes]
        local[width + column] = own_ref[:, lanes]
        local[2 * width + column] = upper_ref[:, lanes]
        local[3 * width + column] = beyond_ref[:, lanes]
        own_out[:, lanes] = jnp.zeros((5, LEAF), F32)
        next_out[:, lanes] = jnp.zeros((5, LEAF), F32)
        col_sum[column] = jnp.zeros((8, LEAF), F32)
        col_sum[width + column] = jnp.zeros((8, LEAF), F32)
        for slab in range(4):
            raw[slab * width + column] = jnp.zeros((32, LEAF), F32)
        return carry

    lax.fori_loop(0, width, load_leaf, 0)
    local[whole] = jnp.zeros((8, LEAF), F32)
    raw[whole] = jnp.zeros((32, LEAF), F32)
    for home in range(leaf_sub):
        row_sum[home] = jnp.zeros((LEAF, LEAF), F32)

    def collect(slot, used):
        order[used] = slot
        return used + rec[5, slot]

    used = lax.fori_loop(0, slot_count, collect, 0, unroll=8)
    for extra in range(UNROLL):
        order[used + extra] = slot_count

    def moment_slot(slot):
        home = rec[0, slot]
        other = rec[1, slot]
        shift = displacement(
            rec[2, slot].astype(F32), rec[3, slot].astype(F32), rec[4, slot].astype(F32)
        )
        near = local[home]
        far = local[other] + shift
        weight = jnp.where(home == other, 0.5, 1.0).astype(F32)
        row = lax.broadcasted_iota(jnp.int32, (8, LEAF), 0)
        near_sq = dot3([near[k : k + 1] for k in range(3)], [near[k : k + 1] for k in range(3)])
        far_sq = dot3([far[k : k + 1] for k in range(3)], [far[k : k + 1] for k in range(3)])
        near_k = jnp.where(row < 3, near, jnp.where(row == 3, near_sq, jnp.where(row == 4, 1.0, 0.0)))
        far_k = jnp.where(
            row < 3, -2.0 * far, jnp.where(row == 4, far_sq, jnp.where(row == 3, 1.0, 0.0))
        )
        smooth = smoothing_of(bilinear(near_k, far_k), KERNEL_NORM * weight)
        high = smooth.astype(BF16)
        low = (smooth - high.astype(F32)).astype(BF16)
        row_part = lax.dot_general(
            moment_features(far),
            jnp.concatenate([high, low], axis=1),
            (((1,), (1,)), ((), ())),
            preferred_element_type=F32,
        )
        col_part = lax.dot_general(
            moment_features(near - shift),
            jnp.concatenate([high, low], axis=0),
            (((1,), (0,)), ((), ())),
            preferred_element_type=F32,
        )
        return home, other, row_part[:32] + row_part[32:], col_part[:32] + col_part[32:]

    def moment_group(group, carry):
        parts = [moment_slot(order[group * UNROLL + k]) for k in range(UNROLL)]
        for home, other, row_part, col_part in parts:
            raw[home] += row_part
            raw[other] += col_part
        return carry

    lax.fori_loop(0, (used + UNROLL - 1) // UNROLL, moment_group, 0)

    base = info[0]
    upper_base = info[1]

    def own_leaf(k):
        return width + lax.rem(base + k, width)

    def upper_leaf(k):
        return 2 * width + lax.rem(upper_base + k, width)

    def finish(leaf):
        pay[leaf] = finish_leaf(raw[leaf], local[leaf])

    def finish_own(k, carry):
        finish(own_leaf(k))
        return carry

    def finish_upper(k, carry):
        finish(upper_leaf(k))
        return carry

    lax.fori_loop(0, leaf_sub + 1, finish_own, 0)
    lax.fori_loop(0, leaf_sub + 2, finish_upper, 0)

    def turn_home(k, carry):
        leaf = own_leaf(k)
        rows = jnp.concatenate(
            [local[leaf], pay[leaf], jnp.zeros((LEAF - 32, LEAF), F32)], axis=0
        )
        near_cols[k] = rows.T
        return carry

    lax.fori_loop(0, leaf_sub, turn_home, 0)

    lane = lax.broadcasted_iota(jnp.int32, (8, LEAF), 1)

    def flux_slot(slot, carry):
        home = rec[0, slot]
        other = rec[1, slot]
        live = rec[6, slot]

        @pl.when(live > 0)
        def _():
            shift = displacement(
                rec[2, slot].astype(F32), rec[3, slot].astype(F32), rec[4, slot].astype(F32)
            )
            far_rows[0:8] = local[other] + shift
            far_rows[8:32] = pay[other]
            weight = jnp.where(home == other, 0.5, 1.0).astype(F32)
            home_column = home - width
            seat = home_column - base
            blocks = (info[8 + home_column] + 7) // 8
            picks = list(range(8)) + list(range(9, 30))

            def row_block(block, sums):
                rows = pl.ds(pl.multiple_of(block * 8, 8), 8)
                cols = near_cols[seat, rows, :]
                near = [jnp.broadcast_to(cols[:, k : k + 1], (8, LEAF)) for k in picks]
                far = [jnp.broadcast_to(far_rows[k : k + 1, :], (8, LEAF)) for k in picks]
                fluxes = face_fluxes(near, far, weight)
                gathered = row_sum[seat, rows, :]
                for k in range(5):
                    part = jnp.sum(fluxes[k], axis=1, keepdims=True)
                    gathered = gathered + jnp.where(lane == k, part, 0.0)
                row_sum[seat, rows, :] = gathered
                return tuple(sums[k] + fluxes[k] for k in range(5))

            sums = lax.fori_loop(
                0, blocks, row_block, tuple(jnp.zeros((8, LEAF), F32) for _ in range(5))
            )
            flat = [jnp.sum(entry, axis=0, keepdims=True) for entry in sums]
            col_sum[other - width] += jnp.concatenate(flat + [jnp.zeros((3, LEAF), F32)], axis=0)

        return carry

    lax.fori_loop(own_first, own_first + own_slots, flux_slot, 0)

    def subtract_rows(k, carry):
        column = own_leaf(k) - width
        col_sum[column] = col_sum[column] - row_sum[k].T[0:8]
        return carry

    lax.fori_loop(0, leaf_sub, subtract_rows, 0)

    def rates(leaf):
        live = local[leaf][0:1] < 0.5 * AWAY
        total = col_sum[leaf - width] * pay[leaf][0:1]
        return jnp.where(live, total, 0.0)[0:5]

    def write_own(k, carry):
        leaf = own_leaf(k)
        own_out[:, pl.ds(pl.multiple_of((leaf - width) * LEAF, LEAF), LEAF)] = rates(leaf)
        return carry

    def write_upper(k, carry):
        leaf = upper_leaf(k)
        next_out[:, pl.ds(pl.multiple_of((leaf - 2 * width) * LEAF, LEAF), LEAF)] = rates(leaf)
        return carry

    lax.fori_loop(0, leaf_sub + 1, write_own, 0)
    lax.fori_loop(0, leaf_sub + 2, write_upper, 0)


def shards(positions, velocity, density, pressure, counts, pair_list):
    width = counts.shape[0]
    slots = pair_list.shape[1]
    particles = width * LEAF
    sub_count = lax.axis_size("sub")
    leaf_sub = width // sub_count
    slab_index = lax.axis_index("slab")
    sub_index = lax.axis_index("sub")

    particle = jnp.arange(particles, dtype=jnp.int32)
    column = particle // LEAF
    live = (particle % LEAF) < jnp.repeat(counts, LEAF, total_repeat_length=particles)
    centre_x = slab_index.astype(F32) + 0.5
    local_x = jnp.where(live, positions[0] - centre_x, AWAY)
    local_y = positions[1] - (column.astype(F32) + 0.5)
    local_z = positions[2] - 0.5
    state = jnp.concatenate(
        [local_x[None], local_y[None], local_z[None], velocity, density[None], pressure[None]], axis=0
    )
    misc = pair_list.reshape(-1).astype(F32)
    lanes = -(-misc.shape[0] // (8 * LEAF)) * LEAF
    misc = jnp.pad(misc, (0, 8 * lanes - misc.shape[0])).reshape(8, lanes)
    packed = jnp.concatenate([state, misc], axis=1)
    lower = shifted(packed, "slab", 1)
    upper = shifted(packed, "slab", -1)
    beyond = shifted(packed, "slab", -2)

    lists = jnp.stack([lower[:, particles:], packed[:, particles:], upper[:, particles:]])
    lists = lists.reshape(3, -1)[:, : 3 * slots].reshape(1, 3, 3, slots)
    mask = 1
    while mask < sub_count:
        lists = jnp.concatenate([lists, swapped(lists, "sub", mask)], axis=0)
        mask *= 2
    lists = lists.astype(jnp.int32)
    head, tail, offset = lists[:, :, 0], lists[:, :, 1], lists[:, :, 2]
    occupied = head >= 0
    head = jnp.where(occupied, head, 0)
    tail = jnp.where(occupied, tail, 0)
    head_col, tail_col = head % width, tail % width
    step_x = (head // width != tail // width).astype(jnp.int32)
    wrap = (tail // width < head // width).astype(jnp.int32)
    from_slab = jnp.arange(3, dtype=jnp.int32)[None, :, None]
    home = from_slab * width + head_col
    other = (from_slab + step_x) * width + tail_col
    step_y = tail_col + offset - head_col
    own_shift = jnp.max(
        jnp.where(occupied[0, 1] & (step_x[0, 1] > 0), (-offset[0, 1]) % width, 0)
    )
    base = sub_index * leaf_sub
    upper_base = (base - 1 + own_shift) % width

    def wanted(leaf_slab, leaf_column):
        in_own = (leaf_slab == 1) & ((leaf_column - base) % width <= leaf_sub)
        in_upper = (leaf_slab == 2) & ((leaf_column - upper_base) % width <= leaf_sub + 1)
        return in_own | in_upper

    needed = occupied & (wanted(from_slab, head_col) | wanted(from_slab + step_x, tail_col))
    slot_count = sub_count * 3 * slots
    rec = jnp.stack(
        [
            jnp.broadcast_to(entry, head.shape).reshape(-1)
            for entry in (
                home,
                other,
                step_x,
                step_y,
                wrap,
                needed.astype(jnp.int32),
                occupied.astype(jnp.int32),
            )
        ]
    )
    spare = jnp.array([[4 * width], [4 * width], [0], [0], [0], [0], [0]], jnp.int32)
    rec = jnp.concatenate([rec, spare], axis=1)
    info = jnp.concatenate(
        [base[None], upper_base[None], jnp.zeros((6,), jnp.int32), counts]
    ).astype(jnp.int32)

    smem = pl.BlockSpec(memory_space=pltpu.SMEM)
    vmem = pl.BlockSpec(memory_space=pltpu.VMEM)
    own_part, next_part = pl.pallas_call(
        functools.partial(step_kernel, width, leaf_sub, slot_count, slots, slots),
        out_shape=[jax.ShapeDtypeStruct((5, particles), F32)] * 2,
        in_specs=[smem, smem, vmem, vmem, vmem, vmem],
        out_specs=[vmem, vmem],
        scratch_shapes=[
            pltpu.SMEM((slot_count + UNROLL + 1,), jnp.int32),
            pltpu.VMEM((4 * width + 1, 8, LEAF), F32),
            pltpu.VMEM((4 * width + 1, 32, LEAF), F32),
            pltpu.VMEM((4 * width, 24, LEAF), F32),
            pltpu.VMEM((leaf_sub, LEAF, LEAF), F32),
            pltpu.VMEM((32, LEAF), F32),
            pltpu.VMEM((2 * width, 8, LEAF), F32),
            pltpu.VMEM((leaf_sub, LEAF, LEAF), F32),
        ],
        compiler_params=pltpu.CompilerParams(vmem_limit_bytes=48 * 1024 * 1024),
        name="hydro_step",
    )(rec, info, lower, packed, upper, beyond)

    merged = own_part + shifted(next_part, "slab", 1)
    mask = 1
    while mask < sub_count:
        merged = merged + swapped(merged, "sub", mask)
        mask *= 2
    return merged


def solution(mesh):
    placed = (
        P(None, "slab"),
        P(None, "slab"),
        P("slab"),
        P("slab"),
        P("slab"),
        P(None, ("slab", "sub")),
    )
    return jax.shard_map(
        shards, mesh=mesh, in_specs=placed, out_specs=P(None, "slab"), check_vma=False
    )
```

```python
import functools
import math

import jax
import jax.numpy as jnp
from jax import lax
from jax.experimental import pallas as pl
from jax.experimental.pallas import tpu as pltpu
from jax.sharding import PartitionSpec as P

LEAF = 128
CAND = 5

GAMMA = 5.0 / 3.0
SUPPORT = 1.5
KERNEL_NORM = 21.0 / (2.0 * math.pi * SUPPORT**3)
MOMENT_REG = 0.05
AREA_FLOOR = 0.0001
AWAY = 64.0
UNROLL = 8
ROWS = 64
F32 = jnp.float32
BF16 = jnp.bfloat16


def shifted(shard, axis, by):
    peers = lax.axis_size(axis)
    return lax.ppermute(shard, axis, [(i, (i + by) % peers) for i in range(peers)])


def swapped(shard, axis, mask):
    peers = lax.axis_size(axis)
    return lax.ppermute(shard, axis, [(i, i ^ mask) for i in range(peers)])


def reciprocal(value):
    return pl.reciprocal(value, approx=True)


def smoothing_of(dist_sq, scale):
    safe = jnp.maximum(dist_sq, 1e-12)
    radius = safe * lax.rsqrt(safe)
    inside = jnp.maximum(1.0 - radius * (1.0 / SUPPORT), 0.0)
    square = inside * inside
    return (square * square) * (scale + (scale * (4.0 / SUPPORT)) * radius)


def split_three(value):
    high = value.astype(BF16).astype(F32)
    rest = value - high
    middle = rest.astype(BF16).astype(F32)
    return high, middle, rest - middle


def stack_near(rows):
    high, middle, low = split_three(rows)
    return jnp.concatenate([high, high, high, middle, middle, low], axis=0).astype(BF16)


def stack_far(rows):
    high, middle, low = split_three(rows)
    return jnp.concatenate([high, middle, low, high, middle, high], axis=0).astype(BF16)


def bilinear(near_rows, far_rows):
    return lax.dot_general(
        stack_near(near_rows),
        stack_far(far_rows),
        (((0,), (0,)), ((), ())),
        preferred_element_type=F32,
    )


def moment_features(tile):
    row = lax.broadcasted_iota(jnp.int32, tile.shape, 0)
    by_x = tile * tile[0:1]
    by_y = jnp.where(row == 0, 1.0, tile * tile[1:2])
    by_z = tile * tile[2:3]
    whole = jnp.concatenate([tile, by_x, by_y, by_z], axis=0)
    high = whole.astype(BF16)
    low = (whole - high.astype(F32)).astype(BF16)
    both = jnp.concatenate([high, low], axis=0)
    return jnp.concatenate([both, both], axis=1)


def displacement(step_x, step_y, wrap):
    row = lax.broadcasted_iota(jnp.int32, (8, LEAF), 0)
    zero = jnp.zeros((8, LEAF), F32)
    out = jnp.where(row == 0, step_x, zero)
    out = jnp.where(row == 1, step_y, out)
    return jnp.where(row == 4, -wrap, out)


def finish_leaf(raw, tile):
    pos = [tile[k : k + 1] for k in range(3)]
    live = pos[0] < 0.5 * AWAY
    total = raw[16:17]
    first = [raw[k : k + 1] - pos[k] * total for k in range(3)]

    def second(left, right):
        lead = raw[8 + 8 * left + right : 9 + 8 * left + right]
        return lead - pos[left] * raw[right : right + 1] - pos[right] * first[left]

    density = jnp.where(live, total, 1.0)
    inverse_density = 1.0 / density

    def scaled(value):
        return jnp.where(live, value * inverse_density, 0.0)

    exx = scaled(second(0, 0)) + MOMENT_REG
    exy = scaled(second(0, 1))
    exz = scaled(second(0, 2))
    eyy = scaled(second(1, 1)) + MOMENT_REG
    eyz = scaled(second(1, 2))
    ezz = scaled(second(2, 2)) + MOMENT_REG
    mxx = eyy * ezz - eyz * eyz
    mxy = exz * eyz - exy * ezz
    mxz = exy * eyz - exz * eyy
    myy = exx * ezz - exz * exz
    myz = exy * exz - exx * eyz
    mzz = exx * eyy - exy * exy
    scale = 1.0 / (exx * mxx + exy * mxy + exz * mxz)
    inverse = [entry * scale for entry in (mxx, mxy, mxz, myy, myz, mzz)]
    square = inverse_density * inverse_density
    rows = [density] + [entry * square for entry in inverse]
    for quantity in range(3, 8):
        value = tile[quantity : quantity + 1]
        along = [
            scaled(
                raw[8 + 8 * k + quantity : 9 + 8 * k + quantity]
                - pos[k] * raw[quantity : quantity + 1]
                - value * first[k]
            )
            for k in range(3)
        ]
        half = [0.5 * term for term in along]
        rows.append(inverse[0] * half[0] + inverse[1] * half[1] + inverse[2] * half[2])
        rows.append(inverse[1] * half[0] + inverse[3] * half[1] + inverse[4] * half[2])
        rows.append(inverse[2] * half[0] + inverse[4] * half[1] + inverse[5] * half[2])
    rows.append(jnp.zeros((2, LEAF), F32))
    return jnp.concatenate(rows, axis=0)


def dot3(left, right):
    return left[0] * right[0] + left[1] * right[1] + left[2] * right[2]


def apply_sym(matrix, vector):
    return [
        dot3((matrix[0], matrix[1], matrix[2]), vector),
        dot3((matrix[1], matrix[3], matrix[4]), vector),
        dot3((matrix[2], matrix[4], matrix[5]), vector),
    ]


def stack_rows(rows):
    row = lax.broadcasted_iota(jnp.int32, (8, LEAF), 0)
    out = jnp.zeros((8, LEAF), F32)
    for k, entry in rows.items():
        out = jnp.where(row == k, entry, out)
    return out


def near_coefficients(tile, pay):
    pos = [tile[k : k + 1] for k in range(3)]
    out = [
        {0: dot3(pos, pos), 1: -2.0 * pos[0], 2: -2.0 * pos[1], 3: -2.0 * pos[2], 7: 1.0}
    ]
    matrix = [pay[1 + k : 2 + k] for k in range(6)]
    for line in ((0, 1, 2), (1, 3, 4), (2, 4, 5)):
        entries = [matrix[k] for k in line]
        out.append({0: -dot3(entries, pos), 1: entries[0], 2: entries[1], 3: entries[2]})
    for quantity in range(5):
        slope = [pay[7 + 3 * quantity + k : 8 + 3 * quantity + k] for k in range(3)]
        value = tile[3 + quantity : 4 + quantity]
        if quantity < 3:
            entry = {0: 0.5 * value - dot3(slope, pos), 4 + quantity: -0.5}
        else:
            entry = {0: value - dot3(slope, pos)}
        entry.update({1: slope[0], 2: slope[1], 3: slope[2]})
        out.append(entry)
    return [stack_rows(entry) for entry in out]


def far_coefficients(tile, pay):
    pos = [tile[k : k + 1] for k in range(3)]
    out = []
    matrix = [pay[1 + k : 2 + k] for k in range(6)]
    for line in ((0, 1, 2), (1, 3, 4), (2, 4, 5)):
        entries = [matrix[k] for k in line]
        out.append({0: dot3(entries, pos), 1: -entries[0], 2: -entries[1], 3: -entries[2]})
    for quantity in range(5):
        slope = [pay[7 + 3 * quantity + k : 8 + 3 * quantity + k] for k in range(3)]
        value = tile[3 + quantity : 4 + quantity]
        if quantity < 3:
            entry = {0: 0.5 * value - dot3(slope, pos), 4 + quantity: -0.5}
        else:
            entry = {0: value - dot3(slope, pos)}
        entry.update({1: slope[0], 2: slope[1], 3: slope[2]})
        out.append(entry)
    return [stack_rows(entry) for entry in out]


def shared_coefficients(tile):
    vel = [tile[3 + k : 4 + k] for k in range(3)]
    out = [{0: 0.5 * vel[k], 1 + k: -0.5} for k in range(3)]
    out += [{0: 0.5 * vel[k], 1 + k: 0.5} for k in range(3)]
    out += [{4: 1.0}, {5: 1.0}]
    out.append(
        {0: 0.125 * dot3(vel, vel), 1: 0.25 * vel[0], 2: 0.25 * vel[1], 3: 0.25 * vel[2], 6: 0.125}
    )
    return [stack_rows(entry) for entry in out]


def limited(value, low, high):
    return jnp.minimum(jnp.maximum(value, low), high)


def face_fluxes(near_out, far_out, shared_out, far_rho, far_press, weight):
    smooth = smoothing_of(near_out[0], KERNEL_NORM)
    toward = [near_out[1 + k] + far_out[k] for k in range(3)]
    length_sq = jnp.maximum(dot3(toward, toward), 1e-30)
    inverse_length = lax.rsqrt(length_sq)
    magnitude = smooth * (length_sq * inverse_length)
    scale = jnp.minimum(inverse_length, smooth * (1.0 / AREA_FLOOR))
    normal = [entry * scale for entry in toward]
    left_vel, right_vel = [], []
    for k in range(3):
        high = jnp.abs(shared_out[k])
        low = -high
        left_vel.append(limited(near_out[4 + k], low, high))
        right_vel.append(limited(far_out[3 + k], low, high))
    face_vel = shared_out[3:6]
    half_sq = shared_out[8]
    thermo = []
    for k, far_value in ((0, far_rho), (1, far_press)):
        low = jnp.minimum(shared_out[6 + k], far_value)
        high = jnp.maximum(shared_out[6 + k], far_value)
        thermo.append(limited(near_out[7 + k], low, high))
        thermo.append(limited(far_out[6 + k], low, high))
    left_rho, right_rho, left_p, right_p = thermo
    left_u = dot3(left_vel, normal)
    right_u = dot3(right_vel, normal)
    left_gp = GAMMA * left_p
    right_gp = GAMMA * right_p
    left_c = left_gp * lax.rsqrt(left_gp * left_rho)
    right_c = right_gp * lax.rsqrt(right_gp * right_rho)
    slow = jnp.minimum(left_u - left_c, right_u - right_c)
    fast = jnp.maximum(left_u + left_c, right_u + right_c)
    left_m = left_rho * (slow - left_u)
    right_m = right_rho * (fast - right_u)
    contact = (right_p - left_p + left_m * left_u - right_m * right_u) * reciprocal(
        left_m - right_m
    )
    is_left = contact >= 0.0
    speed = jnp.where(is_left, jnp.minimum(slow, 0.0), jnp.maximum(fast, 0.0))
    rho = jnp.where(is_left, left_rho, right_rho)
    press = jnp.where(is_left, left_p, right_p)
    normal_speed = jnp.where(is_left, left_u, right_u)
    vel = [jnp.where(is_left, left_vel[k], right_vel[k]) for k in range(3)]
    lag = speed - normal_speed
    ratio = lag * reciprocal(speed - contact)
    through = ratio * contact
    gain = speed * ratio - speed
    push = (rho * lag) * gain
    area = magnitude * weight
    mass = (rho * through) * area
    total_p = (press + push) * area
    mom = [mass * vel[k] + total_p * normal[k] for k in range(3)]
    energy = (press * (through * (1.0 / (GAMMA - 1.0)) + normal_speed + gain) + push * contact) * area
    energy = energy + (0.5 * dot3(vel, vel)) * mass
    energy = energy + dot3(face_vel, mom) + half_sq * mass
    return [mass] + [mom[k] + face_vel[k] * mass for k in range(3)] + [energy]


def pack_kernel(
    width,
    slab_ref,
    counts,
    positions,
    velocity,
    density,
    pressure,
    pair_list,
    packed,
):
    centre_x = slab_ref[0].astype(F32) + 0.5
    row = lax.broadcasted_iota(jnp.int32, (3, LEAF), 0)
    lane = lax.broadcasted_iota(jnp.int32, (3, LEAF), 1)

    def one_leaf(column, carry):
        lanes = pl.ds(pl.multiple_of(column * LEAF, LEAF), LEAF)
        centre_y = column.astype(F32) + 0.5
        centre = jnp.where(row == 0, centre_x, jnp.where(row == 1, centre_y, 0.5))
        dead = (row == 0) & (lane >= counts[column])
        packed[0:3, lanes] = jnp.where(dead, AWAY, positions[:, lanes] - centre)
        packed[3:6, lanes] = velocity[:, lanes]
        packed[6:7, lanes] = density[:, lanes]
        packed[7:8, lanes] = pressure[:, lanes]
        return carry

    lax.fori_loop(0, width, one_leaf, 0, unroll=4)
    particles = width * LEAF
    spare = packed.shape[1] - particles
    packed[:, particles:] = jnp.zeros((8, spare), F32)
    packed[0:3, particles : particles + pair_list.shape[1]] = pair_list[...].astype(F32)


def step_kernel(
    width,
    leaf_sub,
    slot_count,
    own_first,
    own_slots,
    rec,
    info,
    lower_ref,
    own_ref,
    upper_ref,
    beyond_ref,
    own_out,
    next_out,
    order,
    items,
    local,
    raw,
    pay,
    far_coef,
    near_left,
    far_left,
    shared_left,
    near_right,
    far_right,
    shared_right,
    dist,
    near_form,
    far_form,
    shared_form,
    col_sum,
    row_sum,
    row_rate,
):
    whole = 4 * width

    def load_leaf(column, carry):
        lanes = pl.ds(pl.multiple_of(column * LEAF, LEAF), LEAF)
        local[column] = lower_ref[:, lanes]
        local[width + column] = own_ref[:, lanes]
        local[2 * width + column] = upper_ref[:, lanes]
        local[3 * width + column] = beyond_ref[:, lanes]
        own_out[:, lanes] = jnp.zeros((5, LEAF), F32)
        next_out[:, lanes] = jnp.zeros((5, LEAF), F32)
        for slab in range(4):
            raw[slab * width + column] = jnp.zeros((32, LEAF), F32)
        return carry

    lax.fori_loop(0, width, load_leaf, 0)
    local[whole] = jnp.zeros((8, LEAF), F32)
    raw[whole] = jnp.zeros((32, LEAF), F32)

    def clear_rows(home, carry):
        for k in range(5):
            row_sum[home, k] = jnp.zeros((LEAF, LEAF), F32)
        return carry

    lax.fori_loop(0, leaf_sub, clear_rows, 0)

    def clear_cols(seat, carry):
        col_sum[seat] = jnp.zeros((40, LEAF), F32)
        return carry

    lax.fori_loop(0, 2 * leaf_sub + 3, clear_cols, 0)

    def collect(slot, used):
        order[used] = slot
        return used + rec[5, slot]

    used = lax.fori_loop(0, slot_count, collect, 0, unroll=8)
    for extra in range(2 * UNROLL):
        order[used + extra] = slot_count

    def slot_tiles(slot):
        shift = displacement(
            rec[2, slot].astype(F32), rec[3, slot].astype(F32), rec[4, slot].astype(F32)
        )
        return local[rec[0, slot]], local[rec[1, slot]] + shift, shift

    def distances(group):
        row = lax.broadcasted_iota(jnp.int32, (8, LEAF), 0)
        for k in range(UNROLL):
            near, far, _ = slot_tiles(order[group * UNROLL + k])
            near_pos = [near[j : j + 1] for j in range(3)]
            far_pos = [far[j : j + 1] for j in range(3)]
            near_k = jnp.where(
                row < 3,
                near,
                jnp.where(row == 3, dot3(near_pos, near_pos), jnp.where(row == 4, 1.0, 0.0)),
            )
            far_k = jnp.where(
                row < 3,
                -2.0 * far,
                jnp.where(row == 4, dot3(far_pos, far_pos), jnp.where(row == 3, 1.0, 0.0)),
            )
            dist[k] = bilinear(near_k, far_k)

    def moment_group(group, carry):
        parts = []
        for k in range(UNROLL):
            slot = order[group * UNROLL + k]
            near, far, shift = slot_tiles(slot)
            home = rec[0, slot]
            other = rec[1, slot]
            weight = jnp.where(home == other, 0.5, 1.0).astype(F32)
            smooth = smoothing_of(dist[k], KERNEL_NORM * weight)
            high = smooth.astype(BF16)
            low = (smooth - high.astype(F32)).astype(BF16)
            row_part = lax.dot_general(
                moment_features(far),
                jnp.concatenate([high, low], axis=1),
                (((1,), (1,)), ((), ())),
                preferred_element_type=F32,
            )
            col_part = lax.dot_general(
                moment_features(near - shift),
                jnp.concatenate([high, low], axis=0),
                (((1,), (0,)), ((), ())),
                preferred_element_type=F32,
            )
            parts.append((home, other, row_part, col_part))
        distances(group + 1)
        for home, other, row_part, col_part in parts:
            raw[home] += row_part[:32] + row_part[32:]
            raw[other] += col_part[:32] + col_part[32:]
        return carry

    distances(0)
    lax.fori_loop(0, (used + UNROLL - 1) // UNROLL, moment_group, 0)

    base = info[0]
    upper_base = info[1]

    def own_leaf(k):
        return width + lax.rem(base + k, width)

    def upper_leaf(k):
        return 2 * width + lax.rem(upper_base + k, width)

    def window_leaf(seat):
        return jnp.where(seat <= leaf_sub, own_leaf(seat), upper_leaf(seat - leaf_sub - 1))

    def finish(seat, carry):
        leaf = window_leaf(seat)
        payload = finish_leaf(raw[leaf], local[leaf])
        pay[seat] = payload
        for k, entry in enumerate(far_coefficients(local[leaf], payload)):
            far_coef[seat, 8 * k : 8 * k + 8] = entry
        return carry

    window = 2 * leaf_sub + 3
    lax.fori_loop(0, window, finish, 0)

    def turn_home(seat, carry):
        leaf = own_leaf(seat)
        tile = local[leaf]
        for k, entry in enumerate(near_coefficients(tile, pay[seat])):
            turned = stack_near(entry).T
            for part in range(LEAF // ROWS):
                near_left[seat, part, k * ROWS : (k + 1) * ROWS, 0:48] = turned[
                    part * ROWS : (part + 1) * ROWS
                ]
        vel = [tile[3 + k : 4 + k] for k in range(3)]
        generic = {0: 1.0}
        generic.update({1 + k: tile[k : k + 1] for k in range(6)})
        plain = {0: 1.0, 6: dot3(vel, vel)}
        plain.update({1 + k: tile[3 + k : 4 + k] for k in range(5)})
        far_left[seat, :, 0:48] = stack_near(stack_rows(generic)).T
        shared_left[seat, :, 0:48] = stack_near(stack_rows(plain)).T
        return carry

    lax.fori_loop(0, leaf_sub, turn_home, 0)

    def prepare_slot(index, count):
        slot = own_first + index
        other = rec[1, slot]
        other_seat = rec[7, slot]
        step_x = rec[2, slot].astype(F32)
        step_y = rec[3, slot].astype(F32)
        wrap = rec[4, slot].astype(F32)
        live = rec[6, slot]
        column = rec[0, slot] - width
        for part in range(LEAF // ROWS):
            items[count] = index * (LEAF // ROWS) + part
            filled = (info[8 + column] > part * ROWS).astype(jnp.int32)
            count = count + live * filled

        far = local[other] + displacement(step_x, step_y, wrap)
        row = lax.broadcasted_iota(jnp.int32, (8, LEAF), 0)
        pos = [far[k : k + 1] for k in range(3)]
        generic = {0: 1.0, 7: dot3(pos, pos)}
        generic.update({1 + k: far[k : k + 1] for k in range(6)})
        near_right[index] = stack_far(stack_rows(generic))
        for k in range(8):
            entry = far_coef[other_seat, 8 * k : 8 * k + 8]
            change = entry[1:2] * step_x + entry[2:3] * step_y
            if k == 4:
                change = change + 0.5 * wrap
            entry = jnp.where(row == 0, entry - change, entry)
            far_right[index, :, k * LEAF : (k + 1) * LEAF] = stack_far(entry)
        for k, entry in enumerate(shared_coefficients(far)):
            shared_right[index, :, k * LEAF : (k + 1) * LEAF] = stack_far(entry)
        return count

    item_count = lax.fori_loop(0, own_slots, prepare_slot, 0)
    items[item_count] = items[0]

    def forms(position):
        item = items[position]
        index = item // (LEAF // ROWS)
        part = item % (LEAF // ROWS)
        seat = rec[0, own_first + index] - width - base
        rows = pl.ds(pl.multiple_of(part * ROWS, ROWS), ROWS)
        near_form[...] = jnp.dot(
            near_left[seat, part, :, 0:48], near_right[index], preferred_element_type=F32
        )
        far_form[...] = jnp.dot(
            far_left[seat, rows, 0:48], far_right[index], preferred_element_type=F32
        )
        shared_form[...] = jnp.dot(
            shared_left[seat, rows, 0:48], shared_right[index], preferred_element_type=F32
        )

    def flux_item(position, carry):
        item = items[position]
        index = item // (LEAF // ROWS)
        part = item % (LEAF // ROWS)
        home = rec[0, own_first + index]
        other = rec[1, own_first + index]
        other_seat = rec[7, own_first + index]
        seat = home - width - base
        rows = pl.ds(pl.multiple_of(part * ROWS, ROWS), ROWS)
        weight = jnp.where(home == other, 0.5, 1.0).astype(F32)
        fluxes = face_fluxes(
            [near_form[k * ROWS : (k + 1) * ROWS, :] for k in range(9)],
            [far_form[:, k * LEAF : (k + 1) * LEAF] for k in range(8)],
            [shared_form[:, k * LEAF : (k + 1) * LEAF] for k in range(9)],
            local[other, 6:7, :],
            local[other, 7:8, :],
            weight,
        )
        forms(position + 1)
        for k in range(5):
            row_sum[seat, k, rows, :] += fluxes[k]
            col_sum[other_seat, 8 * k : 8 * k + 8] += sum(
                fluxes[k][8 * j : 8 * j + 8] for j in range(ROWS // 8)
            )
        return carry

    forms(0)
    lax.fori_loop(0, item_count, flux_item, 0)

    lane = lax.broadcasted_iota(jnp.int32, (LEAF, LEAF), 1)

    def row_total(seat, carry):
        total = jnp.zeros((LEAF, LEAF), F32)
        for c in range(5):
            total = jnp.where(lane == c, jnp.sum(row_sum[seat, c], axis=1, keepdims=True), total)
        row_rate[seat] = total.T[0:8]
        return carry

    lax.fori_loop(0, leaf_sub, row_total, 0)
    row_rate[leaf_sub] = jnp.zeros((8, LEAF), F32)

    def rates(seat, less):
        leaf = window_leaf(seat)
        total = stack_rows(
            {
                k: jnp.sum(col_sum[seat, 8 * k : 8 * k + 8], axis=0, keepdims=True)
                for k in range(5)
            }
        )
        if less is not None:
            total = total - less
        live = local[leaf][0:1] < 0.5 * AWAY
        column = lax.rem(leaf, width)
        lanes = pl.ds(pl.multiple_of(column * LEAF, LEAF), LEAF)
        return lanes, jnp.where(live, total * pay[seat][0:1], 0.0)[0:5]

    def write_own(k, carry):
        lanes, value = rates(k, row_rate[k])
        own_out[:, lanes] = value
        return carry

    def write_upper(k, carry):
        lanes, value = rates(k, None)
        next_out[:, lanes] = value
        return carry

    lax.fori_loop(0, leaf_sub + 1, write_own, 0)
    lax.fori_loop(leaf_sub + 1, window, write_upper, 0)


def shards(positions, velocity, density, pressure, counts, pair_list):
    width = counts.shape[0]
    slots = pair_list.shape[1]
    particles = width * LEAF
    sub_count = lax.axis_size("sub")
    leaf_sub = width // sub_count
    slab_index = lax.axis_index("slab")
    sub_index = lax.axis_index("sub")

    smem = pl.BlockSpec(memory_space=pltpu.SMEM)
    vmem = pl.BlockSpec(memory_space=pltpu.VMEM)
    lanes = -(-slots // LEAF) * LEAF
    packed = pl.pallas_call(
        functools.partial(pack_kernel, width),
        out_shape=jax.ShapeDtypeStruct((8, particles + lanes), F32),
        in_specs=[smem, smem, vmem, vmem, vmem, vmem, vmem],
        out_specs=vmem,
        name="pack",
    )(
        slab_index.astype(jnp.int32).reshape(1),
        counts,
        positions,
        velocity,
        density[None],
        pressure[None],
        pair_list,
    )
    lower = shifted(packed, "slab", 1)
    upper = shifted(packed, "slab", -1)
    beyond = shifted(packed, "slab", -2)

    lists = jnp.stack(
        [entry[0:3, particles : particles + slots] for entry in (lower, packed, upper)]
    )[None]
    mask = 1
    while mask < sub_count:
        lists = jnp.concatenate([lists, swapped(lists, "sub", mask)], axis=0)
        mask *= 2
    lists = lists.astype(jnp.int32)
    head, tail, offset = lists[:, :, 0], lists[:, :, 1], lists[:, :, 2]
    occupied = head >= 0
    head = jnp.where(occupied, head, 0)
    tail = jnp.where(occupied, tail, 0)
    head_col, tail_col = head % width, tail % width
    step_x = (head // width != tail // width).astype(jnp.int32)
    wrap = (tail // width < head // width).astype(jnp.int32)
    from_slab = jnp.arange(3, dtype=jnp.int32)[None, :, None]
    home = from_slab * width + head_col
    other = (from_slab + step_x) * width + tail_col
    step_y = tail_col + offset - head_col
    own_shift = jnp.max(
        jnp.where(occupied[0, 1] & (step_x[0, 1] > 0), (-offset[0, 1]) % width, 0)
    )
    base = sub_index * leaf_sub
    upper_base = (base - 1 + own_shift) % width

    def wanted(leaf_slab, leaf_column):
        in_own = (leaf_slab == 1) & ((leaf_column - base) % width <= leaf_sub)
        in_upper = (leaf_slab == 2) & ((leaf_column - upper_base) % width <= leaf_sub + 1)
        return in_own | in_upper

    needed = occupied & (wanted(from_slab, head_col) | wanted(from_slab + step_x, tail_col))
    other_seat = jnp.where(
        step_x > 0,
        jnp.minimum((tail_col - upper_base) % width, leaf_sub + 1) + leaf_sub + 1,
        jnp.minimum((tail_col - base) % width, leaf_sub),
    )
    slot_count = sub_count * 3 * slots
    own_items = slots * (LEAF // ROWS) + 1
    rec = jnp.stack(
        [
            jnp.broadcast_to(entry, head.shape).reshape(-1)
            for entry in (
                home,
                other,
                step_x,
                step_y,
                wrap,
                needed.astype(jnp.int32),
                occupied.astype(jnp.int32),
                other_seat,
            )
        ]
    )
    spare = jnp.array([[4 * width], [4 * width], [0], [0], [0], [0], [0], [0]], jnp.int32)
    rec = jnp.concatenate([rec, spare], axis=1)
    info = jnp.concatenate(
        [base[None], upper_base[None], jnp.zeros((6,), jnp.int32), counts]
    ).astype(jnp.int32)

    own_part, next_part = pl.pallas_call(
        functools.partial(step_kernel, width, leaf_sub, slot_count, slots, slots),
        out_shape=[jax.ShapeDtypeStruct((5, particles), F32)] * 2,
        in_specs=[smem, smem, vmem, vmem, vmem, vmem],
        out_specs=[vmem, vmem],
        scratch_shapes=[
            pltpu.SMEM((slot_count + 2 * UNROLL,), jnp.int32),
            pltpu.SMEM((own_items,), jnp.int32),
            pltpu.VMEM((4 * width + 1, 8, LEAF), F32),
            pltpu.VMEM((4 * width + 1, 32, LEAF), F32),
            pltpu.VMEM((2 * leaf_sub + 3, 24, LEAF), F32),
            pltpu.VMEM((2 * leaf_sub + 3, 64, LEAF), F32),
            pltpu.VMEM((leaf_sub, LEAF // ROWS, 9 * ROWS, LEAF), BF16),
            pltpu.VMEM((leaf_sub, LEAF, LEAF), BF16),
            pltpu.VMEM((leaf_sub, LEAF, LEAF), BF16),
            pltpu.VMEM((slots, 48, LEAF), BF16),
            pltpu.VMEM((slots, 48, 8 * LEAF), BF16),
            pltpu.VMEM((slots, 48, 9 * LEAF), BF16),
            pltpu.VMEM((UNROLL, LEAF, LEAF), F32),
            pltpu.VMEM((9 * ROWS, LEAF), F32),
            pltpu.VMEM((ROWS, 8 * LEAF), F32),
            pltpu.VMEM((ROWS, 9 * LEAF), F32),
            pltpu.VMEM((2 * leaf_sub + 3, 40, LEAF), F32),
            pltpu.VMEM((leaf_sub, 5, LEAF, LEAF), F32),
            pltpu.VMEM((leaf_sub + 1, 8, LEAF), F32),
        ],
        compiler_params=pltpu.CompilerParams(vmem_limit_bytes=48 * 1024 * 1024),
        name="hydro_step",
    )(rec, info, lower, packed, upper, beyond)

    merged = own_part + shifted(next_part, "slab", 1)
    mask = 1
    while mask < sub_count:
        merged = merged + swapped(merged, "sub", mask)
        mask *= 2
    return merged


def solution(mesh):
    placed = (
        P(None, "slab"),
        P(None, "slab"),
        P("slab"),
        P("slab"),
        P("slab"),
        P(None, ("slab", "sub")),
    )
    return jax.shard_map(
        shards, mesh=mesh, in_specs=placed, out_specs=P(None, "slab"), check_vma=False
    )
```

```python
import functools
import math

import jax
import jax.numpy as jnp
from jax import lax
from jax.experimental import pallas as pl
from jax.experimental.pallas import tpu as pltpu
from jax.sharding import PartitionSpec as P

LEAF = 128
CAND = 5

GAMMA = 5.0 / 3.0
SUPPORT = 1.5
KERNEL_NORM = 21.0 / (2.0 * math.pi * SUPPORT**3)
MOMENT_REG = 0.05
AREA_FLOOR = 0.0001
AWAY = 64.0
UNROLL = 8
ROWS = 64
COST_LEAF, COST_SLOT, COST_PART = 17, 3, 5
F32 = jnp.float32
BF16 = jnp.bfloat16


def shifted(shard, axis, by):
    peers = lax.axis_size(axis)
    return lax.ppermute(shard, axis, [(i, (i + by) % peers) for i in range(peers)])


def swapped(shard, axis, mask):
    peers = lax.axis_size(axis)
    return lax.ppermute(shard, axis, [(i, i ^ mask) for i in range(peers)])


def reciprocal(value):
    return pl.reciprocal(value, approx=True)


def smoothing_of(dist_sq, scale):
    safe = jnp.maximum(dist_sq, 1e-12)
    radius = safe * lax.rsqrt(safe)
    inside = jnp.maximum(1.0 - radius * (1.0 / SUPPORT), 0.0)
    square = inside * inside
    return (square * square) * (scale + (scale * (4.0 / SUPPORT)) * radius)


def split_three(value):
    high = value.astype(BF16).astype(F32)
    rest = value - high
    middle = rest.astype(BF16).astype(F32)
    return high, middle, rest - middle


def stack_near(rows):
    high, middle, low = split_three(rows)
    return jnp.concatenate([high, high, high, middle, middle, low], axis=0).astype(BF16)


def stack_far(rows):
    high, middle, low = split_three(rows)
    return jnp.concatenate([high, middle, low, high, middle, high], axis=0).astype(BF16)


def bilinear(near_rows, far_rows):
    return lax.dot_general(
        stack_near(near_rows),
        stack_far(far_rows),
        (((0,), (0,)), ((), ())),
        preferred_element_type=F32,
    )


def moment_features(tile):
    row = lax.broadcasted_iota(jnp.int32, tile.shape, 0)
    by_x = tile * tile[0:1]
    by_y = jnp.where(row == 0, 1.0, tile * tile[1:2])
    by_z = tile * tile[2:3]
    whole = jnp.concatenate([tile, by_x, by_y, by_z], axis=0)
    high = whole.astype(BF16)
    low = (whole - high.astype(F32)).astype(BF16)
    both = jnp.concatenate([high, low], axis=0)
    return jnp.concatenate([both, both], axis=1)


def displacement(step_x, step_y, wrap):
    row = lax.broadcasted_iota(jnp.int32, (8, LEAF), 0)
    zero = jnp.zeros((8, LEAF), F32)
    out = jnp.where(row == 0, step_x, zero)
    out = jnp.where(row == 1, step_y, out)
    return jnp.where(row == 4, -wrap, out)


def finish_leaf(raw, tile):
    pos = [tile[k : k + 1] for k in range(3)]
    live = pos[0] < 0.5 * AWAY
    total = raw[16:17]
    first = [raw[k : k + 1] - pos[k] * total for k in range(3)]

    def second(left, right):
        lead = raw[8 + 8 * left + right : 9 + 8 * left + right]
        return lead - pos[left] * raw[right : right + 1] - pos[right] * first[left]

    density = jnp.where(live, total, 1.0)
    inverse_density = 1.0 / density

    def scaled(value):
        return jnp.where(live, value * inverse_density, 0.0)

    exx = scaled(second(0, 0)) + MOMENT_REG
    exy = scaled(second(0, 1))
    exz = scaled(second(0, 2))
    eyy = scaled(second(1, 1)) + MOMENT_REG
    eyz = scaled(second(1, 2))
    ezz = scaled(second(2, 2)) + MOMENT_REG
    mxx = eyy * ezz - eyz * eyz
    mxy = exz * eyz - exy * ezz
    mxz = exy * eyz - exz * eyy
    myy = exx * ezz - exz * exz
    myz = exy * exz - exx * eyz
    mzz = exx * eyy - exy * exy
    scale = 1.0 / (exx * mxx + exy * mxy + exz * mxz)
    inverse = [entry * scale for entry in (mxx, mxy, mxz, myy, myz, mzz)]
    square = inverse_density * inverse_density
    rows = [density] + [entry * square for entry in inverse]
    for quantity in range(3, 8):
        value = tile[quantity : quantity + 1]
        along = [
            scaled(
                raw[8 + 8 * k + quantity : 9 + 8 * k + quantity]
                - pos[k] * raw[quantity : quantity + 1]
                - value * first[k]
            )
            for k in range(3)
        ]
        half = [0.5 * term for term in along]
        rows.append(inverse[0] * half[0] + inverse[1] * half[1] + inverse[2] * half[2])
        rows.append(inverse[1] * half[0] + inverse[3] * half[1] + inverse[4] * half[2])
        rows.append(inverse[2] * half[0] + inverse[4] * half[1] + inverse[5] * half[2])
    rows.append(jnp.zeros((2, LEAF), F32))
    return jnp.concatenate(rows, axis=0)


def dot3(left, right):
    return left[0] * right[0] + left[1] * right[1] + left[2] * right[2]


def apply_sym(matrix, vector):
    return [
        dot3((matrix[0], matrix[1], matrix[2]), vector),
        dot3((matrix[1], matrix[3], matrix[4]), vector),
        dot3((matrix[2], matrix[4], matrix[5]), vector),
    ]


def stack_rows(rows):
    row = lax.broadcasted_iota(jnp.int32, (8, LEAF), 0)
    out = jnp.zeros((8, LEAF), F32)
    for k, entry in rows.items():
        out = jnp.where(row == k, entry, out)
    return out


def near_coefficients(tile, pay):
    pos = [tile[k : k + 1] for k in range(3)]
    out = [
        {0: dot3(pos, pos), 1: -2.0 * pos[0], 2: -2.0 * pos[1], 3: -2.0 * pos[2], 7: 1.0}
    ]
    matrix = [pay[1 + k : 2 + k] for k in range(6)]
    for line in ((0, 1, 2), (1, 3, 4), (2, 4, 5)):
        entries = [matrix[k] for k in line]
        out.append({0: -dot3(entries, pos), 1: entries[0], 2: entries[1], 3: entries[2]})
    for quantity in range(5):
        slope = [pay[7 + 3 * quantity + k : 8 + 3 * quantity + k] for k in range(3)]
        value = tile[3 + quantity : 4 + quantity]
        if quantity < 3:
            entry = {0: 0.5 * value - dot3(slope, pos), 4 + quantity: -0.5}
        else:
            entry = {0: value - dot3(slope, pos)}
        entry.update({1: slope[0], 2: slope[1], 3: slope[2]})
        out.append(entry)
    return [stack_rows(entry) for entry in out]


def far_coefficients(tile, pay):
    pos = [tile[k : k + 1] for k in range(3)]
    out = []
    matrix = [pay[1 + k : 2 + k] for k in range(6)]
    for line in ((0, 1, 2), (1, 3, 4), (2, 4, 5)):
        entries = [matrix[k] for k in line]
        out.append({0: dot3(entries, pos), 1: -entries[0], 2: -entries[1], 3: -entries[2]})
    for quantity in range(5):
        slope = [pay[7 + 3 * quantity + k : 8 + 3 * quantity + k] for k in range(3)]
        value = tile[3 + quantity : 4 + quantity]
        if quantity < 3:
            entry = {0: 0.5 * value - dot3(slope, pos), 4 + quantity: -0.5}
        else:
            entry = {0: value - dot3(slope, pos)}
        entry.update({1: slope[0], 2: slope[1], 3: slope[2]})
        out.append(entry)
    return [stack_rows(entry) for entry in out]


def shared_coefficients(tile):
    vel = [tile[3 + k : 4 + k] for k in range(3)]
    out = [{0: 0.5 * vel[k], 1 + k: -0.5} for k in range(3)]
    out += [{0: 0.5 * vel[k], 1 + k: 0.5} for k in range(3)]
    out += [{4: 1.0}, {5: 1.0}]
    return [stack_rows(entry) for entry in out]


def limited(value, low, high):
    return jnp.minimum(jnp.maximum(value, low), high)


def face_fluxes(near_out, far_out, shared_out, far_rho, far_press):
    smooth = smoothing_of(near_out[0], KERNEL_NORM)
    toward = [near_out[1 + k] + far_out[k] for k in range(3)]
    length_sq = jnp.maximum(dot3(toward, toward), 1e-30)
    inverse_length = lax.rsqrt(length_sq)
    area = smooth * (length_sq * inverse_length)
    scale = jnp.minimum(inverse_length, smooth * (1.0 / AREA_FLOOR))
    normal = [entry * scale for entry in toward]
    left_vel, right_vel = [], []
    for k in range(3):
        high = jnp.abs(shared_out[k])
        low = -high
        left_vel.append(limited(near_out[4 + k], low, high))
        right_vel.append(limited(far_out[3 + k], low, high))
    face_vel = shared_out[3:6]
    thermo = []
    for k, far_value in ((0, far_rho), (1, far_press)):
        low = jnp.minimum(shared_out[6 + k], far_value)
        high = jnp.maximum(shared_out[6 + k], far_value)
        thermo.append(limited(near_out[7 + k], low, high))
        thermo.append(limited(far_out[6 + k], low, high))
    left_rho, right_rho, left_p, right_p = thermo
    left_u = dot3(left_vel, normal)
    right_u = dot3(right_vel, normal)
    left_gp = GAMMA * left_p
    right_gp = GAMMA * right_p
    left_c = left_gp * lax.rsqrt(left_gp * left_rho)
    right_c = right_gp * lax.rsqrt(right_gp * right_rho)
    slow = jnp.minimum(left_u - left_c, right_u - right_c)
    fast = jnp.maximum(left_u + left_c, right_u + right_c)
    left_m = left_rho * (slow - left_u)
    right_m = right_rho * (fast - right_u)
    contact = (right_p - left_p + left_m * left_u - right_m * right_u) * reciprocal(
        left_m - right_m
    )
    is_left = contact >= 0.0
    speed = jnp.where(is_left, jnp.minimum(slow, 0.0), jnp.maximum(fast, 0.0))
    rho = jnp.where(is_left, left_rho, right_rho) * area
    press = jnp.where(is_left, left_p, right_p) * area
    normal_speed = jnp.where(is_left, left_u, right_u)
    vel = [jnp.where(is_left, left_vel[k], right_vel[k]) + face_vel[k] for k in range(3)]
    lag = speed - normal_speed
    ratio = lag * reciprocal(speed - contact)
    through = ratio * contact
    gain = speed * ratio - speed
    push = (rho * lag) * gain
    mass = rho * through
    total_p = press + push
    mom = [mass * vel[k] + total_p * normal[k] for k in range(3)]
    energy = press * (through * (1.0 / (GAMMA - 1.0)) + normal_speed + gain) + push * contact
    energy = energy + (0.5 * mass) * dot3(vel, vel) + total_p * dot3(face_vel, normal)
    return [mass] + mom + [energy]


def pack_kernel(
    width,
    leaf_sub,
    place,
    counts,
    positions,
    velocity,
    density,
    pressure,
    pair_list,
    packed,
):
    centre_x = place[0].astype(F32) + 0.5
    row = lax.broadcasted_iota(jnp.int32, (3, LEAF), 0)
    lane = lax.broadcasted_iota(jnp.int32, (3, LEAF), 1)

    def one_leaf(column, carry):
        lanes = pl.ds(pl.multiple_of(column * LEAF, LEAF), LEAF)
        centre_y = column.astype(F32) + 0.5
        centre = jnp.where(row == 0, centre_x, jnp.where(row == 1, centre_y, 0.5))
        dead = (row == 0) & (lane >= counts[column])
        packed[0:3, lanes] = jnp.where(dead, AWAY, positions[:, lanes] - centre)
        packed[3:6, lanes] = velocity[:, lanes]
        packed[6:7, lanes] = density[:, lanes]
        packed[7:8, lanes] = pressure[:, lanes]
        return carry

    lax.fori_loop(0, width, one_leaf, 0, unroll=4)
    particles = width * LEAF
    spare = packed.shape[1] - particles
    packed[:, particles:] = jnp.zeros((8, spare), F32)
    slots = pair_list.shape[1]
    packed[0:3, particles : particles + slots] = pair_list[...].astype(F32)
    heads = pair_list[0:1, :] - (place[0] * width + place[1] * leaf_sub)
    seat = lax.broadcasted_iota(jnp.int32, (1, slots), 1)
    headed = jnp.zeros((1, slots), F32)
    for k in range(leaf_sub):
        found = jnp.sum(jnp.where(heads == k, 1.0, 0.0), axis=1, keepdims=True)
        headed = jnp.where(seat == k, found, headed)
    packed[3:4, particles : particles + slots] = headed


def step_kernel(
    width,
    sub_count,
    slots,
    rec,
    info,
    lower_ref,
    own_ref,
    upper_ref,
    beyond_ref,
    own_out,
    next_out,
    order,
    mine,
    need,
    item_left,
    item_index,
    item_other,
    item_seat,
    local,
    raw,
    pay,
    far_coef,
    near_left,
    far_left,
    shared_left,
    near_right,
    far_right,
    shared_right,
    dist,
    near_form,
    far_form,
    shared_form,
    col_sum,
    row_sum,
    row_rate,
):
    whole = 4 * width
    leaf_sub = width // sub_count
    cap = 2 * leaf_sub
    slot_count = 3 * sub_count * slots

    def load_leaf(column, carry):
        lanes = pl.ds(pl.multiple_of(column * LEAF, LEAF), LEAF)
        local[column] = lower_ref[:, lanes]
        local[width + column] = own_ref[:, lanes]
        local[2 * width + column] = upper_ref[:, lanes]
        local[3 * width + column] = beyond_ref[:, lanes]
        own_out[:, lanes] = jnp.zeros((5, LEAF), F32)
        next_out[:, lanes] = jnp.zeros((5, LEAF), F32)
        for slab in range(4):
            raw[slab * width + column] = jnp.zeros((32, LEAF), F32)
            need[slab * width + column] = 0
        return carry

    lax.fori_loop(0, width, load_leaf, 0)
    local[whole] = jnp.zeros((8, LEAF), F32)
    raw[whole] = jnp.zeros((32, LEAF), F32)
    need[whole] = 0

    me = info[0]
    shift_w = info[1]

    def column_cost(column):
        group = jnp.bitwise_xor(me, column // leaf_sub)
        headed = info[8 + width + group * leaf_sub + lax.rem(column, leaf_sub)]
        parts = (info[8 + column] + ROWS - 1) // ROWS
        return COST_LEAF + headed * (COST_SLOT + COST_PART * parts)

    total_cost = lax.fori_loop(
        0, width, lambda column, total: total + column_cost(column), jnp.int32(0)
    )

    def deal(column, state):
        owner, length, before, first, mine_length = state
        cost = column_cost(column)
        middle = sub_count * (2 * before + cost)
        wish = (middle >= 2 * total_cost * (owner + 1)) | (length == cap)
        allowed = (owner < sub_count - 1) & (width - column <= (sub_count - 1 - owner) * cap)
        step = (wish & allowed).astype(jnp.int32)
        owner = owner + step
        length = (1 - step) * length + 1
        is_mine = (owner == me).astype(jnp.int32)
        first = jnp.where((is_mine > 0) & (mine_length == 0), column, first)
        return owner, length, before + cost, first, mine_length + is_mine

    zero = jnp.int32(0)
    _, _, _, base, length = lax.fori_loop(0, width, deal, (zero, zero, zero, zero, zero))
    upper_base = lax.rem(base + width - 1 + shift_w, width)

    def own_leaf(k):
        return width + lax.rem(base + k, width)

    def upper_leaf(k):
        return 2 * width + lax.rem(upper_base + k, width)

    def mark_own(k, carry):
        need[own_leaf(k)] = jnp.where(k < length, 3, 1)
        return carry

    def mark_upper(k, carry):
        need[upper_leaf(k)] = 1
        return carry

    lax.fori_loop(0, length + 1, mark_own, 0)
    lax.fori_loop(0, length + 2, mark_upper, 0)

    def collect_outer(first, used):
        def collect(k, used):
            slot = first + k
            order[used] = slot
            flags = need[rec[0, slot]] | need[rec[1, slot]]
            return used + (flags & 1)

        return lax.fori_loop(0, slots, collect, used, unroll=8)

    def collect_own(first, carry):
        def collect(k, carry):
            used, kept = carry
            slot = first + k
            flags = need[rec[0, slot]]
            order[used] = slot
            mine[kept] = slot
            return used + ((flags | need[rec[1, slot]]) & 1), kept + (flags >> 1)

        return lax.fori_loop(0, slots, collect, carry, unroll=8)

    used, kept = zero, zero
    for group in range(sub_count):
        used = collect_outer(3 * group * slots, used)
        used, kept = collect_own((3 * group + 1) * slots, (used, kept))
        used = collect_outer((3 * group + 2) * slots, used)
    for extra in range(2 * UNROLL):
        order[used + extra] = slot_count

    def clear_rows(seat, carry):
        for part in range(LEAF // ROWS):
            for k in range(5):
                row_sum[seat * (LEAF // ROWS) + part, k] = jnp.zeros((ROWS, LEAF), F32)
        return carry

    lax.fori_loop(0, length, clear_rows, 0)

    def clear_cols(seat, carry):
        col_sum[seat] = jnp.zeros((40, LEAF), F32)
        return carry

    lax.fori_loop(0, length + 1, clear_cols, 0)
    lax.fori_loop(cap + 1, cap + length + 3, clear_cols, 0)

    def slot_tiles(slot):
        shift = displacement(
            rec[2, slot].astype(F32), rec[3, slot].astype(F32), rec[4, slot].astype(F32)
        )
        return local[rec[0, slot]], local[rec[1, slot]] + shift, shift

    def distances(group):
        row = lax.broadcasted_iota(jnp.int32, (8, LEAF), 0)
        for k in range(UNROLL):
            near, far, _ = slot_tiles(order[group * UNROLL + k])
            near_pos = [near[j : j + 1] for j in range(3)]
            far_pos = [far[j : j + 1] for j in range(3)]
            near_k = jnp.where(
                row < 3,
                near,
                jnp.where(row == 3, dot3(near_pos, near_pos), jnp.where(row == 4, 1.0, 0.0)),
            )
            far_k = jnp.where(
                row < 3,
                -2.0 * far,
                jnp.where(row == 4, dot3(far_pos, far_pos), jnp.where(row == 3, 1.0, 0.0)),
            )
            dist[k] = bilinear(near_k, far_k)

    def moment_group(group, carry):
        parts = []
        for k in range(UNROLL):
            slot = order[group * UNROLL + k]
            near, far, shift = slot_tiles(slot)
            home = rec[0, slot]
            other = rec[1, slot]
            weight = jnp.where(home == other, 0.5, 1.0).astype(F32)
            smooth = smoothing_of(dist[k], KERNEL_NORM * weight)
            high = smooth.astype(BF16)
            low = (smooth - high.astype(F32)).astype(BF16)
            row_part = lax.dot_general(
                moment_features(far),
                jnp.concatenate([high, low], axis=1),
                (((1,), (1,)), ((), ())),
                preferred_element_type=F32,
            )
            col_part = lax.dot_general(
                moment_features(near - shift),
                jnp.concatenate([high, low], axis=0),
                (((1,), (0,)), ((), ())),
                preferred_element_type=F32,
            )
            parts.append((home, other, row_part, col_part))
        distances(group + 1)
        for home, other, row_part, col_part in parts:
            raw[home] += row_part[:32] + row_part[32:]
            raw[other] += col_part[:32] + col_part[32:]
        return carry

    distances(0)
    lax.fori_loop(0, (used + UNROLL - 1) // UNROLL, moment_group, 0)

    def window_leaf(seat):
        return jnp.where(seat <= cap, own_leaf(seat), upper_leaf(seat - cap - 1))

    def finish(seat, carry):
        leaf = window_leaf(seat)
        payload = finish_leaf(raw[leaf], local[leaf])
        pay[seat] = payload
        for k, entry in enumerate(far_coefficients(local[leaf], payload)):
            far_coef[seat, 8 * k : 8 * k + 8] = entry
        return carry

    lax.fori_loop(0, length + 1, finish, 0)
    lax.fori_loop(cap + 1, cap + length + 3, finish, 0)

    splits = LEAF // ROWS

    def turn_home(seat, carry):
        tile = local[own_leaf(seat)]
        for k, entry in enumerate(near_coefficients(tile, pay[seat])):
            turned = stack_near(entry).T
            for part in range(splits):
                near_left[seat * splits + part, k * ROWS : (k + 1) * ROWS, 0:48] = turned[
                    part * ROWS : (part + 1) * ROWS
                ]
        generic = {0: 1.0}
        generic.update({1 + k: tile[k : k + 1] for k in range(6)})
        plain = {0: 1.0}
        plain.update({1 + k: tile[3 + k : 4 + k] for k in range(5)})
        turned_far = stack_near(stack_rows(generic)).T
        turned_shared = stack_near(stack_rows(plain)).T
        for part in range(splits):
            rows = slice(part * ROWS, (part + 1) * ROWS)
            far_left[seat * splits + part, :, 0:48] = turned_far[rows]
            shared_left[seat * splits + part, :, 0:48] = turned_shared[rows]
        return carry

    lax.fori_loop(0, length, turn_home, 0)

    def prepare_slot(index, count):
        slot = mine[index]
        home = rec[0, slot]
        other = rec[1, slot]
        is_upper = rec[2, slot]
        step_x = is_upper.astype(F32)
        step_y = rec[3, slot].astype(F32)
        wrap = rec[4, slot].astype(F32)
        column = home - width
        away = other - width - is_upper * width
        other_seat = jnp.where(
            is_upper > 0,
            cap + 1 + lax.rem(away + width - upper_base, width),
            lax.rem(away + width - base, width),
        )
        for part in range(splits):
            item_left[count] = (column - base) * splits + part
            item_index[count] = index
            item_other[count] = other
            item_seat[count] = jnp.where(home == other, -1 - other_seat, other_seat)
            count = count + (info[8 + column] > part * ROWS).astype(jnp.int32)

        far = local[other] + displacement(step_x, step_y, wrap)
        row = lax.broadcasted_iota(jnp.int32, (8, LEAF), 0)
        pos = [far[k : k + 1] for k in range(3)]
        generic = {0: 1.0, 7: dot3(pos, pos)}
        generic.update({1 + k: far[k : k + 1] for k in range(6)})
        near_right[index] = stack_far(stack_rows(generic))
        for k in range(8):
            entry = far_coef[other_seat, 8 * k : 8 * k + 8]
            change = entry[1:2] * step_x + entry[2:3] * step_y
            if k == 4:
                change = change + 0.5 * wrap
            entry = jnp.where(row == 0, entry - change, entry)
            far_right[index, :, k * LEAF : (k + 1) * LEAF] = stack_far(entry)
        for k, entry in enumerate(shared_coefficients(far)):
            shared_right[index, :, k * LEAF : (k + 1) * LEAF] = stack_far(entry)
        return count

    item_count = lax.fori_loop(0, kept, prepare_slot, 0)
    item_left[item_count] = 0
    item_index[item_count] = 0

    def forms(position):
        index = item_index[position]
        left = item_left[position]
        near_form[...] = jnp.dot(
            near_left[left, :, 0:48], near_right[index], preferred_element_type=F32
        )
        far_form[...] = jnp.dot(
            far_left[left, :, 0:48], far_right[index], preferred_element_type=F32
        )
        shared_form[...] = jnp.dot(
            shared_left[left, :, 0:48], shared_right[index], preferred_element_type=F32
        )

    def flux_item(position, carry):
        left = item_left[position]
        other = item_other[position]
        coded = item_seat[position]
        other_seat = jnp.where(coded < 0, -1 - coded, coded)
        weight = jnp.where(coded < 0, 0.0, 1.0).astype(F32)
        fluxes = face_fluxes(
            [near_form[k * ROWS : (k + 1) * ROWS, :] for k in range(9)],
            [far_form[:, k * LEAF : (k + 1) * LEAF] for k in range(8)],
            [shared_form[:, k * LEAF : (k + 1) * LEAF] for k in range(8)],
            local[other, 6:7, :],
            local[other, 7:8, :],
        )
        forms(position + 1)
        for k in range(5):
            row_sum[left, k] += fluxes[k]
            col_sum[other_seat, 8 * k : 8 * k + 8] += weight * sum(
                fluxes[k][8 * j : 8 * j + 8] for j in range(ROWS // 8)
            )
        return carry

    forms(0)
    lax.fori_loop(0, item_count, flux_item, 0)

    lane = lax.broadcasted_iota(jnp.int32, (ROWS, LEAF), 1)

    def row_total(seat, carry):
        pieces = []
        for part in range(splits):
            total = jnp.zeros((ROWS, LEAF), F32)
            for c in range(5):
                reduced = jnp.sum(row_sum[seat * splits + part, c], axis=1, keepdims=True)
                total = jnp.where(lane == c, reduced, total)
            pieces.append(total)
        row_rate[seat] = jnp.concatenate(pieces, axis=0).T[0:8]
        return carry

    lax.fori_loop(0, length, row_total, 0)
    row_rate[length] = jnp.zeros((8, LEAF), F32)

    def rates(seat, less):
        leaf = window_leaf(seat)
        total = stack_rows(
            {
                k: jnp.sum(col_sum[seat, 8 * k : 8 * k + 8], axis=0, keepdims=True)
                for k in range(5)
            }
        )
        if less is not None:
            total = total - less
        live = local[leaf][0:1] < 0.5 * AWAY
        column = lax.rem(leaf, width)
        lanes = pl.ds(pl.multiple_of(column * LEAF, LEAF), LEAF)
        return lanes, jnp.where(live, total * pay[seat][0:1], 0.0)[0:5]

    def write_own(k, carry):
        lanes, value = rates(k, row_rate[k])
        own_out[:, lanes] = value
        return carry

    def write_upper(k, carry):
        lanes, value = rates(k, None)
        next_out[:, lanes] = value
        return carry

    lax.fori_loop(0, length + 1, write_own, 0)
    lax.fori_loop(cap + 1, cap + length + 3, write_upper, 0)


def shards(positions, velocity, density, pressure, counts, pair_list):
    width = counts.shape[0]
    slots = pair_list.shape[1]
    particles = width * LEAF
    sub_count = lax.axis_size("sub")
    leaf_sub = width // sub_count
    slab_index = lax.axis_index("slab")
    sub_index = lax.axis_index("sub")

    smem = pl.BlockSpec(memory_space=pltpu.SMEM)
    vmem = pl.BlockSpec(memory_space=pltpu.VMEM)
    lanes = -(-slots // LEAF) * LEAF
    packed = pl.pallas_call(
        functools.partial(pack_kernel, width, leaf_sub),
        out_shape=jax.ShapeDtypeStruct((8, particles + lanes), F32),
        in_specs=[smem, smem, vmem, vmem, vmem, vmem, vmem],
        out_specs=vmem,
        name="pack",
    )(
        jnp.stack([slab_index, sub_index]).astype(jnp.int32),
        counts,
        positions,
        velocity,
        density[None],
        pressure[None],
        pair_list,
    )
    lower = shifted(packed, "slab", 1)
    upper = shifted(packed, "slab", -1)
    beyond = shifted(packed, "slab", -2)

    lists = jnp.stack(
        [entry[0:4, particles : particles + slots] for entry in (lower, packed, upper)]
    )[None]
    mask = 1
    while mask < sub_count:
        lists = jnp.concatenate([lists, swapped(lists, "sub", mask)], axis=0)
        mask *= 2
    lists = lists.astype(jnp.int32)
    head, tail, offset = lists[:, :, 0], lists[:, :, 1], lists[:, :, 2]
    occupied = head >= 0
    head_col, tail_col = head % width, tail % width
    step_x = (head // width != tail // width).astype(jnp.int32)
    wrap = (tail // width < head // width).astype(jnp.int32)
    from_slab = jnp.arange(3, dtype=jnp.int32)[None, :, None]
    spare = 4 * width
    home = jnp.where(occupied, from_slab * width + head_col, spare)
    other = jnp.where(occupied, (from_slab + step_x) * width + tail_col, spare)
    step_y = tail_col + offset - head_col
    slot_count = sub_count * 3 * slots
    rec = jnp.stack([entry.reshape(-1) for entry in (home, other, step_x, step_y, wrap)])
    rec = jnp.concatenate([rec, jnp.array([[spare], [spare], [0], [0], [0]], jnp.int32)], axis=1)
    shift_w = jnp.max(
        jnp.where(occupied[:, 1] & (step_x[:, 1] > 0), (-offset[:, 1]) % width, 0)
    )
    info = jnp.concatenate(
        [
            sub_index[None],
            shift_w[None],
            jnp.zeros((6,), jnp.int32),
            counts,
            lists[:, 1, 3, :leaf_sub].reshape(-1),
        ]
    ).astype(jnp.int32)
    cap = 2 * leaf_sub
    most = cap * CAND
    splits = LEAF // ROWS

    own_part, next_part = pl.pallas_call(
        functools.partial(step_kernel, width, sub_count, slots),
        out_shape=[jax.ShapeDtypeStruct((5, particles), F32)] * 2,
        in_specs=[smem, smem, vmem, vmem, vmem, vmem],
        out_specs=[vmem, vmem],
        scratch_shapes=[
            pltpu.SMEM((slot_count + 2 * UNROLL,), jnp.int32),
            pltpu.SMEM((most + 1,), jnp.int32),
            pltpu.SMEM((4 * width + 1,), jnp.int32),
        ]
        + [pltpu.SMEM((most * splits + 1,), jnp.int32)] * 4
        + [
            pltpu.VMEM((4 * width + 1, 8, LEAF), F32),
            pltpu.VMEM((4 * width + 1, 32, LEAF), F32),
            pltpu.VMEM((2 * cap + 3, 24, LEAF), F32),
            pltpu.VMEM((2 * cap + 3, 64, LEAF), F32),
            pltpu.VMEM((cap * splits, 9 * ROWS, LEAF), BF16),
            pltpu.VMEM((cap * splits, ROWS, LEAF), BF16),
            pltpu.VMEM((cap * splits, ROWS, LEAF), BF16),
            pltpu.VMEM((most, 48, LEAF), BF16),
            pltpu.VMEM((most, 48, 8 * LEAF), BF16),
            pltpu.VMEM((most, 48, 8 * LEAF), BF16),
            pltpu.VMEM((UNROLL, LEAF, LEAF), F32),
            pltpu.VMEM((9 * ROWS, LEAF), F32),
            pltpu.VMEM((ROWS, 8 * LEAF), F32),
            pltpu.VMEM((ROWS, 8 * LEAF), F32),
            pltpu.VMEM((2 * cap + 3, 40, LEAF), F32),
            pltpu.VMEM((cap * splits, 5, ROWS, LEAF), F32),
            pltpu.VMEM((cap + 1, 8, LEAF), F32),
        ],
        compiler_params=pltpu.CompilerParams(vmem_limit_bytes=48 * 1024 * 1024),
        name="hydro_step",
    )(rec, info, lower, packed, upper, beyond)

    merged = own_part + shifted(next_part, "slab", 1)
    mask = 1
    while mask < sub_count:
        merged = merged + swapped(merged, "sub", mask)
        mask *= 2
    return merged


def solution(mesh):
    placed = (
        P(None, "slab"),
        P(None, "slab"),
        P("slab"),
        P("slab"),
        P("slab"),
        P(None, ("slab", "sub")),
    )
    return jax.shard_map(
        shards, mesh=mesh, in_specs=placed, out_specs=P(None, "slab"), check_vma=False
    )
```

```python
import functools
import math

import jax
import jax.numpy as jnp
from jax import lax
from jax.experimental import pallas as pl
from jax.experimental.pallas import tpu as pltpu
from jax.sharding import PartitionSpec as P

LEAF = 128
CAND = 5

GAMMA = 5.0 / 3.0
SUPPORT = 1.5
KERNEL_NORM = 21.0 / (2.0 * math.pi * SUPPORT**3)
MOMENT_REG = 0.05
AREA_FLOOR = 0.0001
AWAY = 64.0
UNROLL = 8
ROWS = 64
ROWS_LOG = 6
COST_LEAF, COST_SLOT, COST_PART = 17, 3, 5
F32 = jnp.float32
BF16 = jnp.bfloat16


def shifted(shard, axis, by):
    peers = lax.axis_size(axis)
    return lax.ppermute(shard, axis, [(i, (i + by) % peers) for i in range(peers)])


def swapped(shard, axis, mask):
    peers = lax.axis_size(axis)
    return lax.ppermute(shard, axis, [(i, i ^ mask) for i in range(peers)])


def reciprocal(value):
    return pl.reciprocal(value, approx=True)


def smoothing_of(dist_sq, scale):
    safe = jnp.maximum(dist_sq, 1e-12)
    radius = safe * lax.rsqrt(safe)
    inside = jnp.maximum(1.0 - radius, 0.0)
    square = inside * inside
    return (square * square) * (scale + (scale * 4.0) * radius)


def split_three(value):
    high = value.astype(BF16).astype(F32)
    rest = value - high
    middle = rest.astype(BF16).astype(F32)
    return high, middle, rest - middle


def stack_near(rows):
    high, middle, low = split_three(rows)
    return jnp.concatenate([high, high, high, middle, middle, low], axis=0).astype(BF16)


def stack_far(rows):
    high, middle, low = split_three(rows)
    return jnp.concatenate([high, middle, low, high, middle, high], axis=0).astype(BF16)


def bilinear(near_rows, far_rows):
    return lax.dot_general(
        stack_near(near_rows),
        stack_far(far_rows),
        (((0,), (0,)), ((), ())),
        preferred_element_type=F32,
    )


def moment_features(tile):
    row = lax.broadcasted_iota(jnp.int32, tile.shape, 0)
    by_x = tile * tile[0:1]
    by_y = jnp.where(row == 0, 1.0, tile * tile[1:2])
    by_z = tile * tile[2:3]
    whole = jnp.concatenate([tile, by_x, by_y, by_z], axis=0)
    high = whole.astype(BF16)
    low = (whole - high.astype(F32)).astype(BF16)
    both = jnp.concatenate([high, low], axis=0)
    return jnp.concatenate([both, both], axis=1)


def displacement(step_x, step_y, wrap):
    row = lax.broadcasted_iota(jnp.int32, (8, LEAF), 0)
    zero = jnp.zeros((8, LEAF), F32)
    out = jnp.where(row == 0, step_x, zero)
    out = jnp.where(row == 1, step_y, out)
    return jnp.where(row == 4, -wrap, out)


def finish_leaf(raw, tile):
    pos = [tile[k : k + 1] for k in range(3)]
    live = pos[0] < 0.5 * AWAY
    total = raw[16:17]
    first = [raw[k : k + 1] - pos[k] * total for k in range(3)]

    def second(left, right):
        lead = raw[8 + 8 * left + right : 9 + 8 * left + right]
        return lead - pos[left] * raw[right : right + 1] - pos[right] * first[left]

    density = jnp.where(live, total, 1.0)
    inverse_density = 1.0 / density

    def scaled(value):
        return jnp.where(live, value * inverse_density, 0.0)

    exx = scaled(second(0, 0)) + MOMENT_REG
    exy = scaled(second(0, 1))
    exz = scaled(second(0, 2))
    eyy = scaled(second(1, 1)) + MOMENT_REG
    eyz = scaled(second(1, 2))
    ezz = scaled(second(2, 2)) + MOMENT_REG
    mxx = eyy * ezz - eyz * eyz
    mxy = exz * eyz - exy * ezz
    mxz = exy * eyz - exz * eyy
    myy = exx * ezz - exz * exz
    myz = exy * exz - exx * eyz
    mzz = exx * eyy - exy * exy
    scale = 1.0 / (exx * mxx + exy * mxy + exz * mxz)
    inverse = [entry * scale for entry in (mxx, mxy, mxz, myy, myz, mzz)]
    square = inverse_density * inverse_density
    rows = [density] + [entry * square for entry in inverse]
    for quantity in range(3, 8):
        value = tile[quantity : quantity + 1]
        along = [
            scaled(
                raw[8 + 8 * k + quantity : 9 + 8 * k + quantity]
                - pos[k] * raw[quantity : quantity + 1]
                - value * first[k]
            )
            for k in range(3)
        ]
        half = [0.5 * term for term in along]
        rows.append(inverse[0] * half[0] + inverse[1] * half[1] + inverse[2] * half[2])
        rows.append(inverse[1] * half[0] + inverse[3] * half[1] + inverse[4] * half[2])
        rows.append(inverse[2] * half[0] + inverse[4] * half[1] + inverse[5] * half[2])
    rows.append(jnp.zeros((2, LEAF), F32))
    return jnp.concatenate(rows, axis=0)


def dot3(left, right):
    return left[0] * right[0] + left[1] * right[1] + left[2] * right[2]


def apply_sym(matrix, vector):
    return [
        dot3((matrix[0], matrix[1], matrix[2]), vector),
        dot3((matrix[1], matrix[3], matrix[4]), vector),
        dot3((matrix[2], matrix[4], matrix[5]), vector),
    ]


def stack_rows(rows):
    row = lax.broadcasted_iota(jnp.int32, (8, LEAF), 0)
    out = jnp.zeros((8, LEAF), F32)
    for k, entry in rows.items():
        out = jnp.where(row == k, entry, out)
    return out


def near_coefficients(tile, pay):
    pos = [tile[k : k + 1] for k in range(3)]
    twice = [(-2.0 / SUPPORT**2) * entry for entry in pos]
    out = [
        {
            0: dot3(pos, pos) * (1.0 / SUPPORT**2),
            1: twice[0],
            2: twice[1],
            3: twice[2],
            7: 1.0 / SUPPORT**2,
        }
    ]
    matrix = [pay[1 + k : 2 + k] for k in range(6)]
    for line in ((0, 1, 2), (1, 3, 4), (2, 4, 5)):
        entries = [matrix[k] for k in line]
        out.append({0: -dot3(entries, pos), 1: entries[0], 2: entries[1], 3: entries[2]})
    for quantity in range(5):
        slope = [pay[7 + 3 * quantity + k : 8 + 3 * quantity + k] for k in range(3)]
        value = tile[3 + quantity : 4 + quantity]
        if quantity < 3:
            entry = {0: 0.5 * value - dot3(slope, pos), 4 + quantity: -0.5}
        else:
            entry = {0: value - dot3(slope, pos)}
        entry.update({1: slope[0], 2: slope[1], 3: slope[2]})
        out.append(entry)
    return [stack_rows(entry) for entry in out]


def far_coefficients(tile, pay):
    pos = [tile[k : k + 1] for k in range(3)]
    out = []
    matrix = [pay[1 + k : 2 + k] for k in range(6)]
    for line in ((0, 1, 2), (1, 3, 4), (2, 4, 5)):
        entries = [matrix[k] for k in line]
        out.append({0: dot3(entries, pos), 1: -entries[0], 2: -entries[1], 3: -entries[2]})
    for quantity in range(5):
        slope = [pay[7 + 3 * quantity + k : 8 + 3 * quantity + k] for k in range(3)]
        value = tile[3 + quantity : 4 + quantity]
        if quantity < 3:
            entry = {0: 0.5 * value - dot3(slope, pos), 4 + quantity: -0.5}
        else:
            entry = {0: value - dot3(slope, pos)}
        entry.update({1: slope[0], 2: slope[1], 3: slope[2]})
        out.append(entry)
    return [stack_rows(entry) for entry in out]


def limited(value, low, high):
    return jnp.minimum(jnp.maximum(value, low), high)


def face_fluxes(near_out, far_out, toward, near_plain, far_plain):
    smooth = smoothing_of(near_out[0], KERNEL_NORM / AREA_FLOOR)
    length_sq = jnp.maximum(dot3(toward, toward), 1e-30)
    inverse_length = lax.rsqrt(length_sq)
    area = smooth * (length_sq * inverse_length)
    scale = jnp.minimum(inverse_length, smooth)
    normal = [entry * scale for entry in toward]
    left_vel, right_vel = [], []
    for k in range(3):
        high = jnp.abs(far_plain[k] - near_plain[k])
        low = -high
        left_vel.append(limited(near_out[1 + k], low, high))
        right_vel.append(limited(far_out[k], low, high))
    face_vel = [near_plain[k] + far_plain[k] for k in range(3)]
    thermo = []
    for k in range(2):
        low = jnp.minimum(near_plain[3 + k], far_plain[3 + k])
        high = jnp.maximum(near_plain[3 + k], far_plain[3 + k])
        thermo.append(limited(near_out[4 + k], low, high))
        thermo.append(limited(far_out[3 + k], low, high))
    left_rho, right_rho, left_p, right_p = thermo
    left_u = dot3(left_vel, normal)
    right_u = dot3(right_vel, normal)
    left_gp = GAMMA * left_p
    right_gp = GAMMA * right_p
    left_c = left_gp * lax.rsqrt(left_gp * left_rho)
    right_c = right_gp * lax.rsqrt(right_gp * right_rho)
    slow = jnp.minimum(left_u - left_c, right_u - right_c)
    fast = jnp.maximum(left_u + left_c, right_u + right_c)
    left_m = left_rho * (slow - left_u)
    right_m = right_rho * (fast - right_u)
    contact = (right_p - left_p + left_m * left_u - right_m * right_u) * reciprocal(
        left_m - right_m
    )
    is_left = contact >= 0.0
    speed = jnp.where(is_left, jnp.minimum(slow, 0.0), jnp.maximum(fast, 0.0))
    rho = jnp.where(is_left, left_rho, right_rho) * area
    press = jnp.where(is_left, left_p, right_p) * area
    normal_speed = jnp.where(is_left, left_u, right_u)
    vel = [jnp.where(is_left, left_vel[k], right_vel[k]) + face_vel[k] for k in range(3)]
    lag = speed - normal_speed
    ratio = lag * reciprocal(speed - contact)
    through = ratio * contact
    gain = speed * ratio - speed
    push = (rho * lag) * gain
    mass = rho * through
    total_p = press + push
    mom = [mass * vel[k] + total_p * normal[k] for k in range(3)]
    energy = press * (through * (1.0 / (GAMMA - 1.0)) + normal_speed + gain) + push * contact
    energy = energy + (0.5 * mass) * dot3(vel, vel) + total_p * dot3(face_vel, normal)
    return [mass] + mom + [energy]


def pack_kernel(
    width,
    leaf_sub,
    counts,
    positions,
    velocity,
    density,
    pressure,
    pair_list,
    state,
    listed,
):
    slab = lax.axis_index("slab")
    centre_x = slab.astype(F32) + 0.5
    row = lax.broadcasted_iota(jnp.int32, (3, LEAF), 0)
    lane = lax.broadcasted_iota(jnp.int32, (3, LEAF), 1)

    def one_leaf(column, carry):
        lanes = pl.ds(pl.multiple_of(column * LEAF, LEAF), LEAF)
        centre_y = column.astype(F32) + 0.5
        centre = jnp.where(row == 0, centre_x, jnp.where(row == 1, centre_y, 0.5))
        dead = (row == 0) & (lane >= counts[column])
        state[0:3, lanes] = jnp.where(dead, AWAY, positions[:, lanes] - centre)
        state[3:6, lanes] = velocity[:, lanes]
        state[6:7, lanes] = density[:, lanes]
        state[7:8, lanes] = pressure[:, lanes]
        return carry

    lax.fori_loop(0, width, one_leaf, 0, unroll=4)
    listed[...] = jnp.zeros(listed.shape, F32)
    slots = pair_list.shape[1]
    heads = pair_list[0:1, :]
    tails = pair_list[1:2, :]
    offsets = pair_list[2:3, :]
    occupied = heads >= 0
    head_col = heads - slab * width
    inside = (tails >= slab * width) & (tails < (slab + 1) * width)
    next_slab = lax.rem(slab + 1, lax.axis_size("slab"))
    tail_col = jnp.where(inside, tails - slab * width, tails - next_slab * width)
    outside = occupied & jnp.logical_not(inside)
    wraps = outside & (tails < heads)
    step_y = tail_col + offsets - head_col
    empty = 4 * width
    here = slice(0, slots)
    listed[0:1, here] = jnp.where(occupied, head_col, empty).astype(F32)
    listed[1:2, here] = jnp.where(
        occupied, jnp.where(inside, tail_col, tail_col + width), empty
    ).astype(F32)
    listed[2:3, here] = jnp.where(occupied, step_y, 0).astype(F32)
    listed[3:4, here] = jnp.where(wraps, 1.0, 0.0)
    seats = head_col - lax.axis_index("sub") * leaf_sub
    behind = lax.broadcasted_iota(jnp.int32, (1, leaf_sub + 1), 1)
    shifts = lax.rem(5 * width * LEAF - offsets, width)
    shift = jnp.max(jnp.where(outside, shifts, 0), axis=1, keepdims=True).astype(F32)
    facts = jnp.where(behind == leaf_sub, shift, 0.0)
    for k in range(leaf_sub):
        found = jnp.where(occupied & (seats == k), 1.0, 0.0)
        facts = jnp.where(behind == k, jnp.sum(found, axis=1, keepdims=True), facts)
    listed[3:4, slots : slots + leaf_sub + 1] = facts


def step_kernel(
    width,
    sub_count,
    slots,
    rec,
    counts,
    lower_ref,
    own_ref,
    upper_ref,
    beyond_ref,
    own_out,
    next_out,
    order,
    mine,
    need,
    costs,
    item_left,
    item_index,
    item_seat,
    local,
    raw,
    pay,
    far_coef,
    near_left,
    far_left,
    toward_left,
    near_plane,
    near_right,
    far_right,
    toward_right,
    far_half,
    spread,
    dist,
    near_form,
    far_form,
    toward_form,
    col_sum,
    row_sum,
    row_rate,
):
    whole = 4 * width
    leaf_sub = width // sub_count
    cap = 2 * leaf_sub
    stride = rec.shape[0] // (12 * sub_count)
    block = 4 * stride

    def slot_home(slot):
        return rec[slot]

    def slot_other(slot):
        return rec[slot + stride]

    def slot_step_y(slot):
        return rec[slot + 2 * stride].astype(F32)

    def slot_wrap(slot):
        return rec[slot + 3 * stride].astype(F32)

    def load_leaf(column, carry):
        lanes = pl.ds(pl.multiple_of(column * LEAF, LEAF), LEAF)
        local[column] = lower_ref[:, lanes]
        local[width + column] = own_ref[:, lanes]
        local[2 * width + column] = upper_ref[:, lanes]
        local[3 * width + column] = beyond_ref[:, lanes]
        for k in range(5):
            own_out[pl.ds(k * width + column, 1), :] = jnp.zeros((1, LEAF), F32)
            next_out[pl.ds(k * width + column, 1), :] = jnp.zeros((1, LEAF), F32)
        for slab in range(4):
            raw[slab * width + column] = jnp.zeros((32, LEAF), F32)
            need[slab * width + column] = 0
            need[(slab + 3) * width + column] = 0
        return carry

    lax.fori_loop(0, width, load_leaf, 0)
    local[whole] = jnp.zeros((8, LEAF), F32)
    raw[whole] = jnp.zeros((32, LEAF), F32)
    need[7 * width] = 0

    me = lax.axis_index("sub")
    total_cost = jnp.int32(0)
    shift_w = jnp.int32(0)
    for group in range(sub_count):
        seats = jnp.bitwise_xor(me, group) * leaf_sub
        facts = (3 * group + 1) * block + 3 * stride + slots
        shift_w = jnp.maximum(shift_w, rec[facts + leaf_sub])
        for k in range(leaf_sub):
            parts = lax.shift_right_logical(counts[seats + k] + (ROWS - 1), ROWS_LOG)
            cost = COST_LEAF + rec[facts + k] * (COST_SLOT + COST_PART * parts)
            costs[seats + k] = cost
            total_cost = total_cost + cost

    def deal(column, state):
        owner, length, before, first, mine_length = state
        cost = costs[column]
        middle = sub_count * (2 * before + cost)
        wish = (middle >= 2 * total_cost * (owner + 1)) | (length == cap)
        allowed = (owner < sub_count - 1) & (width - column <= (sub_count - 1 - owner) * cap)
        step = (wish & allowed).astype(jnp.int32)
        owner = owner + step
        length = (1 - step) * length + 1
        is_mine = (owner == me).astype(jnp.int32)
        first = jnp.where((is_mine > 0) & (mine_length == 0), column, first)
        return owner, length, before + cost, first, mine_length + is_mine

    zero = jnp.int32(0)
    _, _, _, base, length = lax.fori_loop(
        0, width, deal, (zero, zero, zero, zero, zero), unroll=4
    )
    upper_base = lax.rem(base + width - 1 + shift_w, width)

    def own_leaf(k):
        return width + lax.rem(base + k, width)

    def upper_leaf(k):
        return 2 * width + lax.rem(upper_base + k, width)

    def mark_own(k, carry):
        need[own_leaf(k)] = jnp.where(k < length, 3, 1)
        return carry

    def mark_upper(k, carry):
        need[upper_leaf(k)] = 1
        return carry

    lax.fori_loop(0, length + 1, mark_own, 0)
    lax.fori_loop(0, length + 2, mark_upper, 0)

    def collect_lower(k, carry):
        used, first = carry
        order[used] = first + k
        return used + (need[slot_other(first + k)] & 1), first

    def collect_own(k, carry):
        used, kept, first = carry
        slot = first + k
        flags = need[width + slot_home(slot)]
        order[used] = slot
        mine[kept] = slot
        used = used + ((flags | need[width + slot_other(slot)]) & 1)
        return used, kept + lax.shift_right_logical(flags, 1), first

    def collect_upper(k, carry):
        used, first = carry
        slot = first + k
        order[used] = slot
        flags = need[2 * width + slot_home(slot)] | need[2 * width + slot_other(slot)]
        return used + (flags & 1), first

    used, kept = zero, zero
    for group in range(sub_count):
        used, _ = lax.fori_loop(0, slots, collect_lower, (used, 3 * group * block), unroll=8)
    from_own = used
    for group in range(sub_count):
        used, kept, _ = lax.fori_loop(
            0, slots, collect_own, (used, kept, (3 * group + 1) * block), unroll=8
        )
    from_upper = used
    for group in range(sub_count):
        used, _ = lax.fori_loop(
            0, slots, collect_upper, (used, (3 * group + 2) * block), unroll=8
        )
    for extra in range(2 * UNROLL):
        order[used + extra] = -1

    def slab_base(position):
        return jnp.where(position < from_own, 0, jnp.where(position < from_upper, width, 2 * width))

    def clear_rows(seat, carry):
        for part in range(LEAF // ROWS):
            for k in range(5):
                row_sum[seat * (LEAF // ROWS) + part, k] = jnp.zeros((ROWS, LEAF), F32)
        return carry

    lax.fori_loop(0, length, clear_rows, 0)

    def clear_cols(seat, carry):
        col_sum[seat] = jnp.zeros((40, LEAF), F32)
        return carry

    lax.fori_loop(0, length + 1, clear_cols, 0)
    lax.fori_loop(cap + 1, cap + length + 3, clear_cols, 0)

    def slot_tiles(position):
        named = order[position]
        slot = jnp.maximum(named, 0)
        start = slab_base(position)
        other = slot_other(slot)
        shift = displacement(
            jnp.where(other >= width, 1.0, 0.0).astype(F32), slot_step_y(slot), slot_wrap(slot)
        )
        home = jnp.where(named < 0, whole, start + slot_home(slot))
        other = jnp.where(named < 0, whole, start + other)
        return home, other, local[home], local[other] + shift, shift

    def distances(group):
        row = lax.broadcasted_iota(jnp.int32, (8, LEAF), 0)
        for k in range(UNROLL):
            _, _, near, far, _ = slot_tiles(group * UNROLL + k)
            near_pos = [near[j : j + 1] for j in range(3)]
            far_pos = [far[j : j + 1] for j in range(3)]
            near_k = jnp.where(
                row < 3,
                near,
                jnp.where(row == 3, dot3(near_pos, near_pos), jnp.where(row == 4, 1.0, 0.0)),
            )
            far_k = jnp.where(
                row < 3,
                (-2.0 / SUPPORT**2) * far,
                jnp.where(
                    row == 4,
                    dot3(far_pos, far_pos) * (1.0 / SUPPORT**2),
                    jnp.where(row == 3, 1.0 / SUPPORT**2, 0.0),
                ),
            )
            dist[k] = bilinear(near_k, far_k)

    def moment_group(group, carry):
        parts = []
        for k in range(UNROLL):
            home, other, near, far, shift = slot_tiles(group * UNROLL + k)
            weight = jnp.where(home == other, 0.5, 1.0).astype(F32)
            smooth = smoothing_of(dist[k], KERNEL_NORM * weight)
            high = smooth.astype(BF16)
            low = (smooth - high.astype(F32)).astype(BF16)
            row_part = lax.dot_general(
                moment_features(far),
                jnp.concatenate([high, low], axis=1),
                (((1,), (1,)), ((), ())),
                preferred_element_type=F32,
            )
            col_part = lax.dot_general(
                moment_features(near - shift),
                jnp.concatenate([high, low], axis=0),
                (((1,), (0,)), ((), ())),
                preferred_element_type=F32,
            )
            parts.append((home, other, row_part, col_part))
        distances(group + 1)
        for home, other, row_part, col_part in parts:
            raw[home] += row_part[:32] + row_part[32:]
            raw[other] += col_part[:32] + col_part[32:]
        return carry

    distances(0)
    lax.fori_loop(0, (used + UNROLL - 1) // UNROLL, moment_group, 0)

    def window_leaf(seat):
        return jnp.where(seat <= cap, own_leaf(seat), upper_leaf(seat - cap - 1))

    def finish(seat, carry):
        leaf = window_leaf(seat)
        payload = finish_leaf(raw[leaf], local[leaf])
        pay[seat] = payload
        for k, entry in enumerate(far_coefficients(local[leaf], payload)):
            far_coef[seat, 8 * k : 8 * k + 8] = entry
        return carry

    lax.fori_loop(0, length + 1, finish, 0)
    lax.fori_loop(cap + 1, cap + length + 3, finish, 0)

    splits = LEAF // ROWS

    picked = lax.broadcasted_iota(jnp.int32, (48, LEAF), 0)
    for k in range(5):
        chosen = (picked == 3 + k) | (picked == 27 + k) | (picked == 43 + k)
        spread[:, k * LEAF : (k + 1) * LEAF] = jnp.where(chosen, 0.5 if k < 3 else 1.0, 0.0).astype(
            BF16
        )

    def turn_home(seat):
        tile = local[own_leaf(seat)]
        generic = {0: 1.0}
        generic.update({1 + k: tile[k : k + 1] for k in range(6)})
        generic = stack_near(stack_rows(generic))
        coefficients = [stack_near(entry) for entry in near_coefficients(tile, pay[seat])]
        planes = jnp.dot(stack_near(tile).T, spread[...], preferred_element_type=F32)
        turned_far = generic.T
        turned_near = [coefficients[k].T for k in (0, 4, 5, 6, 7, 8)]
        turned_toward = [
            jnp.concatenate([coefficients[1 + k], generic], axis=0).T for k in range(3)
        ]
        for part in range(splits):
            rows = slice(part * ROWS, (part + 1) * ROWS)
            place = seat * splits + part
            for k in range(6):
                near_left[place, k * ROWS : (k + 1) * ROWS, 0:48] = turned_near[k][rows]
            for k in range(3):
                toward_left[place, k * ROWS : (k + 1) * ROWS, 0:96] = turned_toward[k][rows]
            far_left[place, :, 0:48] = turned_far[rows]
            for k in range(5):
                near_plane[place, k] = planes[rows, k * LEAF : (k + 1) * LEAF]

    def turn_two(pair, carry):
        turn_home(2 * pair)
        turn_home(2 * pair + 1)
        return carry

    lax.fori_loop(0, (length + 1) // 2, turn_two, 0)

    def prepare_slot(index, count):
        slot = mine[index]
        valid = (index < kept).astype(jnp.int32)
        column = slot_home(slot)
        away = slot_other(slot)
        is_upper = away >= width
        other = width + away
        step_x = jnp.where(is_upper, 1.0, 0.0).astype(F32)
        step_y = slot_step_y(slot)
        wrap = slot_wrap(slot)
        other_seat = jnp.where(
            is_upper,
            cap + 1 + lax.rem(away - upper_base, width),
            lax.rem(away + width - base, width),
        )
        for part in range(splits):
            item_left[count] = (column - base) * splits + part
            item_index[count] = index
            item_seat[count] = jnp.where(column == away, -1 - other_seat, other_seat)
            count = count + valid * (counts[column] > part * ROWS).astype(jnp.int32)

        far = local[other] + displacement(step_x, step_y, wrap)
        row = lax.broadcasted_iota(jnp.int32, (8, LEAF), 0)
        pos = [far[k : k + 1] for k in range(3)]
        generic = {0: 1.0, 7: dot3(pos, pos)}
        generic.update({1 + k: far[k : k + 1] for k in range(6)})
        generic = stack_far(stack_rows(generic))
        near_right[index] = generic
        for k in range(8):
            entry = far_coef[other_seat, 8 * k : 8 * k + 8]
            change = entry[1:2] * step_x + entry[2:3] * step_y
            if k == 4:
                change = change + 0.5 * wrap
            entry = stack_far(jnp.where(row == 0, entry - change, entry))
            if k < 3:
                toward_right[index, 0:48, k * LEAF : (k + 1) * LEAF] = generic
                toward_right[index, 48:96, k * LEAF : (k + 1) * LEAF] = entry
            else:
                far_right[index, :, (k - 3) * LEAF : (k - 2) * LEAF] = entry
        far_half[index, 0:5] = jnp.concatenate([0.5 * far[3:6], far[6:8]], axis=0)
        return count

    def prepare_two(pair, count):
        return prepare_slot(2 * pair + 1, prepare_slot(2 * pair, count))

    mine[kept] = mine[0]
    item_count = lax.fori_loop(0, (kept + 1) // 2, prepare_two, 0)
    item_left[item_count] = 0
    item_index[item_count] = 0

    def forms(position):
        index = item_index[position]
        left = item_left[position]
        near_form[...] = jnp.dot(
            near_left[left, :, 0:48], near_right[index], preferred_element_type=F32
        )
        far_form[...] = jnp.dot(
            far_left[left, :, 0:48], far_right[index], preferred_element_type=F32
        )
        for k in range(3):
            toward_form[k * ROWS : (k + 1) * ROWS, :] = jnp.dot(
                toward_left[left, k * ROWS : (k + 1) * ROWS, 0:96],
                toward_right[index, :, k * LEAF : (k + 1) * LEAF],
                preferred_element_type=F32,
            )

    def flux_item(position, carry):
        left = item_left[position]
        index = item_index[position]
        coded = item_seat[position]
        other_seat = jnp.where(coded < 0, -1 - coded, coded)
        weight = jnp.where(coded < 0, 0.0, 1.0).astype(F32)
        fluxes = face_fluxes(
            [near_form[k * ROWS : (k + 1) * ROWS, :] for k in range(6)],
            [far_form[:, k * LEAF : (k + 1) * LEAF] for k in range(5)],
            [toward_form[k * ROWS : (k + 1) * ROWS, :] for k in range(3)],
            [near_plane[left, k] for k in range(5)],
            [far_half[index, k : k + 1, :] for k in range(5)],
        )
        forms(position + 1)
        for k in range(5):
            row_sum[left, k] += fluxes[k]
            col_sum[other_seat, 8 * k : 8 * k + 8] += weight * sum(
                fluxes[k][8 * j : 8 * j + 8] for j in range(ROWS // 8)
            )
        return carry

    forms(0)
    lax.fori_loop(0, item_count, flux_item, 0)

    lane = lax.broadcasted_iota(jnp.int32, (ROWS, LEAF), 1)

    def row_total(seat, carry):
        pieces = []
        for part in range(splits):
            total = jnp.zeros((ROWS, LEAF), F32)
            for c in range(5):
                reduced = jnp.sum(row_sum[seat * splits + part, c], axis=1, keepdims=True)
                total = jnp.where(lane == c, reduced, total)
            pieces.append(total)
        row_rate[seat] = jnp.concatenate(pieces, axis=0).T[0:8]
        return carry

    lax.fori_loop(0, length, row_total, 0)
    row_rate[length] = jnp.zeros((8, LEAF), F32)

    def rates(seat, less):
        leaf = window_leaf(seat)
        total = stack_rows(
            {
                k: jnp.sum(col_sum[seat, 8 * k : 8 * k + 8], axis=0, keepdims=True)
                for k in range(5)
            }
        )
        if less is not None:
            total = total - less
        live = local[leaf][0:1] < 0.5 * AWAY
        scale = AREA_FLOOR * pay[seat][0:1]
        return lax.rem(leaf, width), jnp.where(live, total * scale, 0.0)

    def write_own(k, carry):
        column, value = rates(k, row_rate[k])
        for c in range(5):
            own_out[pl.ds(c * width + column, 1), :] = value[c : c + 1]
        return carry

    def write_upper(k, carry):
        column, value = rates(k, None)
        for c in range(5):
            next_out[pl.ds(c * width + column, 1), :] = value[c : c + 1]
        return carry

    lax.fori_loop(0, length + 1, write_own, 0)
    lax.fori_loop(cap + 1, cap + length + 3, write_upper, 0)


def shards(positions, velocity, density, pressure, counts, pair_list):
    width = counts.shape[0]
    slots = pair_list.shape[1]
    particles = width * LEAF
    sub_count = lax.axis_size("sub")
    leaf_sub = width // sub_count

    smem = pl.BlockSpec(memory_space=pltpu.SMEM)
    vmem = pl.BlockSpec(memory_space=pltpu.VMEM)
    lanes = -(-(slots + leaf_sub + 1) // LEAF) * LEAF
    state, listed = pl.pallas_call(
        functools.partial(pack_kernel, width, leaf_sub),
        out_shape=[
            jax.ShapeDtypeStruct((8, particles), F32),
            jax.ShapeDtypeStruct((4, lanes), F32),
        ],
        in_specs=[smem, vmem, vmem, vmem, vmem, vmem],
        out_specs=[vmem, vmem],
        name="pack",
    )(
        counts,
        positions,
        velocity,
        density[None],
        pressure[None],
        pair_list,
    )
    lists = jnp.stack([shifted(listed, "slab", 1), listed, shifted(listed, "slab", -1)])[None]
    lower = shifted(state, "slab", 1)
    upper = shifted(state, "slab", -1)
    beyond = shifted(state, "slab", -2)
    mask = 1
    while mask < sub_count:
        lists = jnp.concatenate([lists, swapped(lists, "sub", mask)], axis=0)
        mask *= 2
    rec = lists.astype(jnp.int32).reshape(-1)
    cap = 2 * leaf_sub
    most = cap * CAND
    splits = LEAF // ROWS

    own_part, next_part = pl.pallas_call(
        functools.partial(step_kernel, width, sub_count, slots),
        out_shape=[jax.ShapeDtypeStruct((5 * width, LEAF), F32)] * 2,
        in_specs=[smem, smem, vmem, vmem, vmem, vmem],
        out_specs=[vmem, vmem],
        scratch_shapes=[
            pltpu.SMEM((3 * sub_count * slots + 2 * UNROLL,), jnp.int32),
            pltpu.SMEM((most + 1,), jnp.int32),
            pltpu.SMEM((7 * width + 1,), jnp.int32),
            pltpu.SMEM((width,), jnp.int32),
        ]
        + [pltpu.SMEM((most * splits + 1,), jnp.int32)] * 3
        + [
            pltpu.VMEM((4 * width + 1, 8, LEAF), F32),
            pltpu.VMEM((4 * width + 1, 32, LEAF), F32),
            pltpu.VMEM((2 * cap + 3, 24, LEAF), F32),
            pltpu.VMEM((2 * cap + 3, 64, LEAF), F32),
            pltpu.VMEM((cap * splits, 6 * ROWS, LEAF), BF16),
            pltpu.VMEM((cap * splits, ROWS, LEAF), BF16),
            pltpu.VMEM((cap * splits, 3 * ROWS, LEAF), BF16),
            pltpu.VMEM((cap * splits, 5, ROWS, LEAF), F32),
            pltpu.VMEM((most, 48, LEAF), BF16),
            pltpu.VMEM((most, 48, 5 * LEAF), BF16),
            pltpu.VMEM((most, 96, 3 * LEAF), BF16),
            pltpu.VMEM((most, 8, LEAF), F32),
            pltpu.VMEM((48, 5 * LEAF), BF16),
            pltpu.VMEM((UNROLL, LEAF, LEAF), F32),
            pltpu.VMEM((6 * ROWS, LEAF), F32),
            pltpu.VMEM((ROWS, 5 * LEAF), F32),
            pltpu.VMEM((3 * ROWS, LEAF), F32),
            pltpu.VMEM((2 * cap + 3, 40, LEAF), F32),
            pltpu.VMEM((cap * splits, 5, ROWS, LEAF), F32),
            pltpu.VMEM((cap + 1, 8, LEAF), F32),
        ],
        compiler_params=pltpu.CompilerParams(vmem_limit_bytes=48 * 1024 * 1024),
        name="hydro_step",
    )(rec, counts, lower, state, upper, beyond)

    merged = own_part + shifted(next_part, "slab", 1)
    mask = 1
    while mask < sub_count:
        merged = merged + swapped(merged, "sub", mask)
        mask *= 2
    return merged.reshape(5, particles)


def solution(mesh):
    placed = (
        P(None, "slab"),
        P(None, "slab"),
        P("slab"),
        P("slab"),
        P("slab"),
        P(None, ("slab", "sub")),
    )
    return jax.shard_map(
        shards, mesh=mesh, in_specs=placed, out_specs=P(None, "slab"), check_vma=False
    )
```

```python
import functools
import math

import jax
import jax.numpy as jnp
from jax import lax
from jax.experimental import pallas as pl
from jax.experimental.pallas import tpu as pltpu
from jax.sharding import PartitionSpec as P

LEAF = 128
CAND = 5

GAMMA = 5.0 / 3.0
SUPPORT = 1.5
KERNEL_NORM = 21.0 / (2.0 * math.pi * SUPPORT**3)
MOMENT_REG = 0.05
AREA_FLOOR = 0.0001
AWAY = 64.0
UNROLL = 8
ROWS = 64
ROWS_LOG = 6
COST_LEAF, COST_SLOT, COST_PART = 17, 3, 5
F32 = jnp.float32
BF16 = jnp.bfloat16


def shifted(shard, axis, by):
    peers = lax.axis_size(axis)
    return lax.ppermute(shard, axis, [(i, (i + by) % peers) for i in range(peers)])


def swapped(shard, axis, mask):
    peers = lax.axis_size(axis)
    return lax.ppermute(shard, axis, [(i, i ^ mask) for i in range(peers)])


def reciprocal(value):
    return pl.reciprocal(value, approx=True)


def smoothing_of(dist_sq, scale):
    safe = jnp.maximum(dist_sq, 1e-12)
    radius = safe * lax.rsqrt(safe)
    inside = jnp.maximum(1.0 - radius, 0.0)
    square = inside * inside
    return (square * square) * (scale + (scale * 4.0) * radius)


def split_three(value):
    high = value.astype(BF16).astype(F32)
    rest = value - high
    middle = rest.astype(BF16).astype(F32)
    return high, middle, rest - middle


def stack_near(rows):
    high, middle, low = split_three(rows)
    return jnp.concatenate([high, high, high, middle, middle, low], axis=0).astype(BF16)


def stack_far(rows):
    high, middle, low = split_three(rows)
    return jnp.concatenate([high, middle, low, high, middle, high], axis=0).astype(BF16)


def bilinear(near_rows, far_rows):
    return lax.dot_general(
        stack_near(near_rows),
        stack_far(far_rows),
        (((0,), (0,)), ((), ())),
        preferred_element_type=F32,
    )


def moment_features(tile):
    row = lax.broadcasted_iota(jnp.int32, tile.shape, 0)
    by_x = tile * tile[0:1]
    by_y = jnp.where(row == 0, 1.0, tile * tile[1:2])
    by_z = tile * tile[2:3]
    whole = jnp.concatenate([tile, by_x, by_y, by_z], axis=0)
    high = whole.astype(BF16)
    low = (whole - high.astype(F32)).astype(BF16)
    both = jnp.concatenate([high, low], axis=0)
    return jnp.concatenate([both, both], axis=1)


def displacement(step_x, step_y, wrap):
    row = lax.broadcasted_iota(jnp.int32, (8, LEAF), 0)
    zero = jnp.zeros((8, LEAF), F32)
    out = jnp.where(row == 0, step_x, zero)
    out = jnp.where(row == 1, step_y, out)
    return jnp.where(row == 4, -wrap, out)


def finish_leaf(raw, tile):
    pos = [tile[k : k + 1] for k in range(3)]
    live = pos[0] < 0.5 * AWAY
    total = raw[16:17]
    first = [raw[k : k + 1] - pos[k] * total for k in range(3)]

    def second(left, right):
        lead = raw[8 + 8 * left + right : 9 + 8 * left + right]
        return lead - pos[left] * raw[right : right + 1] - pos[right] * first[left]

    density = jnp.where(live, total, 1.0)
    inverse_density = 1.0 / density

    def scaled(value):
        return jnp.where(live, value * inverse_density, 0.0)

    exx = scaled(second(0, 0)) + MOMENT_REG
    exy = scaled(second(0, 1))
    exz = scaled(second(0, 2))
    eyy = scaled(second(1, 1)) + MOMENT_REG
    eyz = scaled(second(1, 2))
    ezz = scaled(second(2, 2)) + MOMENT_REG
    mxx = eyy * ezz - eyz * eyz
    mxy = exz * eyz - exy * ezz
    mxz = exy * eyz - exz * eyy
    myy = exx * ezz - exz * exz
    myz = exy * exz - exx * eyz
    mzz = exx * eyy - exy * exy
    scale = 1.0 / (exx * mxx + exy * mxy + exz * mxz)
    inverse = [entry * scale for entry in (mxx, mxy, mxz, myy, myz, mzz)]
    square = inverse_density * inverse_density
    rows = [density] + [entry * square for entry in inverse]
    for quantity in range(3, 8):
        value = tile[quantity : quantity + 1]
        along = [
            scaled(
                raw[8 + 8 * k + quantity : 9 + 8 * k + quantity]
                - pos[k] * raw[quantity : quantity + 1]
                - value * first[k]
            )
            for k in range(3)
        ]
        half = [0.5 * term for term in along]
        rows.append(inverse[0] * half[0] + inverse[1] * half[1] + inverse[2] * half[2])
        rows.append(inverse[1] * half[0] + inverse[3] * half[1] + inverse[4] * half[2])
        rows.append(inverse[2] * half[0] + inverse[4] * half[1] + inverse[5] * half[2])
    rows.append(jnp.zeros((2, LEAF), F32))
    return jnp.concatenate(rows, axis=0)


def dot3(left, right):
    return left[0] * right[0] + left[1] * right[1] + left[2] * right[2]


def apply_sym(matrix, vector):
    return [
        dot3((matrix[0], matrix[1], matrix[2]), vector),
        dot3((matrix[1], matrix[3], matrix[4]), vector),
        dot3((matrix[2], matrix[4], matrix[5]), vector),
    ]


def stack_rows(rows):
    row = lax.broadcasted_iota(jnp.int32, (8, LEAF), 0)
    out = jnp.zeros((8, LEAF), F32)
    for k, entry in rows.items():
        out = jnp.where(row == k, entry, out)
    return out


def near_coefficients(tile, pay):
    pos = [tile[k : k + 1] for k in range(3)]
    twice = [(-2.0 / SUPPORT**2) * entry for entry in pos]
    out = [
        {
            0: dot3(pos, pos) * (1.0 / SUPPORT**2),
            1: twice[0],
            2: twice[1],
            3: twice[2],
            7: 1.0 / SUPPORT**2,
        }
    ]
    matrix = [pay[1 + k : 2 + k] for k in range(6)]
    for line in ((0, 1, 2), (1, 3, 4), (2, 4, 5)):
        entries = [matrix[k] for k in line]
        out.append({0: -dot3(entries, pos), 1: entries[0], 2: entries[1], 3: entries[2]})
    for quantity in range(5):
        slope = [pay[7 + 3 * quantity + k : 8 + 3 * quantity + k] for k in range(3)]
        value = tile[3 + quantity : 4 + quantity]
        if quantity < 3:
            entry = {0: 0.5 * value - dot3(slope, pos), 4 + quantity: -0.5}
        else:
            entry = {0: value - dot3(slope, pos)}
        entry.update({1: slope[0], 2: slope[1], 3: slope[2]})
        out.append(entry)
    return [stack_rows(entry) for entry in out]


def far_coefficients(tile, pay):
    pos = [tile[k : k + 1] for k in range(3)]
    out = []
    matrix = [pay[1 + k : 2 + k] for k in range(6)]
    for line in ((0, 1, 2), (1, 3, 4), (2, 4, 5)):
        entries = [matrix[k] for k in line]
        out.append({0: dot3(entries, pos), 1: -entries[0], 2: -entries[1], 3: -entries[2]})
    for quantity in range(5):
        slope = [pay[7 + 3 * quantity + k : 8 + 3 * quantity + k] for k in range(3)]
        value = tile[3 + quantity : 4 + quantity]
        if quantity < 3:
            entry = {0: 0.5 * value - dot3(slope, pos), 4 + quantity: -0.5}
        else:
            entry = {0: value - dot3(slope, pos)}
        entry.update({1: slope[0], 2: slope[1], 3: slope[2]})
        out.append(entry)
    return [stack_rows(entry) for entry in out]


def limited(value, low, high):
    return jnp.minimum(jnp.maximum(value, low), high)


def face_geometry(dist_sq, toward):
    smooth = smoothing_of(dist_sq, KERNEL_NORM / AREA_FLOOR)
    length_sq = jnp.maximum(dot3(toward, toward), 1e-30)
    inverse_length = lax.rsqrt(length_sq)
    area = smooth * (length_sq * inverse_length)
    scale = jnp.minimum(inverse_length, smooth)
    return [entry * scale for entry in toward] + [area]


def face_fluxes(near_out, far_out, normal, area, near_plain, far_plain):
    left_vel, right_vel = [], []
    for k in range(3):
        high = jnp.abs(far_plain[k] - near_plain[k])
        low = -high
        left_vel.append(limited(near_out[k], low, high))
        right_vel.append(limited(far_out[k], low, high))
    face_vel = [near_plain[k] + far_plain[k] for k in range(3)]
    thermo = []
    for k in range(2):
        low = jnp.minimum(near_plain[3 + k], far_plain[3 + k])
        high = jnp.maximum(near_plain[3 + k], far_plain[3 + k])
        thermo.append(limited(near_out[3 + k], low, high))
        thermo.append(limited(far_out[3 + k], low, high))
    left_rho, right_rho, left_p, right_p = thermo
    left_u = dot3(left_vel, normal)
    right_u = dot3(right_vel, normal)
    left_gp = GAMMA * left_p
    right_gp = GAMMA * right_p
    left_c = left_gp * lax.rsqrt(left_gp * left_rho)
    right_c = right_gp * lax.rsqrt(right_gp * right_rho)
    slow = jnp.minimum(left_u - left_c, right_u - right_c)
    fast = jnp.maximum(left_u + left_c, right_u + right_c)
    left_m = left_rho * (slow - left_u)
    right_m = right_rho * (fast - right_u)
    contact = (right_p - left_p + left_m * left_u - right_m * right_u) * reciprocal(
        left_m - right_m
    )
    is_left = contact >= 0.0
    speed = jnp.where(is_left, jnp.minimum(slow, 0.0), jnp.maximum(fast, 0.0))
    rho = jnp.where(is_left, left_rho, right_rho) * area
    press = jnp.where(is_left, left_p, right_p) * area
    normal_speed = jnp.where(is_left, left_u, right_u)
    vel = [jnp.where(is_left, left_vel[k], right_vel[k]) + face_vel[k] for k in range(3)]
    lag = speed - normal_speed
    ratio = lag * reciprocal(speed - contact)
    through = ratio * contact
    gain = speed * ratio - speed
    push = (rho * lag) * gain
    mass = rho * through
    total_p = press + push
    mom = [mass * vel[k] + total_p * normal[k] for k in range(3)]
    energy = press * (through * (1.0 / (GAMMA - 1.0)) + normal_speed + gain) + push * contact
    energy = energy + (0.5 * mass) * dot3(vel, vel) + total_p * dot3(face_vel, normal)
    return [mass] + mom + [energy]


def pack_kernel(
    width,
    leaf_sub,
    counts,
    counts_row,
    positions,
    velocity,
    density,
    pressure,
    pair_list,
    state,
    listed,
):
    slab = lax.axis_index("slab")
    centre_x = slab.astype(F32) + 0.5
    row = lax.broadcasted_iota(jnp.int32, (3, LEAF), 0)
    lane = lax.broadcasted_iota(jnp.int32, (3, LEAF), 1)

    def one_leaf(column, carry):
        lanes = pl.ds(pl.multiple_of(column * LEAF, LEAF), LEAF)
        centre_y = column.astype(F32) + 0.5
        centre = jnp.where(row == 0, centre_x, jnp.where(row == 1, centre_y, 0.5))
        dead = (row == 0) & (lane >= counts[column])
        state[0:3, lanes] = jnp.where(dead, AWAY, positions[:, lanes] - centre)
        state[3:6, lanes] = velocity[:, lanes]
        state[6:7, lanes] = density[:, lanes]
        state[7:8, lanes] = pressure[:, lanes]
        return carry

    lax.fori_loop(0, width, one_leaf, 0, unroll=4)
    listed[...] = jnp.zeros(listed.shape, F32)
    slots = pair_list.shape[1]
    heads = pair_list[0:1, :]
    tails = pair_list[1:2, :]
    offsets = pair_list[2:3, :]
    occupied = heads >= 0
    head_col = heads - slab * width
    inside = (tails >= slab * width) & (tails < (slab + 1) * width)
    next_slab = lax.rem(slab + 1, lax.axis_size("slab"))
    tail_col = jnp.where(inside, tails - slab * width, tails - next_slab * width)
    outside = occupied & jnp.logical_not(inside)
    wraps = outside & (tails < heads)
    step_y = tail_col + offsets - head_col
    empty = 4 * width
    here = slice(0, slots)
    listed[0:1, here] = jnp.where(occupied, head_col, empty).astype(F32)
    listed[0:1, slots : slots + width] = counts_row[...].astype(F32)
    listed[1:2, here] = jnp.where(
        occupied, jnp.where(inside, tail_col, tail_col + width), empty
    ).astype(F32)
    listed[2:3, here] = jnp.where(occupied, step_y, 0).astype(F32)
    listed[3:4, here] = jnp.where(wraps, 1.0, 0.0)
    seats = head_col - lax.axis_index("sub") * leaf_sub
    behind = lax.broadcasted_iota(jnp.int32, (1, leaf_sub + 1), 1)
    shifts = lax.rem(5 * width * LEAF - offsets, width)
    shift = jnp.max(jnp.where(outside, shifts, 0), axis=1, keepdims=True).astype(F32)
    facts = jnp.where(behind == leaf_sub, shift, 0.0)
    for k in range(leaf_sub):
        found = jnp.where(occupied & (seats == k), 1.0, 0.0)
        facts = jnp.where(behind == k, jnp.sum(found, axis=1, keepdims=True), facts)
    listed[3:4, slots : slots + leaf_sub + 1] = facts


def step_kernel(
    width,
    sub_count,
    slots,
    rec,
    lower_ref,
    own_ref,
    upper_ref,
    beyond_ref,
    own_out,
    next_out,
    order,
    mine,
    need,
    costs,
    item_left,
    item_index,
    item_seat,
    local,
    raw,
    pay,
    far_coef,
    near_left,
    far_left,
    toward_left,
    near_plane,
    near_right,
    far_right,
    toward_right,
    far_half,
    spread,
    dist,
    near_form,
    far_form,
    toward_form,
    dist_form,
    geo_form,
    col_sum,
    row_sum,
    row_rate,
):
    whole = 4 * width
    leaf_sub = width // sub_count
    cap = 2 * leaf_sub
    stride = rec.shape[0] // (12 * sub_count)
    block = 4 * stride

    def count_of(column):
        return rec[block + slots + column]

    def slot_home(slot):
        return rec[slot]

    def slot_other(slot):
        return rec[slot + stride]

    def slot_step_y(slot):
        return rec[slot + 2 * stride].astype(F32)

    def slot_wrap(slot):
        return rec[slot + 3 * stride].astype(F32)

    def clear_need(entry, carry):
        need[entry] = 0
        return carry

    lax.fori_loop(0, 7 * width, clear_need, 0, unroll=16)
    need[7 * width] = 0

    me = lax.axis_index("sub")
    total_cost = jnp.int32(0)
    shift_w = jnp.int32(0)
    for group in range(sub_count):
        seats = jnp.bitwise_xor(me, group) * leaf_sub
        facts = (3 * group + 1) * block + 3 * stride + slots
        shift_w = jnp.maximum(shift_w, rec[facts + leaf_sub])
        for k in range(leaf_sub):
            parts = lax.shift_right_logical(count_of(seats + k) + (ROWS - 1), ROWS_LOG)
            cost = COST_LEAF + rec[facts + k] * (COST_SLOT + COST_PART * parts)
            costs[seats + k] = cost
            total_cost = total_cost + cost

    def deal(column, state):
        owner, length, before, first, mine_length = state
        cost = costs[column]
        middle = sub_count * (2 * before + cost)
        wish = (middle >= 2 * total_cost * (owner + 1)) | (length == cap)
        allowed = (owner < sub_count - 1) & (width - column <= (sub_count - 1 - owner) * cap)
        step = (wish & allowed).astype(jnp.int32)
        owner = owner + step
        length = (1 - step) * length + 1
        is_mine = (owner == me).astype(jnp.int32)
        first = jnp.where((is_mine > 0) & (mine_length == 0), column, first)
        return owner, length, before + cost, first, mine_length + is_mine

    zero = jnp.int32(0)
    _, _, _, base, length = lax.fori_loop(
        0, width, deal, (zero, zero, zero, zero, zero), unroll=4
    )
    upper_base = lax.rem(base + width - 1 + shift_w, width)

    def own_leaf(k):
        return width + lax.rem(base + k, width)

    def upper_leaf(k):
        return 2 * width + lax.rem(upper_base + k, width)

    def mark_own(k, carry):
        need[own_leaf(k)] = jnp.where(k < length, 3, 1)
        return carry

    def mark_upper(k, carry):
        need[upper_leaf(k)] = 1
        return carry

    lax.fori_loop(0, length + 1, mark_own, 0)
    lax.fori_loop(0, length + 2, mark_upper, 0)

    def collect_lower(k, carry):
        used, first = carry
        order[used] = first + k
        return used + (need[slot_other(first + k)] & 1), first

    def collect_own(k, carry):
        used, kept, first = carry
        slot = first + k
        flags = need[width + slot_home(slot)]
        order[used] = slot
        mine[kept] = slot
        used = used + ((flags | need[width + slot_other(slot)]) & 1)
        return used, kept + lax.shift_right_logical(flags, 1), first

    def collect_upper(k, carry):
        used, first = carry
        slot = first + k
        order[used] = slot
        flags = need[2 * width + slot_home(slot)] | need[2 * width + slot_other(slot)]
        return used + (flags & 1), first

    def touches(first, last, start, count):
        ahead = lax.rem(first - start + 4 * width, width) < count
        return ahead | (lax.rem(start - first + 4 * width, width) <= last - first)

    used, kept = zero, zero
    for group in range(sub_count):
        first = jnp.bitwise_xor(me, group) * leaf_sub
        slot = 3 * group * block
        moved = first + rec[slot + 3 * stride + slots + leaf_sub]
        used = lax.cond(
            touches(moved - 1, moved + leaf_sub, base, length + 1),
            lambda used, slot=slot: lax.fori_loop(
                0, slots, collect_lower, (used, slot), unroll=8
            )[0],
            lambda used: used,
            used,
        )
    from_own = used
    for group in range(sub_count):
        first = jnp.bitwise_xor(me, group) * leaf_sub
        slot = (3 * group + 1) * block
        used, kept = lax.cond(
            touches(first - 1, first + leaf_sub, base - 1, length + 2),
            lambda used, kept, slot=slot: lax.fori_loop(
                0, slots, collect_own, (used, kept, slot), unroll=8
            )[0:2],
            lambda used, kept: (used, kept),
            used,
            kept,
        )
    from_upper = used
    for group in range(sub_count):
        first = jnp.bitwise_xor(me, group) * leaf_sub
        slot = (3 * group + 2) * block
        used = lax.cond(
            touches(first, first + leaf_sub, upper_base, length + 2),
            lambda used, slot=slot: lax.fori_loop(
                0, slots, collect_upper, (used, slot), unroll=8
            )[0],
            lambda used: used,
            used,
        )
    for extra in range(2 * UNROLL):
        order[used + extra] = -1

    def load_leaf(column, carry):
        lanes = pl.ds(pl.multiple_of(column * LEAF, LEAF), LEAF)
        local[column] = lower_ref[:, lanes]
        local[width + column] = own_ref[:, lanes]
        local[2 * width + column] = upper_ref[:, lanes]
        local[3 * width + column] = beyond_ref[:, lanes]
        for k in range(5):
            own_out[pl.ds(k * width + column, 1), :] = jnp.zeros((1, LEAF), F32)
            next_out[pl.ds(k * width + column, 1), :] = jnp.zeros((1, LEAF), F32)
        for slab in range(4):
            raw[slab * width + column] = jnp.zeros((32, LEAF), F32)
        return carry

    lax.fori_loop(0, width, load_leaf, 0)
    local[whole] = jnp.zeros((8, LEAF), F32)
    raw[whole] = jnp.zeros((32, LEAF), F32)


    def slab_base(position):
        return jnp.where(position < from_own, 0, jnp.where(position < from_upper, width, 2 * width))

    def clear_rows(seat, carry):
        for part in range(LEAF // ROWS):
            for k in range(5):
                row_sum[seat * (LEAF // ROWS) + part, k] = jnp.zeros((ROWS, LEAF), F32)
        return carry

    lax.fori_loop(0, length, clear_rows, 0)

    def clear_cols(seat, carry):
        col_sum[seat] = jnp.zeros((40, LEAF), F32)
        return carry

    lax.fori_loop(0, length + 1, clear_cols, 0)
    lax.fori_loop(cap + 1, cap + length + 3, clear_cols, 0)

    def slot_tiles(position):
        named = order[position]
        slot = jnp.maximum(named, 0)
        start = slab_base(position)
        other = slot_other(slot)
        shift = displacement(
            jnp.where(other >= width, 1.0, 0.0).astype(F32), slot_step_y(slot), slot_wrap(slot)
        )
        home = jnp.where(named < 0, whole, start + slot_home(slot))
        other = jnp.where(named < 0, whole, start + other)
        return home, other, local[home], local[other] + shift, shift

    def distances(group):
        row = lax.broadcasted_iota(jnp.int32, (8, LEAF), 0)
        for k in range(UNROLL):
            _, _, near, far, _ = slot_tiles(group * UNROLL + k)
            near_pos = [near[j : j + 1] for j in range(3)]
            far_pos = [far[j : j + 1] for j in range(3)]
            near_k = jnp.where(
                row < 3,
                near,
                jnp.where(row == 3, dot3(near_pos, near_pos), jnp.where(row == 4, 1.0, 0.0)),
            )
            far_k = jnp.where(
                row < 3,
                (-2.0 / SUPPORT**2) * far,
                jnp.where(
                    row == 4,
                    dot3(far_pos, far_pos) * (1.0 / SUPPORT**2),
                    jnp.where(row == 3, 1.0 / SUPPORT**2, 0.0),
                ),
            )
            dist[k] = bilinear(near_k, far_k)

    def moment_group(group, carry):
        parts = []
        for k in range(UNROLL):
            home, other, near, far, shift = slot_tiles(group * UNROLL + k)
            weight = jnp.where(home == other, 0.5, 1.0).astype(F32)
            smooth = smoothing_of(dist[k], KERNEL_NORM * weight)
            high = smooth.astype(BF16)
            low = (smooth - high.astype(F32)).astype(BF16)
            row_part = lax.dot_general(
                moment_features(far),
                jnp.concatenate([high, low], axis=1),
                (((1,), (1,)), ((), ())),
                preferred_element_type=F32,
            )
            col_part = lax.dot_general(
                moment_features(near - shift),
                jnp.concatenate([high, low], axis=0),
                (((1,), (0,)), ((), ())),
                preferred_element_type=F32,
            )
            parts.append((home, other, row_part, col_part))
        distances(group + 1)
        for home, other, row_part, col_part in parts:
            raw[home] += row_part[:32] + row_part[32:]
            raw[other] += col_part[:32] + col_part[32:]
        return carry

    distances(0)
    lax.fori_loop(0, (used + UNROLL - 1) // UNROLL, moment_group, 0)

    def window_leaf(seat):
        return jnp.where(seat <= cap, own_leaf(seat), upper_leaf(seat - cap - 1))

    def finish(seat, carry):
        leaf = window_leaf(seat)
        payload = finish_leaf(raw[leaf], local[leaf])
        pay[seat] = payload
        for k, entry in enumerate(far_coefficients(local[leaf], payload)):
            far_coef[seat, 8 * k : 8 * k + 8] = entry
        return carry

    lax.fori_loop(0, length + 1, finish, 0)
    lax.fori_loop(cap + 1, cap + length + 3, finish, 0)

    splits = LEAF // ROWS

    picked = lax.broadcasted_iota(jnp.int32, (48, LEAF), 0)
    for k in range(5):
        chosen = (picked == 3 + k) | (picked == 27 + k) | (picked == 43 + k)
        spread[:, k * LEAF : (k + 1) * LEAF] = jnp.where(chosen, 0.5 if k < 3 else 1.0, 0.0).astype(
            BF16
        )

    def turn_home(seat):
        tile = local[own_leaf(seat)]
        generic = {0: 1.0}
        generic.update({1 + k: tile[k : k + 1] for k in range(6)})
        generic = stack_near(stack_rows(generic))
        coefficients = [stack_near(entry) for entry in near_coefficients(tile, pay[seat])]
        planes = jnp.dot(stack_near(tile).T, spread[...], preferred_element_type=F32)
        turned_far = generic.T
        turned_near = [coefficients[k].T for k in (0, 4, 5, 6, 7, 8)]
        turned_toward = [
            jnp.concatenate([coefficients[1 + k], generic], axis=0).T for k in range(3)
        ]
        for part in range(splits):
            rows = slice(part * ROWS, (part + 1) * ROWS)
            place = seat * splits + part
            for k in range(6):
                near_left[place, k * ROWS : (k + 1) * ROWS, 0:48] = turned_near[k][rows]
            for k in range(3):
                toward_left[place, k * ROWS : (k + 1) * ROWS, 0:96] = turned_toward[k][rows]
            far_left[place, :, 0:48] = turned_far[rows]
            for k in range(5):
                near_plane[place, k] = planes[rows, k * LEAF : (k + 1) * LEAF]

    def turn_two(pair, carry):
        turn_home(2 * pair)
        turn_home(2 * pair + 1)
        return carry

    lax.fori_loop(0, (length + 1) // 2, turn_two, 0)

    def prepare_slot(index, count):
        slot = mine[index]
        valid = (index < kept).astype(jnp.int32)
        column = slot_home(slot)
        away = slot_other(slot)
        is_upper = away >= width
        other = width + away
        step_x = jnp.where(is_upper, 1.0, 0.0).astype(F32)
        step_y = slot_step_y(slot)
        wrap = slot_wrap(slot)
        other_seat = jnp.where(
            is_upper,
            cap + 1 + lax.rem(away - upper_base, width),
            lax.rem(away + width - base, width),
        )
        for part in range(splits):
            item_left[count] = (column - base) * splits + part
            item_index[count] = index
            item_seat[count] = jnp.where(column == away, -1 - other_seat, other_seat)
            count = count + valid * (count_of(column) > part * ROWS).astype(jnp.int32)

        far = local[other] + displacement(step_x, step_y, wrap)
        row = lax.broadcasted_iota(jnp.int32, (8, LEAF), 0)
        pos = [far[k : k + 1] for k in range(3)]
        generic = {0: 1.0, 7: dot3(pos, pos)}
        generic.update({1 + k: far[k : k + 1] for k in range(6)})
        generic = stack_far(stack_rows(generic))
        near_right[index] = generic
        for k in range(8):
            entry = far_coef[other_seat, 8 * k : 8 * k + 8]
            change = entry[1:2] * step_x + entry[2:3] * step_y
            if k == 4:
                change = change + 0.5 * wrap
            entry = stack_far(jnp.where(row == 0, entry - change, entry))
            if k < 3:
                toward_right[index, 0:48, k * LEAF : (k + 1) * LEAF] = generic
                toward_right[index, 48:96, k * LEAF : (k + 1) * LEAF] = entry
            else:
                far_right[index, :, (k - 3) * LEAF : (k - 2) * LEAF] = entry
        far_half[index, 0:5] = jnp.concatenate([0.5 * far[3:6], far[6:8]], axis=0)
        return count

    def prepare_two(pair, count):
        return prepare_slot(2 * pair + 1, prepare_slot(2 * pair, count))

    mine[kept] = mine[0]
    item_count = lax.fori_loop(0, (kept + 1) // 2, prepare_two, 0)
    for extra in range(2):
        item_left[item_count + extra] = 0
        item_index[item_count + extra] = 0

    def state_forms(position):
        index = item_index[position]
        left = item_left[position]
        near_form[...] = jnp.dot(
            near_left[left, ROWS : 6 * ROWS, 0:48], near_right[index], preferred_element_type=F32
        )
        far_form[...] = jnp.dot(
            far_left[left, :, 0:48], far_right[index], preferred_element_type=F32
        )

    def space_forms(position):
        index = item_index[position]
        left = item_left[position]
        dist_form[...] = jnp.dot(
            near_left[left, 0:ROWS, 0:48], near_right[index], preferred_element_type=F32
        )
        for k in range(3):
            toward_form[k * ROWS : (k + 1) * ROWS, :] = jnp.dot(
                toward_left[left, k * ROWS : (k + 1) * ROWS, 0:96],
                toward_right[index, :, k * LEAF : (k + 1) * LEAF],
                preferred_element_type=F32,
            )

    def geometry():
        return face_geometry(
            dist_form[...], [toward_form[k * ROWS : (k + 1) * ROWS, :] for k in range(3)]
        )

    def keep_geometry(values):
        for k in range(4):
            geo_form[k * ROWS : (k + 1) * ROWS, :] = values[k]

    def flux_item(position, carry):
        left = item_left[position]
        index = item_index[position]
        coded = item_seat[position]
        other_seat = jnp.where(coded < 0, -1 - coded, coded)
        weight = jnp.where(coded < 0, 0.0, 1.0).astype(F32)
        fluxes = face_fluxes(
            [near_form[k * ROWS : (k + 1) * ROWS, :] for k in range(5)],
            [far_form[:, k * LEAF : (k + 1) * LEAF] for k in range(5)],
            [geo_form[k * ROWS : (k + 1) * ROWS, :] for k in range(3)],
            geo_form[3 * ROWS : 4 * ROWS, :],
            [near_plane[left, k] for k in range(5)],
            [far_half[index, k : k + 1, :] for k in range(5)],
        )
        following = geometry()
        keep_geometry(following)
        state_forms(position + 1)
        space_forms(position + 2)
        for k in range(5):
            row_sum[left, k] += fluxes[k]
            col_sum[other_seat, 8 * k : 8 * k + 8] += weight * sum(
                fluxes[k][8 * j : 8 * j + 8] for j in range(ROWS // 8)
            )
        return carry

    space_forms(0)
    keep_geometry(geometry())
    state_forms(0)
    space_forms(1)
    lax.fori_loop(0, item_count, flux_item, 0)

    lane = lax.broadcasted_iota(jnp.int32, (ROWS, LEAF), 1)

    def row_total(seat, carry):
        pieces = []
        for part in range(splits):
            total = jnp.zeros((ROWS, LEAF), F32)
            for c in range(5):
                reduced = jnp.sum(row_sum[seat * splits + part, c], axis=1, keepdims=True)
                total = jnp.where(lane == c, reduced, total)
            pieces.append(total)
        row_rate[seat] = jnp.concatenate(pieces, axis=0).T[0:8]
        return carry

    lax.fori_loop(0, length, row_total, 0)
    row_rate[length] = jnp.zeros((8, LEAF), F32)

    def rates(seat, less):
        leaf = window_leaf(seat)
        total = stack_rows(
            {
                k: jnp.sum(col_sum[seat, 8 * k : 8 * k + 8], axis=0, keepdims=True)
                for k in range(5)
            }
        )
        if less is not None:
            total = total - less
        live = local[leaf][0:1] < 0.5 * AWAY
        scale = AREA_FLOOR * pay[seat][0:1]
        return lax.rem(leaf, width), jnp.where(live, total * scale, 0.0)

    def write_own(k, carry):
        column, value = rates(k, row_rate[k])
        for c in range(5):
            own_out[pl.ds(c * width + column, 1), :] = value[c : c + 1]
        return carry

    def write_upper(k, carry):
        column, value = rates(k, None)
        for c in range(5):
            next_out[pl.ds(c * width + column, 1), :] = value[c : c + 1]
        return carry

    lax.fori_loop(0, length + 1, write_own, 0)
    lax.fori_loop(cap + 1, cap + length + 3, write_upper, 0)


def shards(positions, velocity, density, pressure, counts, pair_list):
    width = counts.shape[0]
    slots = pair_list.shape[1]
    particles = width * LEAF
    sub_count = lax.axis_size("sub")
    leaf_sub = width // sub_count

    smem = pl.BlockSpec(memory_space=pltpu.SMEM)
    vmem = pl.BlockSpec(memory_space=pltpu.VMEM)
    lanes = -(-(slots + max(leaf_sub + 1, width)) // LEAF) * LEAF
    state, listed = pl.pallas_call(
        functools.partial(pack_kernel, width, leaf_sub),
        out_shape=[
            jax.ShapeDtypeStruct((8, particles), F32),
            jax.ShapeDtypeStruct((4, lanes), F32),
        ],
        in_specs=[smem, vmem, vmem, vmem, vmem, vmem, vmem],
        out_specs=[vmem, vmem],
        name="pack",
    )(
        counts,
        counts[None],
        positions,
        velocity,
        density[None],
        pressure[None],
        pair_list,
    )
    kept_state, kept_listed = lax.optimization_barrier(
        (jnp.where(state == state, state, 0.0), jnp.where(listed == listed, listed, 0.0))
    )
    lists = jnp.stack([shifted(listed, "slab", 1), kept_listed, shifted(listed, "slab", -1)])[None]
    lower = shifted(state, "slab", 1)
    upper = shifted(state, "slab", -1)
    beyond = shifted(state, "slab", -2)
    mask = 1
    while mask < sub_count:
        lists = jnp.concatenate([lists, swapped(lists, "sub", mask)], axis=0)
        mask *= 2
    rec = lists.astype(jnp.int32).reshape(-1)
    cap = 2 * leaf_sub
    most = cap * CAND
    splits = LEAF // ROWS

    own_part, next_part = pl.pallas_call(
        functools.partial(step_kernel, width, sub_count, slots),
        out_shape=[jax.ShapeDtypeStruct((5 * width, LEAF), F32)] * 2,
        in_specs=[smem, vmem, vmem, vmem, vmem],
        out_specs=[vmem, vmem],
        scratch_shapes=[
            pltpu.SMEM((3 * sub_count * slots + 2 * UNROLL,), jnp.int32),
            pltpu.SMEM((most + 1,), jnp.int32),
            pltpu.SMEM((7 * width + 1,), jnp.int32),
            pltpu.SMEM((width,), jnp.int32),
        ]
        + [pltpu.SMEM((most * splits + 2,), jnp.int32)] * 3
        + [
            pltpu.VMEM((4 * width + 1, 8, LEAF), F32),
            pltpu.VMEM((4 * width + 1, 32, LEAF), F32),
            pltpu.VMEM((2 * cap + 3, 24, LEAF), F32),
            pltpu.VMEM((2 * cap + 3, 64, LEAF), F32),
            pltpu.VMEM((cap * splits, 6 * ROWS, LEAF), BF16),
            pltpu.VMEM((cap * splits, ROWS, LEAF), BF16),
            pltpu.VMEM((cap * splits, 3 * ROWS, LEAF), BF16),
            pltpu.VMEM((cap * splits, 5, ROWS, LEAF), F32),
            pltpu.VMEM((most, 48, LEAF), BF16),
            pltpu.VMEM((most, 48, 5 * LEAF), BF16),
            pltpu.VMEM((most, 96, 3 * LEAF), BF16),
            pltpu.VMEM((most, 8, LEAF), F32),
            pltpu.VMEM((48, 5 * LEAF), BF16),
            pltpu.VMEM((UNROLL, LEAF, LEAF), F32),
            pltpu.VMEM((5 * ROWS, LEAF), F32),
            pltpu.VMEM((ROWS, 5 * LEAF), F32),
            pltpu.VMEM((3 * ROWS, LEAF), F32),
            pltpu.VMEM((ROWS, LEAF), F32),
            pltpu.VMEM((4 * ROWS, LEAF), F32),
            pltpu.VMEM((2 * cap + 3, 40, LEAF), F32),
            pltpu.VMEM((cap * splits, 5, ROWS, LEAF), F32),
            pltpu.VMEM((cap + 1, 8, LEAF), F32),
        ],
        compiler_params=pltpu.CompilerParams(vmem_limit_bytes=48 * 1024 * 1024),
        name="hydro_step",
    )(rec, lower, kept_state, upper, beyond)

    merged = own_part + shifted(next_part, "slab", 1)
    mask = 1
    while mask < sub_count:
        merged = merged + swapped(merged, "sub", mask)
        mask *= 2
    return merged.reshape(5, particles)


def solution(mesh):
    placed = (
        P(None, "slab"),
        P(None, "slab"),
        P("slab"),
        P("slab"),
        P("slab"),
        P(None, ("slab", "sub")),
    )
    return jax.shard_map(
        shards, mesh=mesh, in_specs=placed, out_specs=P(None, "slab"), check_vma=False
    )
```

```python
import functools
import math

import jax
import jax.numpy as jnp
from jax import lax
from jax.experimental import pallas as pl
from jax.experimental.pallas import tpu as pltpu
from jax.sharding import PartitionSpec as P

LEAF = 128
CAND = 5

GAMMA = 5.0 / 3.0
SUPPORT = 1.5
KERNEL_NORM = 21.0 / (2.0 * math.pi * SUPPORT**3)
MOMENT_REG = 0.05
AREA_FLOOR = 0.0001
AWAY = 64.0
UNROLL = 8
ROWS = 64
ROWS_LOG = 6
COST_LEAF, COST_SLOT, COST_PART = 17, 3, 5
F32 = jnp.float32
BF16 = jnp.bfloat16


def shifted(shard, axis, by):
    peers = lax.axis_size(axis)
    return lax.ppermute(shard, axis, [(i, (i + by) % peers) for i in range(peers)])


def swapped(shard, axis, mask):
    peers = lax.axis_size(axis)
    return lax.ppermute(shard, axis, [(i, i ^ mask) for i in range(peers)])


def reciprocal(value):
    return pl.reciprocal(value, approx=True)


def smoothing_of(dist_sq, scale):
    safe = jnp.maximum(dist_sq, 1e-12)
    radius = safe * lax.rsqrt(safe)
    inside = jnp.maximum(1.0 - radius, 0.0)
    square = inside * inside
    return (square * square) * (scale + (scale * 4.0) * radius)


def split_three(value):
    high = value.astype(BF16).astype(F32)
    rest = value - high
    middle = rest.astype(BF16).astype(F32)
    return high, middle, rest - middle


def stack_near(rows):
    high, middle, low = split_three(rows)
    return jnp.concatenate([high, high, high, middle, middle, low], axis=0).astype(BF16)


def stack_far(rows):
    high, middle, low = split_three(rows)
    return jnp.concatenate([high, middle, low, high, middle, high], axis=0).astype(BF16)


def bilinear(near_rows, far_rows):
    return lax.dot_general(
        stack_near(near_rows),
        stack_far(far_rows),
        (((0,), (0,)), ((), ())),
        preferred_element_type=F32,
    )


def moment_features(tile):
    row = lax.broadcasted_iota(jnp.int32, tile.shape, 0)
    by_x = tile * tile[0:1]
    by_y = jnp.where(row == 0, 1.0, tile * tile[1:2])
    by_z = tile * tile[2:3]
    whole = jnp.concatenate([tile, by_x, by_y, by_z], axis=0)
    high = whole.astype(BF16)
    low = (whole - high.astype(F32)).astype(BF16)
    both = jnp.concatenate([high, low], axis=0)
    return jnp.concatenate([both, both], axis=1)


def displacement(step_x, step_y, wrap):
    row = lax.broadcasted_iota(jnp.int32, (8, LEAF), 0)
    zero = jnp.zeros((8, LEAF), F32)
    out = jnp.where(row == 0, step_x, zero)
    out = jnp.where(row == 1, step_y, out)
    return jnp.where(row == 4, -wrap, out)


def finish_leaves(raw, tile):
    pos = [tile(k) for k in range(3)]
    live = pos[0] < 0.5 * AWAY
    total = raw(16)
    first = [raw(k) - pos[k] * total for k in range(3)]

    def second(left, right):
        lead = raw(8 + 8 * left + right)
        return lead - pos[left] * raw(right) - pos[right] * first[left]

    density = jnp.where(live, total, 1.0)
    inverse_density = 1.0 / density

    def scaled(value):
        return jnp.where(live, value * inverse_density, 0.0)

    exx = scaled(second(0, 0)) + MOMENT_REG
    exy = scaled(second(0, 1))
    exz = scaled(second(0, 2))
    eyy = scaled(second(1, 1)) + MOMENT_REG
    eyz = scaled(second(1, 2))
    ezz = scaled(second(2, 2)) + MOMENT_REG
    mxx = eyy * ezz - eyz * eyz
    mxy = exz * eyz - exy * ezz
    mxz = exy * eyz - exz * eyy
    myy = exx * ezz - exz * exz
    myz = exy * exz - exx * eyz
    mzz = exx * eyy - exy * exy
    scale = 1.0 / (exx * mxx + exy * mxy + exz * mxz)
    inverse = [entry * scale for entry in (mxx, mxy, mxz, myy, myz, mzz)]
    square = inverse_density * inverse_density
    rows = [density] + [entry * square for entry in inverse]
    for quantity in range(3, 8):
        value = tile(quantity)
        along = [
            scaled(
                raw(8 + 8 * k + quantity)
                - pos[k] * raw(quantity)
                - value * first[k]
            )
            for k in range(3)
        ]
        half = [0.5 * term for term in along]
        rows.append(inverse[0] * half[0] + inverse[1] * half[1] + inverse[2] * half[2])
        rows.append(inverse[1] * half[0] + inverse[3] * half[1] + inverse[4] * half[2])
        rows.append(inverse[2] * half[0] + inverse[4] * half[1] + inverse[5] * half[2])
    return rows


def dot3(left, right):
    return left[0] * right[0] + left[1] * right[1] + left[2] * right[2]


def apply_sym(matrix, vector):
    return [
        dot3((matrix[0], matrix[1], matrix[2]), vector),
        dot3((matrix[1], matrix[3], matrix[4]), vector),
        dot3((matrix[2], matrix[4], matrix[5]), vector),
    ]


def stack_rows(rows):
    row = lax.broadcasted_iota(jnp.int32, (8, LEAF), 0)
    out = jnp.zeros((8, LEAF), F32)
    for k, entry in rows.items():
        out = jnp.where(row == k, entry, out)
    return out


def near_coefficients(tile, pay):
    pos = [tile[k : k + 1] for k in range(3)]
    twice = [(-2.0 / SUPPORT**2) * entry for entry in pos]
    out = [
        {
            0: dot3(pos, pos) * (1.0 / SUPPORT**2),
            1: twice[0],
            2: twice[1],
            3: twice[2],
            7: 1.0 / SUPPORT**2,
        }
    ]
    matrix = [pay[1 + k : 2 + k] for k in range(6)]
    for line in ((0, 1, 2), (1, 3, 4), (2, 4, 5)):
        entries = [matrix[k] for k in line]
        out.append({0: -dot3(entries, pos), 1: entries[0], 2: entries[1], 3: entries[2]})
    for quantity in range(5):
        slope = [pay[7 + 3 * quantity + k : 8 + 3 * quantity + k] for k in range(3)]
        value = tile[3 + quantity : 4 + quantity]
        if quantity < 3:
            entry = {0: 0.5 * value - dot3(slope, pos), 4 + quantity: -0.5}
        else:
            entry = {0: value - dot3(slope, pos)}
        entry.update({1: slope[0], 2: slope[1], 3: slope[2]})
        out.append(entry)
    return [stack_rows(entry) for entry in out]


def far_coefficients(tile, pay):
    pos = [tile(k) for k in range(3)]
    out = []
    matrix = [pay[1 + k] for k in range(6)]
    for line in ((0, 1, 2), (1, 3, 4), (2, 4, 5)):
        entries = [matrix[k] for k in line]
        out.append({0: dot3(entries, pos), 1: -entries[0], 2: -entries[1], 3: -entries[2]})
    for quantity in range(5):
        slope = [pay[7 + 3 * quantity + k] for k in range(3)]
        value = tile(3 + quantity)
        if quantity < 3:
            entry = {0: 0.5 * value - dot3(slope, pos), 4 + quantity: -0.5}
        else:
            entry = {0: value - dot3(slope, pos)}
        entry.update({1: slope[0], 2: slope[1], 3: slope[2]})
        out.append(entry)
    return out


def limited(value, low, high):
    return jnp.minimum(jnp.maximum(value, low), high)


def face_geometry(dist_sq, toward):
    smooth = smoothing_of(dist_sq, KERNEL_NORM / AREA_FLOOR)
    length_sq = jnp.maximum(dot3(toward, toward), 1e-30)
    inverse_length = lax.rsqrt(length_sq)
    area = smooth * (length_sq * inverse_length)
    scale = jnp.minimum(inverse_length, smooth)
    return [entry * scale for entry in toward] + [area]


def face_fluxes(near_out, far_out, normal, area, near_plain, far_plain):
    left_vel, right_vel = [], []
    for k in range(3):
        high = jnp.abs(far_plain[k] - near_plain[k])
        low = -high
        left_vel.append(limited(near_out[k], low, high))
        right_vel.append(limited(far_out[k], low, high))
    face_vel = [near_plain[k] + far_plain[k] for k in range(3)]
    thermo = []
    for k in range(2):
        low = jnp.minimum(near_plain[3 + k], far_plain[3 + k])
        high = jnp.maximum(near_plain[3 + k], far_plain[3 + k])
        thermo.append(limited(near_out[3 + k], low, high))
        thermo.append(limited(far_out[3 + k], low, high))
    left_rho, right_rho, left_p, right_p = thermo
    left_u = dot3(left_vel, normal)
    right_u = dot3(right_vel, normal)
    left_gp = GAMMA * left_p
    right_gp = GAMMA * right_p
    left_c = left_gp * lax.rsqrt(left_gp * left_rho)
    right_c = right_gp * lax.rsqrt(right_gp * right_rho)
    slow = jnp.minimum(left_u - left_c, right_u - right_c)
    fast = jnp.maximum(left_u + left_c, right_u + right_c)
    left_m = left_rho * (slow - left_u)
    right_m = right_rho * (fast - right_u)
    contact = (right_p - left_p + left_m * left_u - right_m * right_u) * reciprocal(
        left_m - right_m
    )
    is_left = contact >= 0.0
    speed = jnp.where(is_left, jnp.minimum(slow, 0.0), jnp.maximum(fast, 0.0))
    rho = jnp.where(is_left, left_rho, right_rho) * area
    press = jnp.where(is_left, left_p, right_p) * area
    normal_speed = jnp.where(is_left, left_u, right_u)
    vel = [jnp.where(is_left, left_vel[k], right_vel[k]) + face_vel[k] for k in range(3)]
    lag = speed - normal_speed
    ratio = lag * reciprocal(speed - contact)
    through = ratio * contact
    gain = speed * ratio - speed
    push = (rho * lag) * gain
    mass = rho * through
    total_p = press + push
    mom = [mass * vel[k] + total_p * normal[k] for k in range(3)]
    energy = press * (through * (1.0 / (GAMMA - 1.0)) + normal_speed + gain) + push * contact
    energy = energy + (0.5 * mass) * dot3(vel, vel) + total_p * dot3(face_vel, normal)
    return [mass] + mom + [energy]


def pack_kernel(
    width,
    leaf_sub,
    counts,
    counts_row,
    positions,
    velocity,
    density,
    pressure,
    pair_list,
    state,
    listed,
):
    slab = lax.axis_index("slab")
    centre_x = slab.astype(F32) + 0.5
    row = lax.broadcasted_iota(jnp.int32, (3, LEAF), 0)
    lane = lax.broadcasted_iota(jnp.int32, (3, LEAF), 1)

    def one_leaf(column, carry):
        lanes = pl.ds(pl.multiple_of(column * LEAF, LEAF), LEAF)
        centre_y = column.astype(F32) + 0.5
        centre = jnp.where(row == 0, centre_x, jnp.where(row == 1, centre_y, 0.5))
        dead = (row == 0) & (lane >= counts[column])
        state[0:3, lanes] = jnp.where(dead, AWAY, positions[:, lanes] - centre)
        state[3:6, lanes] = velocity[:, lanes]
        state[6:7, lanes] = density[:, lanes]
        state[7:8, lanes] = pressure[:, lanes]
        return carry

    lax.fori_loop(0, width, one_leaf, 0, unroll=4)
    listed[...] = jnp.zeros(listed.shape, F32)
    slots = pair_list.shape[1]
    heads = pair_list[0:1, :]
    tails = pair_list[1:2, :]
    offsets = pair_list[2:3, :]
    occupied = heads >= 0
    head_col = heads - slab * width
    inside = (tails >= slab * width) & (tails < (slab + 1) * width)
    next_slab = lax.rem(slab + 1, lax.axis_size("slab"))
    tail_col = jnp.where(inside, tails - slab * width, tails - next_slab * width)
    outside = occupied & jnp.logical_not(inside)
    wraps = outside & (tails < heads)
    step_y = tail_col + offsets - head_col
    empty = 4 * width
    here = slice(0, slots)
    listed[0:1, here] = jnp.where(occupied, head_col, empty).astype(F32)
    listed[0:1, slots : slots + width] = counts_row[...].astype(F32)
    listed[1:2, here] = jnp.where(
        occupied, jnp.where(inside, tail_col, tail_col + width), empty
    ).astype(F32)
    listed[2:3, here] = jnp.where(occupied, step_y, 0).astype(F32)
    listed[3:4, here] = jnp.where(wraps, 1.0, 0.0)
    seats = head_col - lax.axis_index("sub") * leaf_sub
    behind = lax.broadcasted_iota(jnp.int32, (1, leaf_sub + 1), 1)
    shifts = lax.rem(5 * width * LEAF - offsets, width)
    shift = jnp.max(jnp.where(outside, shifts, 0), axis=1, keepdims=True).astype(F32)
    facts = jnp.where(behind == leaf_sub, shift, 0.0)
    for k in range(leaf_sub):
        found = jnp.where(occupied & (seats == k), 1.0, 0.0)
        facts = jnp.where(behind == k, jnp.sum(found, axis=1, keepdims=True), facts)
    listed[3:4, slots : slots + leaf_sub + 1] = facts


def upper_seat_of(cap):
    return -(-(cap + 2) // 8) * 8


def step_kernel(
    width,
    sub_count,
    slots,
    rec,
    lower_ref,
    own_ref,
    upper_ref,
    beyond_ref,
    own_out,
    next_out,
    order,
    mine,
    need,
    costs,
    item_left,
    item_index,
    item_seat,
    turned_leaf,
    local,
    raw,
    pay,
    far_coef,
    near_left,
    far_left,
    toward_left,
    near_plane,
    near_right,
    far_right,
    toward_right,
    far_half,
    spread,
    dist,
    near_form,
    far_form,
    toward_form,
    dist_form,
    geo_form,
    col_sum,
    row_sum,
    row_rate,
):
    whole = 4 * width
    leaf_sub = width // sub_count
    cap = 2 * leaf_sub
    up = upper_seat_of(cap)
    stride = rec.shape[0] // (12 * sub_count)
    block = 4 * stride

    def count_of(column):
        return rec[block + slots + column]

    def slot_home(slot):
        return rec[slot]

    def slot_other(slot):
        return rec[slot + stride]

    def slot_step_y(slot):
        return rec[slot + 2 * stride].astype(F32)

    def slot_wrap(slot):
        return rec[slot + 3 * stride].astype(F32)

    def clear_need(entry, carry):
        need[entry] = 0
        return carry

    lax.fori_loop(0, 7 * width, clear_need, 0, unroll=16)
    need[7 * width] = 0

    me = lax.axis_index("sub")
    total_cost = jnp.int32(0)
    shift_w = jnp.int32(0)
    for group in range(sub_count):
        seats = jnp.bitwise_xor(me, group) * leaf_sub
        facts = (3 * group + 1) * block + 3 * stride + slots
        shift_w = jnp.maximum(shift_w, rec[facts + leaf_sub])
        for k in range(leaf_sub):
            parts = lax.shift_right_logical(count_of(seats + k) + (ROWS - 1), ROWS_LOG)
            cost = COST_LEAF + rec[facts + k] * (COST_SLOT + COST_PART * parts)
            costs[seats + k] = cost
            total_cost = total_cost + cost

    def deal(column, state):
        owner, length, before, first, mine_length = state
        cost = costs[column]
        middle = sub_count * (2 * before + cost)
        wish = (middle >= 2 * total_cost * (owner + 1)) | (length == cap)
        allowed = (owner < sub_count - 1) & (width - column <= (sub_count - 1 - owner) * cap)
        step = (wish & allowed).astype(jnp.int32)
        owner = owner + step
        length = (1 - step) * length + 1
        is_mine = (owner == me).astype(jnp.int32)
        first = jnp.where((is_mine > 0) & (mine_length == 0), column, first)
        return owner, length, before + cost, first, mine_length + is_mine

    zero = jnp.int32(0)
    _, _, _, base, length = lax.fori_loop(
        0, width, deal, (zero, zero, zero, zero, zero), unroll=4
    )
    upper_base = lax.rem(base + width - 1 + shift_w, width)

    def own_leaf(k):
        return width + lax.rem(base + k, width)

    def upper_leaf(k):
        return 2 * width + lax.rem(upper_base + k, width)

    def mark_own(k, carry):
        need[own_leaf(k)] = jnp.where(k < length, 3, 1)
        return carry

    def mark_upper(k, carry):
        need[upper_leaf(k)] = 1
        return carry

    lax.fori_loop(0, length + 1, mark_own, 0)
    lax.fori_loop(0, length + 2, mark_upper, 0)

    def collect_lower(k, carry):
        used, first = carry
        order[used] = first + k
        return used + (need[slot_other(first + k)] & 1), first

    def collect_own(k, carry):
        used, kept, first = carry
        slot = first + k
        flags = need[width + slot_home(slot)]
        order[used] = slot
        mine[kept] = slot
        used = used + ((flags | need[width + slot_other(slot)]) & 1)
        return used, kept + lax.shift_right_logical(flags, 1), first

    def collect_upper(k, carry):
        used, first = carry
        slot = first + k
        order[used] = slot
        flags = need[2 * width + slot_home(slot)] | need[2 * width + slot_other(slot)]
        return used + (flags & 1), first

    def touches(first, last, start, count):
        ahead = lax.rem(first - start + 4 * width, width) < count
        return ahead | (lax.rem(start - first + 4 * width, width) <= last - first)

    used, kept = zero, zero
    for group in range(sub_count):
        first = jnp.bitwise_xor(me, group) * leaf_sub
        slot = 3 * group * block
        moved = first + rec[slot + 3 * stride + slots + leaf_sub]
        used = lax.cond(
            touches(moved - 1, moved + leaf_sub, base, length + 1),
            lambda used, slot=slot: lax.fori_loop(
                0, slots, collect_lower, (used, slot), unroll=8
            )[0],
            lambda used: used,
            used,
        )
    from_own = used
    for group in range(sub_count):
        first = jnp.bitwise_xor(me, group) * leaf_sub
        slot = (3 * group + 1) * block
        used, kept = lax.cond(
            touches(first - 1, first + leaf_sub, base - 1, length + 2),
            lambda used, kept, slot=slot: lax.fori_loop(
                0, slots, collect_own, (used, kept, slot), unroll=8
            )[0:2],
            lambda used, kept: (used, kept),
            used,
            kept,
        )
    from_upper = used
    for group in range(sub_count):
        first = jnp.bitwise_xor(me, group) * leaf_sub
        slot = (3 * group + 2) * block
        used = lax.cond(
            touches(first, first + leaf_sub, upper_base, length + 2),
            lambda used, slot=slot: lax.fori_loop(
                0, slots, collect_upper, (used, slot), unroll=8
            )[0],
            lambda used: used,
            used,
        )
    for extra in range(2 * UNROLL):
        order[used + extra] = -1

    def rows_of(leaf, count):
        return pl.ds(pl.multiple_of(leaf * count, count), count)

    def load_leaf(column, carry):
        lanes = pl.ds(pl.multiple_of(column * LEAF, LEAF), LEAF)
        places = (
            column,
            width + lax.rem(column - base + width, width),
            2 * width + lax.rem(column - upper_base + width, width),
            3 * width + column,
        )
        for slab, ref in enumerate((lower_ref, own_ref, upper_ref, beyond_ref)):
            local[rows_of(places[slab], 8), :] = ref[:, lanes]
            turned_leaf[slab * width + column] = places[slab]
            raw[rows_of(slab * width + column, 32), :] = jnp.zeros((32, LEAF), F32)
        for k in range(5):
            own_out[pl.ds(k * width + column, 1), :] = jnp.zeros((1, LEAF), F32)
            next_out[pl.ds(k * width + column, 1), :] = jnp.zeros((1, LEAF), F32)
        return carry

    lax.fori_loop(0, width, load_leaf, 0)
    local[rows_of(whole, 8), :] = jnp.zeros((8, LEAF), F32)
    raw[rows_of(whole, 32), :] = jnp.zeros((32, LEAF), F32)

    def tile_of(leaf):
        return local[rows_of(leaf, 8), :]

    def slab_base(position):
        return jnp.where(position < from_own, 0, jnp.where(position < from_upper, width, 2 * width))

    def clear_rows(seat, carry):
        for part in range(LEAF // ROWS):
            for k in range(5):
                row_sum[seat * (LEAF // ROWS) + part, k] = jnp.zeros((ROWS, LEAF), F32)
        return carry

    lax.fori_loop(0, length, clear_rows, 0)

    def clear_cols(seat, carry):
        col_sum[seat] = jnp.zeros((40, LEAF), F32)
        return carry

    lax.fori_loop(0, length + 1, clear_cols, 0)
    lax.fori_loop(up, up + length + 2, clear_cols, 0)

    def slot_tiles(position):
        named = order[position]
        slot = jnp.maximum(named, 0)
        start = slab_base(position)
        other = slot_other(slot)
        shift = displacement(
            jnp.where(other >= width, 1.0, 0.0).astype(F32), slot_step_y(slot), slot_wrap(slot)
        )
        home = jnp.where(named < 0, whole, turned_leaf[jnp.where(named < 0, 0, start + slot_home(slot))])
        other = jnp.where(named < 0, whole, turned_leaf[jnp.where(named < 0, 0, start + other)])
        return home, other, tile_of(home), tile_of(other) + shift, shift

    def distances(group):
        row = lax.broadcasted_iota(jnp.int32, (8, LEAF), 0)
        for k in range(UNROLL):
            _, _, near, far, _ = slot_tiles(group * UNROLL + k)
            near_pos = [near[j : j + 1] for j in range(3)]
            far_pos = [far[j : j + 1] for j in range(3)]
            near_k = jnp.where(
                row < 3,
                near,
                jnp.where(row == 3, dot3(near_pos, near_pos), jnp.where(row == 4, 1.0, 0.0)),
            )
            far_k = jnp.where(
                row < 3,
                (-2.0 / SUPPORT**2) * far,
                jnp.where(
                    row == 4,
                    dot3(far_pos, far_pos) * (1.0 / SUPPORT**2),
                    jnp.where(row == 3, 1.0 / SUPPORT**2, 0.0),
                ),
            )
            dist[k] = bilinear(near_k, far_k)

    def moment_group(group, carry):
        parts = []
        for k in range(UNROLL):
            home, other, near, far, shift = slot_tiles(group * UNROLL + k)
            weight = jnp.where(home == other, 0.5, 1.0).astype(F32)
            smooth = smoothing_of(dist[k], KERNEL_NORM * weight)
            high = smooth.astype(BF16)
            low = (smooth - high.astype(F32)).astype(BF16)
            row_part = lax.dot_general(
                moment_features(far),
                jnp.concatenate([high, low], axis=1),
                (((1,), (1,)), ((), ())),
                preferred_element_type=F32,
            )
            col_part = lax.dot_general(
                moment_features(near - shift),
                jnp.concatenate([high, low], axis=0),
                (((1,), (0,)), ((), ())),
                preferred_element_type=F32,
            )
            parts.append((home, other, row_part, col_part))
        distances(group + 1)
        for home, other, row_part, col_part in parts:
            raw[rows_of(home, 32), :] += row_part[:32] + row_part[32:]
            raw[rows_of(other, 32), :] += col_part[:32] + col_part[32:]
        return carry

    distances(0)
    lax.fori_loop(0, (used + UNROLL - 1) // UNROLL, moment_group, 0)

    def finish(first_leaf, first_seat):
        def tile(k):
            return local[pl.ds(first_leaf * 8 + k, 8, stride=8), :]

        payload = finish_leaves(lambda k: raw[pl.ds(first_leaf * 32 + k, 8, stride=32), :], tile)
        for k, entry in enumerate(payload):
            pay[pl.ds(first_seat * 24 + k, 8, stride=24), :] = entry
        for k, entry in enumerate(far_coefficients(tile, payload)):
            for row in range(8):
                value = jnp.broadcast_to(jnp.asarray(entry.get(row, 0.0), F32), (8, LEAF))
                far_coef[pl.ds(first_seat * 64 + 8 * k + row, 8, stride=64), :] = value

    def finish_own(group, carry):
        finish(width + 8 * group, 8 * group)
        return carry

    def finish_upper(group, carry):
        finish(2 * width + 8 * group, up + 8 * group)
        return carry

    lax.fori_loop(0, (length + 8) // 8, finish_own, 0)
    lax.fori_loop(0, (length + 9) // 8, finish_upper, 0)

    splits = LEAF // ROWS

    picked = lax.broadcasted_iota(jnp.int32, (48, LEAF), 0)
    for k in range(5):
        chosen = (picked == 3 + k) | (picked == 27 + k) | (picked == 43 + k)
        spread[:, k * LEAF : (k + 1) * LEAF] = jnp.where(chosen, 0.5 if k < 3 else 1.0, 0.0).astype(
            BF16
        )

    def turn_home(seat):
        tile = tile_of(width + seat)
        payload = pay[rows_of(seat, 24), :]
        generic = {0: 1.0}
        generic.update({1 + k: tile[k : k + 1] for k in range(6)})
        generic = stack_near(stack_rows(generic))
        coefficients = [stack_near(entry) for entry in near_coefficients(tile, payload)]
        planes = jnp.dot(stack_near(tile).T, spread[...], preferred_element_type=F32)
        turned_far = generic.T
        turned_near = [coefficients[k].T for k in (0, 4, 5, 6, 7, 8)]
        turned_toward = [
            jnp.concatenate([coefficients[1 + k], generic], axis=0).T for k in range(3)
        ]
        for part in range(splits):
            rows = slice(part * ROWS, (part + 1) * ROWS)
            place = seat * splits + part
            for k in range(6):
                near_left[place, k * ROWS : (k + 1) * ROWS, 0:48] = turned_near[k][rows]
            for k in range(3):
                toward_left[place, k * ROWS : (k + 1) * ROWS, 0:96] = turned_toward[k][rows]
            far_left[place, :, 0:48] = turned_far[rows]
            for k in range(5):
                near_plane[place, k] = planes[rows, k * LEAF : (k + 1) * LEAF]

    def turn_two(pair, carry):
        turn_home(2 * pair)
        turn_home(2 * pair + 1)
        return carry

    lax.fori_loop(0, (length + 1) // 2, turn_two, 0)

    def prepare_slot(index, count):
        slot = mine[index]
        valid = (index < kept).astype(jnp.int32)
        column = slot_home(slot)
        away = slot_other(slot)
        is_upper = away >= width
        other = width + away
        step_x = jnp.where(is_upper, 1.0, 0.0).astype(F32)
        step_y = slot_step_y(slot)
        wrap = slot_wrap(slot)
        other_seat = jnp.where(
            is_upper,
            up + lax.rem(away - upper_base, width),
            lax.rem(away + width - base, width),
        )
        for part in range(splits):
            item_left[count] = (column - base) * splits + part
            item_index[count] = index
            item_seat[count] = jnp.where(column == away, -1 - other_seat, other_seat)
            count = count + valid * (count_of(column) > part * ROWS).astype(jnp.int32)

        far = tile_of(turned_leaf[other]) + displacement(step_x, step_y, wrap)
        row = lax.broadcasted_iota(jnp.int32, (8, LEAF), 0)
        pos = [far[k : k + 1] for k in range(3)]
        generic = {0: 1.0, 7: dot3(pos, pos)}
        generic.update({1 + k: far[k : k + 1] for k in range(6)})
        generic = stack_far(stack_rows(generic))
        near_right[index] = generic
        for k in range(8):
            entry = far_coef[pl.ds(pl.multiple_of(other_seat * 64 + 8 * k, 8), 8), :]
            change = entry[1:2] * step_x + entry[2:3] * step_y
            if k == 4:
                change = change + 0.5 * wrap
            entry = stack_far(jnp.where(row == 0, entry - change, entry))
            if k < 3:
                toward_right[index, 0:48, k * LEAF : (k + 1) * LEAF] = generic
                toward_right[index, 48:96, k * LEAF : (k + 1) * LEAF] = entry
            else:
                far_right[index, :, (k - 3) * LEAF : (k - 2) * LEAF] = entry
        far_half[index, 0:5] = jnp.concatenate([0.5 * far[3:6], far[6:8]], axis=0)
        return count

    def prepare_two(pair, count):
        return prepare_slot(2 * pair + 1, prepare_slot(2 * pair, count))

    mine[kept] = mine[0]
    item_count = lax.fori_loop(0, (kept + 1) // 2, prepare_two, 0)
    for extra in range(2):
        item_left[item_count + extra] = 0
        item_index[item_count + extra] = 0

    def state_forms(position):
        index = item_index[position]
        left = item_left[position]
        near_form[...] = jnp.dot(
            near_left[left, ROWS : 6 * ROWS, 0:48], near_right[index], preferred_element_type=F32
        )
        far_form[...] = jnp.dot(
            far_left[left, :, 0:48], far_right[index], preferred_element_type=F32
        )

    def space_forms(position):
        index = item_index[position]
        left = item_left[position]
        dist_form[...] = jnp.dot(
            near_left[left, 0:ROWS, 0:48], near_right[index], preferred_element_type=F32
        )
        for k in range(3):
            toward_form[k * ROWS : (k + 1) * ROWS, :] = jnp.dot(
                toward_left[left, k * ROWS : (k + 1) * ROWS, 0:96],
                toward_right[index, :, k * LEAF : (k + 1) * LEAF],
                preferred_element_type=F32,
            )

    def geometry():
        return face_geometry(
            dist_form[...], [toward_form[k * ROWS : (k + 1) * ROWS, :] for k in range(3)]
        )

    def keep_geometry(values):
        for k in range(4):
            geo_form[k * ROWS : (k + 1) * ROWS, :] = values[k]

    def flux_item(position, carry):
        left = item_left[position]
        index = item_index[position]
        coded = item_seat[position]
        other_seat = jnp.where(coded < 0, -1 - coded, coded)
        weight = jnp.where(coded < 0, 0.0, 1.0).astype(F32)
        fluxes = face_fluxes(
            [near_form[k * ROWS : (k + 1) * ROWS, :] for k in range(5)],
            [far_form[:, k * LEAF : (k + 1) * LEAF] for k in range(5)],
            [geo_form[k * ROWS : (k + 1) * ROWS, :] for k in range(3)],
            geo_form[3 * ROWS : 4 * ROWS, :],
            [near_plane[left, k] for k in range(5)],
            [far_half[index, k : k + 1, :] for k in range(5)],
        )
        following = geometry()
        keep_geometry(following)
        state_forms(position + 1)
        space_forms(position + 2)
        for k in range(5):
            row_sum[left, k] += fluxes[k]
            col_sum[other_seat, 8 * k : 8 * k + 8] += weight * sum(
                fluxes[k][8 * j : 8 * j + 8] for j in range(ROWS // 8)
            )
        return carry

    space_forms(0)
    keep_geometry(geometry())
    state_forms(0)
    space_forms(1)
    lax.fori_loop(0, item_count, flux_item, 0)

    def row_total(seat, carry):
        sums = {}
        for c in range(5):
            pieces = [row_sum[seat * splits + part, c] for part in range(splits)]
            turned = jnp.concatenate(pieces, axis=0).T
            sums[c] = jnp.sum(turned, axis=0, keepdims=True)
        row_rate[seat] = stack_rows(sums)
        return carry

    lax.fori_loop(0, length, row_total, 0)
    row_rate[length] = jnp.zeros((8, LEAF), F32)

    def rates(seat, less, leaf, column):
        total = stack_rows(
            {
                k: jnp.sum(col_sum[seat, 8 * k : 8 * k + 8], axis=0, keepdims=True)
                for k in range(5)
            }
        )
        if less is not None:
            total = total - less
        live = tile_of(leaf)[0:1] < 0.5 * AWAY
        scale = AREA_FLOOR * pay[rows_of(seat, 24), :][0:1]
        return lax.rem(column, width), jnp.where(live, total * scale, 0.0)

    def write_own(k, carry):
        column, value = rates(k, row_rate[k], width + k, base + k)
        for c in range(5):
            own_out[pl.ds(c * width + column, 1), :] = value[c : c + 1]
        return carry

    def write_upper(k, carry):
        column, value = rates(up + k, None, 2 * width + k, upper_base + k)
        for c in range(5):
            next_out[pl.ds(c * width + column, 1), :] = value[c : c + 1]
        return carry

    lax.fori_loop(0, length + 1, write_own, 0)
    lax.fori_loop(0, length + 2, write_upper, 0)


def shards(positions, velocity, density, pressure, counts, pair_list):
    width = counts.shape[0]
    slots = pair_list.shape[1]
    particles = width * LEAF
    sub_count = lax.axis_size("sub")
    leaf_sub = width // sub_count

    smem = pl.BlockSpec(memory_space=pltpu.SMEM)
    vmem = pl.BlockSpec(memory_space=pltpu.VMEM)
    lanes = -(-(slots + max(leaf_sub + 1, width)) // LEAF) * LEAF
    state, listed = pl.pallas_call(
        functools.partial(pack_kernel, width, leaf_sub),
        out_shape=[
            jax.ShapeDtypeStruct((8, particles), F32),
            jax.ShapeDtypeStruct((4, lanes), F32),
        ],
        in_specs=[smem, vmem, vmem, vmem, vmem, vmem, vmem],
        out_specs=[vmem, vmem],
        name="pack",
    )(
        counts,
        counts[None],
        positions,
        velocity,
        density[None],
        pressure[None],
        pair_list,
    )
    kept_state, kept_listed = lax.optimization_barrier(
        (jnp.where(state == state, state, 0.0), jnp.where(listed == listed, listed, 0.0))
    )
    lists = jnp.stack([shifted(listed, "slab", 1), kept_listed, shifted(listed, "slab", -1)])[None]
    lower = shifted(state, "slab", 1)
    upper = shifted(state, "slab", -1)
    beyond = shifted(state, "slab", -2)
    mask = 1
    while mask < sub_count:
        lists = jnp.concatenate([lists, swapped(lists, "sub", mask)], axis=0)
        mask *= 2
    rec = lists.astype(jnp.int32).reshape(-1)
    cap = 2 * leaf_sub
    most = cap * CAND
    splits = LEAF // ROWS
    seats = 2 * upper_seat_of(cap)

    own_part, next_part = pl.pallas_call(
        functools.partial(step_kernel, width, sub_count, slots),
        out_shape=[jax.ShapeDtypeStruct((5 * width, LEAF), F32)] * 2,
        in_specs=[smem, vmem, vmem, vmem, vmem],
        out_specs=[vmem, vmem],
        scratch_shapes=[
            pltpu.SMEM((3 * sub_count * slots + 2 * UNROLL,), jnp.int32),
            pltpu.SMEM((most + 1,), jnp.int32),
            pltpu.SMEM((7 * width + 1,), jnp.int32),
            pltpu.SMEM((width,), jnp.int32),
        ]
        + [pltpu.SMEM((most * splits + 2,), jnp.int32)] * 3
        + [
            pltpu.SMEM((4 * width,), jnp.int32),
            pltpu.VMEM(((4 * width + 1) * 8, LEAF), F32),
            pltpu.VMEM(((4 * width + 1) * 32, LEAF), F32),
            pltpu.VMEM((seats * 24, LEAF), F32),
            pltpu.VMEM((seats * 64, LEAF), F32),
            pltpu.VMEM((cap * splits, 6 * ROWS, LEAF), BF16),
            pltpu.VMEM((cap * splits, ROWS, LEAF), BF16),
            pltpu.VMEM((cap * splits, 3 * ROWS, LEAF), BF16),
            pltpu.VMEM((cap * splits, 5, ROWS, LEAF), F32),
            pltpu.VMEM((most, 48, LEAF), BF16),
            pltpu.VMEM((most, 48, 5 * LEAF), BF16),
            pltpu.VMEM((most, 96, 3 * LEAF), BF16),
            pltpu.VMEM((most, 8, LEAF), F32),
            pltpu.VMEM((48, 5 * LEAF), BF16),
            pltpu.VMEM((UNROLL, LEAF, LEAF), F32),
            pltpu.VMEM((5 * ROWS, LEAF), F32),
            pltpu.VMEM((ROWS, 5 * LEAF), F32),
            pltpu.VMEM((3 * ROWS, LEAF), F32),
            pltpu.VMEM((ROWS, LEAF), F32),
            pltpu.VMEM((4 * ROWS, LEAF), F32),
            pltpu.VMEM((seats, 40, LEAF), F32),
            pltpu.VMEM((cap * splits, 5, ROWS, LEAF), F32),
            pltpu.VMEM((cap + 1, 8, LEAF), F32),
        ],
        compiler_params=pltpu.CompilerParams(vmem_limit_bytes=48 * 1024 * 1024),
        name="hydro_step",
    )(rec, lower, kept_state, upper, beyond)

    merged = own_part + shifted(next_part, "slab", 1)
    mask = 1
    while mask < sub_count:
        merged = merged + swapped(merged, "sub", mask)
        mask *= 2
    return merged.reshape(5, particles)


def solution(mesh):
    placed = (
        P(None, "slab"),
        P(None, "slab"),
        P("slab"),
        P("slab"),
        P("slab"),
        P(None, ("slab", "sub")),
    )
    return jax.shard_map(
        shards, mesh=mesh, in_specs=placed, out_specs=P(None, "slab"), check_vma=False
    )
```

```python
import functools
import math

import jax
import jax.numpy as jnp
from jax import lax
from jax.experimental import pallas as pl
from jax.experimental.pallas import tpu as pltpu
from jax.sharding import PartitionSpec as P

LEAF = 128
CAND = 5

GAMMA = 5.0 / 3.0
SUPPORT = 1.5
KERNEL_NORM = 21.0 / (2.0 * math.pi * SUPPORT**3)
MOMENT_REG = 0.05
AREA_FLOOR = 0.0001
AWAY = 64.0
UNROLL = 12
ROWS = 64
ROWS_LOG = 6
COST_LEAF, COST_SLOT, COST_PART = 17, 3, 5
F32 = jnp.float32
BF16 = jnp.bfloat16


def shifted(shard, axis, by):
    peers = lax.axis_size(axis)
    return lax.ppermute(shard, axis, [(i, (i + by) % peers) for i in range(peers)])


def swapped(shard, axis, mask):
    peers = lax.axis_size(axis)
    return lax.ppermute(shard, axis, [(i, i ^ mask) for i in range(peers)])


def reciprocal(value):
    return pl.reciprocal(value, approx=True)


def smoothing_of(dist_sq, scale):
    safe = jnp.maximum(dist_sq, 1e-12)
    radius = safe * lax.rsqrt(safe)
    inside = jnp.maximum(1.0 - radius, 0.0)
    square = inside * inside
    return (square * square) * (scale + (scale * 4.0) * radius)


def split_three(value):
    high = value.astype(BF16).astype(F32)
    rest = value - high
    middle = rest.astype(BF16).astype(F32)
    return high, middle, rest - middle


def stack_near(rows):
    high, middle, low = split_three(rows)
    return jnp.concatenate([high, high, high, middle, middle, low], axis=0).astype(BF16)


def stack_far(rows):
    high, middle, low = split_three(rows)
    return jnp.concatenate([high, middle, low, high, middle, high], axis=0).astype(BF16)


def bilinear(near_rows, far_rows):
    return lax.dot_general(
        stack_near(near_rows),
        stack_far(far_rows),
        (((0,), (0,)), ((), ())),
        preferred_element_type=F32,
    )


def moment_features(tile):
    row = lax.broadcasted_iota(jnp.int32, tile.shape, 0)
    by_x = tile * tile[0:1]
    by_y = jnp.where(row == 0, 1.0, tile * tile[1:2])
    by_z = tile * tile[2:3]
    whole = jnp.concatenate([tile, by_x, by_y, by_z], axis=0)
    high = whole.astype(BF16)
    low = (whole - high.astype(F32)).astype(BF16)
    both = jnp.concatenate([high, low], axis=0)
    return jnp.concatenate([both, both], axis=1)


def displacement(step_x, step_y, wrap):
    row = lax.broadcasted_iota(jnp.int32, (8, LEAF), 0)
    zero = jnp.zeros((8, LEAF), F32)
    out = jnp.where(row == 0, step_x, zero)
    out = jnp.where(row == 1, step_y, out)
    return jnp.where(row == 4, -wrap, out)


def finish_leaves(raw, tile):
    pos = [tile(k) for k in range(3)]
    live = pos[0] < 0.5 * AWAY
    total = raw(16)
    first = [raw(k) - pos[k] * total for k in range(3)]

    def second(left, right):
        lead = raw(8 + 8 * left + right)
        return lead - pos[left] * raw(right) - pos[right] * first[left]

    density = jnp.where(live, total, 1.0)
    inverse_density = 1.0 / density

    def scaled(value):
        return jnp.where(live, value * inverse_density, 0.0)

    exx = scaled(second(0, 0)) + MOMENT_REG
    exy = scaled(second(0, 1))
    exz = scaled(second(0, 2))
    eyy = scaled(second(1, 1)) + MOMENT_REG
    eyz = scaled(second(1, 2))
    ezz = scaled(second(2, 2)) + MOMENT_REG
    mxx = eyy * ezz - eyz * eyz
    mxy = exz * eyz - exy * ezz
    mxz = exy * eyz - exz * eyy
    myy = exx * ezz - exz * exz
    myz = exy * exz - exx * eyz
    mzz = exx * eyy - exy * exy
    scale = 1.0 / (exx * mxx + exy * mxy + exz * mxz)
    inverse = [entry * scale for entry in (mxx, mxy, mxz, myy, myz, mzz)]
    square = inverse_density * inverse_density
    rows = [density] + [entry * square for entry in inverse]
    for quantity in range(3, 8):
        value = tile(quantity)
        along = [
            scaled(
                raw(8 + 8 * k + quantity)
                - pos[k] * raw(quantity)
                - value * first[k]
            )
            for k in range(3)
        ]
        half = [0.5 * term for term in along]
        rows.append(inverse[0] * half[0] + inverse[1] * half[1] + inverse[2] * half[2])
        rows.append(inverse[1] * half[0] + inverse[3] * half[1] + inverse[4] * half[2])
        rows.append(inverse[2] * half[0] + inverse[4] * half[1] + inverse[5] * half[2])
    return rows


def dot3(left, right):
    return left[0] * right[0] + left[1] * right[1] + left[2] * right[2]


def apply_sym(matrix, vector):
    return [
        dot3((matrix[0], matrix[1], matrix[2]), vector),
        dot3((matrix[1], matrix[3], matrix[4]), vector),
        dot3((matrix[2], matrix[4], matrix[5]), vector),
    ]


def stack_rows(rows):
    row = lax.broadcasted_iota(jnp.int32, (8, LEAF), 0)
    out = jnp.zeros((8, LEAF), F32)
    for k, entry in rows.items():
        out = jnp.where(row == k, entry, out)
    return out


def near_coefficients(tile, pay):
    pos = [tile[k : k + 1] for k in range(3)]
    twice = [(-2.0 / SUPPORT**2) * entry for entry in pos]
    out = [
        {
            0: dot3(pos, pos) * (1.0 / SUPPORT**2),
            1: twice[0],
            2: twice[1],
            3: twice[2],
            7: 1.0 / SUPPORT**2,
        }
    ]
    matrix = [pay[1 + k : 2 + k] for k in range(6)]
    for line in ((0, 1, 2), (1, 3, 4), (2, 4, 5)):
        entries = [matrix[k] for k in line]
        out.append({0: -dot3(entries, pos), 1: entries[0], 2: entries[1], 3: entries[2]})
    for quantity in range(5):
        slope = [pay[7 + 3 * quantity + k : 8 + 3 * quantity + k] for k in range(3)]
        value = tile[3 + quantity : 4 + quantity]
        if quantity < 3:
            entry = {0: 0.5 * value - dot3(slope, pos), 4 + quantity: -0.5}
        else:
            entry = {0: value - dot3(slope, pos)}
        entry.update({1: slope[0], 2: slope[1], 3: slope[2]})
        out.append(entry)
    return [stack_rows(entry) for entry in out]


def far_coefficients(tile, pay):
    pos = [tile(k) for k in range(3)]
    out = []
    matrix = [pay[1 + k] for k in range(6)]
    for line in ((0, 1, 2), (1, 3, 4), (2, 4, 5)):
        entries = [matrix[k] for k in line]
        out.append({0: dot3(entries, pos), 1: -entries[0], 2: -entries[1], 3: -entries[2]})
    for quantity in range(5):
        slope = [pay[7 + 3 * quantity + k] for k in range(3)]
        value = tile(3 + quantity)
        if quantity < 3:
            entry = {0: 0.5 * value - dot3(slope, pos), 4 + quantity: -0.5}
        else:
            entry = {0: value - dot3(slope, pos)}
        entry.update({1: slope[0], 2: slope[1], 3: slope[2]})
        out.append(entry)
    return out


def limited(value, low, high):
    return jnp.minimum(jnp.maximum(value, low), high)


def face_geometry(dist_sq, toward):
    smooth = smoothing_of(dist_sq, KERNEL_NORM / AREA_FLOOR)
    length_sq = jnp.maximum(dot3(toward, toward), 1e-30)
    inverse_length = lax.rsqrt(length_sq)
    area = smooth * (length_sq * inverse_length)
    scale = jnp.minimum(inverse_length, smooth)
    return [entry * scale for entry in toward] + [area]


def face_fluxes(near_out, far_out, normal, area, near_plain, far_plain):
    left_vel, right_vel = [], []
    for k in range(3):
        high = jnp.abs(far_plain[k] - near_plain[k])
        low = -high
        left_vel.append(limited(near_out[k], low, high))
        right_vel.append(limited(far_out[k], low, high))
    face_vel = [near_plain[k] + far_plain[k] for k in range(3)]
    thermo = []
    for k in range(2):
        low = jnp.minimum(near_plain[3 + k], far_plain[3 + k])
        high = jnp.maximum(near_plain[3 + k], far_plain[3 + k])
        thermo.append(limited(near_out[3 + k], low, high))
        thermo.append(limited(far_out[3 + k], low, high))
    left_rho, right_rho, left_p, right_p = thermo
    left_u = dot3(left_vel, normal)
    right_u = dot3(right_vel, normal)
    left_gp = GAMMA * left_p
    right_gp = GAMMA * right_p
    left_c = left_gp * lax.rsqrt(left_gp * left_rho)
    right_c = right_gp * lax.rsqrt(right_gp * right_rho)
    slow = jnp.minimum(left_u - left_c, right_u - right_c)
    fast = jnp.maximum(left_u + left_c, right_u + right_c)
    left_m = left_rho * (slow - left_u)
    right_m = right_rho * (fast - right_u)
    contact = (right_p - left_p + left_m * left_u - right_m * right_u) * reciprocal(
        left_m - right_m
    )
    is_left = contact >= 0.0
    speed = jnp.where(is_left, jnp.minimum(slow, 0.0), jnp.maximum(fast, 0.0))
    rho = jnp.where(is_left, left_rho, right_rho) * area
    press = jnp.where(is_left, left_p, right_p) * area
    normal_speed = jnp.where(is_left, left_u, right_u)
    vel = [jnp.where(is_left, left_vel[k], right_vel[k]) + face_vel[k] for k in range(3)]
    lag = speed - normal_speed
    ratio = lag * reciprocal(speed - contact)
    through = ratio * contact
    gain = speed * ratio - speed
    push = (rho * lag) * gain
    mass = rho * through
    total_p = press + push
    mom = [mass * vel[k] + total_p * normal[k] for k in range(3)]
    energy = press * (through * (1.0 / (GAMMA - 1.0)) + normal_speed + gain) + push * contact
    energy = energy + (0.5 * mass) * dot3(vel, vel) + total_p * dot3(face_vel, normal)
    return [mass] + mom + [energy]


def pack_kernel(
    width,
    leaf_sub,
    counts,
    counts_row,
    positions,
    velocity,
    density,
    pressure,
    pair_list,
    state,
    listed,
):
    slab = lax.axis_index("slab")
    centre_x = slab.astype(F32) + 0.5
    row = lax.broadcasted_iota(jnp.int32, (3, LEAF), 0)
    lane = lax.broadcasted_iota(jnp.int32, (3, LEAF), 1)

    def one_leaf(column, carry):
        lanes = pl.ds(pl.multiple_of(column * LEAF, LEAF), LEAF)
        centre_y = column.astype(F32) + 0.5
        centre = jnp.where(row == 0, centre_x, jnp.where(row == 1, centre_y, 0.5))
        dead = (row == 0) & (lane >= counts[column])
        state[0:3, lanes] = jnp.where(dead, AWAY, positions[:, lanes] - centre)
        state[3:6, lanes] = velocity[:, lanes]
        state[6:7, lanes] = density[:, lanes]
        state[7:8, lanes] = pressure[:, lanes]
        return carry

    lax.fori_loop(0, width, one_leaf, 0, unroll=4)
    listed[...] = jnp.zeros(listed.shape, F32)
    slots = pair_list.shape[1]
    heads = pair_list[0:1, :]
    tails = pair_list[1:2, :]
    offsets = pair_list[2:3, :]
    occupied = heads >= 0
    head_col = heads - slab * width
    inside = (tails >= slab * width) & (tails < (slab + 1) * width)
    next_slab = lax.rem(slab + 1, lax.axis_size("slab"))
    tail_col = jnp.where(inside, tails - slab * width, tails - next_slab * width)
    outside = occupied & jnp.logical_not(inside)
    wraps = outside & (tails < heads)
    step_y = tail_col + offsets - head_col
    empty = 4 * width
    here = slice(0, slots)
    listed[0:1, here] = jnp.where(occupied, head_col, empty).astype(F32)
    listed[0:1, slots : slots + width] = counts_row[...].astype(F32)
    listed[1:2, here] = jnp.where(
        occupied, jnp.where(inside, tail_col, tail_col + width), empty
    ).astype(F32)
    listed[2:3, here] = jnp.where(occupied, step_y, 0).astype(F32)
    listed[3:4, here] = jnp.where(wraps, 1.0, 0.0)
    seats = head_col - lax.axis_index("sub") * leaf_sub
    behind = lax.broadcasted_iota(jnp.int32, (1, leaf_sub + 1), 1)
    shifts = lax.rem(5 * width * LEAF - offsets, width)
    shift = jnp.max(jnp.where(outside, shifts, 0), axis=1, keepdims=True).astype(F32)
    facts = jnp.where(behind == leaf_sub, shift, 0.0)
    for k in range(leaf_sub):
        found = jnp.where(occupied & (seats == k), 1.0, 0.0)
        facts = jnp.where(behind == k, jnp.sum(found, axis=1, keepdims=True), facts)
    listed[3:4, slots : slots + leaf_sub + 1] = facts


def upper_seat_of(cap):
    return -(-(cap + 2) // 8) * 8


def step_kernel(
    width,
    sub_count,
    slots,
    rec,
    lower_ref,
    own_ref,
    upper_ref,
    beyond_ref,
    own_out,
    next_out,
    order,
    mine,
    need,
    costs,
    item_left,
    item_index,
    item_seat,
    turned_leaf,
    local,
    raw,
    pay,
    far_coef,
    near_left,
    far_left,
    toward_left,
    near_plane,
    near_right,
    far_right,
    toward_right,
    far_half,
    spread,
    dist,
    near_form,
    far_form,
    toward_form,
    dist_form,
    geo_form,
    col_sum,
    row_sum,
    row_rate,
):
    whole = 4 * width
    leaf_sub = width // sub_count
    cap = -(-2 * leaf_sub // 4) * 4
    up = upper_seat_of(cap)
    stride = rec.shape[0] // (12 * sub_count)
    block = 4 * stride

    def count_of(column):
        return rec[block + slots + column]

    def slot_home(slot):
        return rec[slot]

    def slot_other(slot):
        return rec[slot + stride]

    def slot_step_y(slot):
        return rec[slot + 2 * stride].astype(F32)

    def slot_wrap(slot):
        return rec[slot + 3 * stride].astype(F32)

    def clear_need(entry, carry):
        need[entry] = 0
        return carry

    lax.fori_loop(0, 7 * width, clear_need, 0, unroll=16)
    need[7 * width] = 0

    me = lax.axis_index("sub")
    total_cost = jnp.int32(0)
    shift_w = jnp.int32(0)
    for group in range(sub_count):
        seats = jnp.bitwise_xor(me, group) * leaf_sub
        facts = (3 * group + 1) * block + 3 * stride + slots
        shift_w = jnp.maximum(shift_w, rec[facts + leaf_sub])
        for k in range(leaf_sub):
            parts = lax.shift_right_logical(count_of(seats + k) + (ROWS - 1), ROWS_LOG)
            cost = COST_LEAF + rec[facts + k] * (COST_SLOT + COST_PART * parts)
            costs[seats + k] = cost
            total_cost = total_cost + cost

    def deal(column, state):
        owner, length, before, first, mine_length = state
        cost = costs[column]
        middle = sub_count * (2 * before + cost)
        wish = (middle >= 2 * total_cost * (owner + 1)) | (length == cap)
        allowed = (owner < sub_count - 1) & (width - column <= (sub_count - 1 - owner) * cap)
        step = (wish & allowed).astype(jnp.int32)
        owner = owner + step
        length = (1 - step) * length + 1
        is_mine = (owner == me).astype(jnp.int32)
        first = jnp.where((is_mine > 0) & (mine_length == 0), column, first)
        return owner, length, before + cost, first, mine_length + is_mine

    zero = jnp.int32(0)
    _, _, _, base, length = lax.fori_loop(
        0, width, deal, (zero, zero, zero, zero, zero), unroll=4
    )
    upper_base = lax.rem(base + width - 1 + shift_w, width)

    def own_leaf(k):
        return width + lax.rem(base + k, width)

    def upper_leaf(k):
        return 2 * width + lax.rem(upper_base + k, width)

    def mark_own(k, carry):
        need[own_leaf(k)] = jnp.where(k < length, 3, 1)
        return carry

    def mark_upper(k, carry):
        need[upper_leaf(k)] = 1
        return carry

    lax.fori_loop(0, length + 1, mark_own, 0)
    lax.fori_loop(0, length + 2, mark_upper, 0)

    def collect_lower(k, carry):
        used, first = carry
        order[used] = first + k
        return used + (need[slot_other(first + k)] & 1), first

    def collect_own(k, carry):
        used, kept, first = carry
        slot = first + k
        flags = need[width + slot_home(slot)]
        order[used] = slot
        mine[kept] = slot
        used = used + ((flags | need[width + slot_other(slot)]) & 1)
        return used, kept + lax.shift_right_logical(flags, 1), first

    def collect_upper(k, carry):
        used, first = carry
        slot = first + k
        order[used] = slot
        flags = need[2 * width + slot_home(slot)] | need[2 * width + slot_other(slot)]
        return used + (flags & 1), first

    def touches(first, last, start, count):
        ahead = lax.rem(first - start + 4 * width, width) < count
        return ahead | (lax.rem(start - first + 4 * width, width) <= last - first)

    used, kept = zero, zero
    for group in range(sub_count):
        first = jnp.bitwise_xor(me, group) * leaf_sub
        slot = 3 * group * block
        moved = first + rec[slot + 3 * stride + slots + leaf_sub]
        used = lax.cond(
            touches(moved - 1, moved + leaf_sub, base, length + 1),
            lambda used, slot=slot: lax.fori_loop(
                0, slots, collect_lower, (used, slot), unroll=8
            )[0],
            lambda used: used,
            used,
        )
    from_own = used
    for group in range(sub_count):
        first = jnp.bitwise_xor(me, group) * leaf_sub
        slot = (3 * group + 1) * block
        used, kept = lax.cond(
            touches(first - 1, first + leaf_sub, base - 1, length + 2),
            lambda used, kept, slot=slot: lax.fori_loop(
                0, slots, collect_own, (used, kept, slot), unroll=8
            )[0:2],
            lambda used, kept: (used, kept),
            used,
            kept,
        )
    from_upper = used
    for group in range(sub_count):
        first = jnp.bitwise_xor(me, group) * leaf_sub
        slot = (3 * group + 2) * block
        used = lax.cond(
            touches(first, first + leaf_sub, upper_base, length + 2),
            lambda used, slot=slot: lax.fori_loop(
                0, slots, collect_upper, (used, slot), unroll=8
            )[0],
            lambda used: used,
            used,
        )
    for extra in range(2 * UNROLL):
        order[used + extra] = -1

    def rows_of(leaf, count):
        return pl.ds(pl.multiple_of(leaf * count, count), count)

    def load_leaf(column, carry):
        lanes = pl.ds(pl.multiple_of(column * LEAF, LEAF), LEAF)
        places = (
            column,
            width + lax.rem(column - base + width, width),
            2 * width + lax.rem(column - upper_base + width, width),
            3 * width + column,
        )
        for slab, ref in enumerate((lower_ref, own_ref, upper_ref, beyond_ref)):
            local[rows_of(places[slab], 8), :] = ref[:, lanes]
            turned_leaf[slab * width + column] = places[slab]
            raw[rows_of(slab * width + column, 32), :] = jnp.zeros((32, LEAF), F32)
        for k in range(5):
            own_out[pl.ds(k * width + column, 1), :] = jnp.zeros((1, LEAF), F32)
            next_out[pl.ds(k * width + column, 1), :] = jnp.zeros((1, LEAF), F32)
        return carry

    lax.fori_loop(0, width, load_leaf, 0)
    local[rows_of(whole, 8), :] = jnp.zeros((8, LEAF), F32)
    raw[rows_of(whole, 32), :] = jnp.zeros((32, LEAF), F32)

    def tile_of(leaf):
        return local[rows_of(leaf, 8), :]

    def slab_base(position):
        return jnp.where(position < from_own, 0, jnp.where(position < from_upper, width, 2 * width))

    def clear_rows(seat, carry):
        for part in range(LEAF // ROWS):
            for k in range(5):
                row_sum[seat * (LEAF // ROWS) + part, k] = jnp.zeros((ROWS, LEAF), F32)
        return carry

    lax.fori_loop(0, length, clear_rows, 0)

    def clear_cols(seat, carry):
        col_sum[seat] = jnp.zeros((40, LEAF), F32)
        return carry

    lax.fori_loop(0, length + 1, clear_cols, 0)
    lax.fori_loop(up, up + length + 2, clear_cols, 0)

    def slot_tiles(position):
        named = order[position]
        slot = jnp.maximum(named, 0)
        start = slab_base(position)
        other = slot_other(slot)
        shift = displacement(
            jnp.where(other >= width, 1.0, 0.0).astype(F32), slot_step_y(slot), slot_wrap(slot)
        )
        home = jnp.where(named < 0, whole, turned_leaf[jnp.where(named < 0, 0, start + slot_home(slot))])
        other = jnp.where(named < 0, whole, turned_leaf[jnp.where(named < 0, 0, start + other)])
        return home, other, tile_of(home), tile_of(other) + shift, shift

    def distances(group):
        row = lax.broadcasted_iota(jnp.int32, (8, LEAF), 0)
        for k in range(UNROLL):
            _, _, near, far, _ = slot_tiles(group * UNROLL + k)
            near_pos = [near[j : j + 1] for j in range(3)]
            far_pos = [far[j : j + 1] for j in range(3)]
            near_k = jnp.where(
                row < 3,
                near,
                jnp.where(row == 3, dot3(near_pos, near_pos), jnp.where(row == 4, 1.0, 0.0)),
            )
            far_k = jnp.where(
                row < 3,
                (-2.0 / SUPPORT**2) * far,
                jnp.where(
                    row == 4,
                    dot3(far_pos, far_pos) * (1.0 / SUPPORT**2),
                    jnp.where(row == 3, 1.0 / SUPPORT**2, 0.0),
                ),
            )
            dist[k] = bilinear(near_k, far_k)

    def moment_group(group, carry):
        parts = []
        for k in range(UNROLL):
            home, other, near, far, shift = slot_tiles(group * UNROLL + k)
            weight = jnp.where(home == other, 0.5, 1.0).astype(F32)
            smooth = smoothing_of(dist[k], KERNEL_NORM * weight)
            high = smooth.astype(BF16)
            low = (smooth - high.astype(F32)).astype(BF16)
            row_part = lax.dot_general(
                moment_features(far),
                jnp.concatenate([high, low], axis=1),
                (((1,), (1,)), ((), ())),
                preferred_element_type=F32,
            )
            col_part = lax.dot_general(
                moment_features(near - shift),
                jnp.concatenate([high, low], axis=0),
                (((1,), (0,)), ((), ())),
                preferred_element_type=F32,
            )
            parts.append((home, other, row_part, col_part))
        distances(group + 1)
        for home, other, row_part, col_part in parts:
            raw[rows_of(home, 32), :] += row_part[:32] + row_part[32:]
            raw[rows_of(other, 32), :] += col_part[:32] + col_part[32:]
        return carry

    distances(0)
    lax.fori_loop(0, (used + UNROLL - 1) // UNROLL, moment_group, 0)

    def finish(first_leaf, first_seat):
        def tile(k):
            return local[pl.ds(first_leaf * 8 + k, 8, stride=8), :]

        payload = finish_leaves(lambda k: raw[pl.ds(first_leaf * 32 + k, 8, stride=32), :], tile)
        for k, entry in enumerate(payload):
            pay[pl.ds(first_seat * 24 + k, 8, stride=24), :] = entry
        for k, entry in enumerate(far_coefficients(tile, payload)):
            for row in range(8):
                value = jnp.broadcast_to(jnp.asarray(entry.get(row, 0.0), F32), (8, LEAF))
                far_coef[pl.ds(first_seat * 64 + 8 * k + row, 8, stride=64), :] = value

    def finish_own(group, carry):
        finish(width + 8 * group, 8 * group)
        return carry

    def finish_upper(group, carry):
        finish(2 * width + 8 * group, up + 8 * group)
        return carry

    lax.fori_loop(0, (length + 8) // 8, finish_own, 0)
    lax.fori_loop(0, (length + 9) // 8, finish_upper, 0)

    splits = LEAF // ROWS

    picked = lax.broadcasted_iota(jnp.int32, (48, LEAF), 0)
    for k in range(5):
        chosen = (picked == 3 + k) | (picked == 27 + k) | (picked == 43 + k)
        spread[:, k * LEAF : (k + 1) * LEAF] = jnp.where(chosen, 0.5 if k < 3 else 1.0, 0.0).astype(
            BF16
        )

    def turn_home(seat):
        tile = tile_of(width + seat)
        payload = pay[rows_of(seat, 24), :]
        generic = {0: 1.0}
        generic.update({1 + k: tile[k : k + 1] for k in range(6)})
        generic = stack_near(stack_rows(generic))
        coefficients = [stack_near(entry) for entry in near_coefficients(tile, payload)]
        planes = jnp.dot(stack_near(tile).T, spread[...], preferred_element_type=F32)
        turned_far = generic.T
        turned_near = [coefficients[k].T for k in (0, 4, 5, 6, 7, 8)]
        turned_toward = [
            jnp.concatenate([coefficients[1 + k], generic], axis=0).T for k in range(3)
        ]
        for part in range(splits):
            rows = slice(part * ROWS, (part + 1) * ROWS)
            place = seat * splits + part
            for k in range(6):
                near_left[place, k * ROWS : (k + 1) * ROWS, 0:48] = turned_near[k][rows]
            for k in range(3):
                toward_left[place, k * ROWS : (k + 1) * ROWS, 0:96] = turned_toward[k][rows]
            far_left[place, :, 0:48] = turned_far[rows]
            for k in range(5):
                near_plane[place, k] = planes[rows, k * LEAF : (k + 1) * LEAF]

    def turn_four(group, carry):
        for k in range(4):
            turn_home(4 * group + k)
        return carry

    lax.fori_loop(0, (length + 3) // 4, turn_four, 0)

    def prepare_slot(index, count):
        slot = mine[index]
        valid = (index < kept).astype(jnp.int32)
        column = slot_home(slot)
        away = slot_other(slot)
        is_upper = away >= width
        other = width + away
        step_x = jnp.where(is_upper, 1.0, 0.0).astype(F32)
        step_y = slot_step_y(slot)
        wrap = slot_wrap(slot)
        other_seat = jnp.where(
            is_upper,
            up + lax.rem(away - upper_base, width),
            lax.rem(away + width - base, width),
        )
        for part in range(splits):
            item_left[count] = (column - base) * splits + part
            item_index[count] = index
            item_seat[count] = jnp.where(column == away, -1 - other_seat, other_seat)
            count = count + valid * (count_of(column) > part * ROWS).astype(jnp.int32)

        far = tile_of(turned_leaf[other]) + displacement(step_x, step_y, wrap)
        row = lax.broadcasted_iota(jnp.int32, (8, LEAF), 0)
        pos = [far[k : k + 1] for k in range(3)]
        generic = {0: 1.0, 7: dot3(pos, pos)}
        generic.update({1 + k: far[k : k + 1] for k in range(6)})
        generic = stack_far(stack_rows(generic))
        near_right[index] = generic
        for k in range(8):
            entry = far_coef[pl.ds(pl.multiple_of(other_seat * 64 + 8 * k, 8), 8), :]
            change = entry[1:2] * step_x + entry[2:3] * step_y
            if k == 4:
                change = change + 0.5 * wrap
            entry = stack_far(jnp.where(row == 0, entry - change, entry))
            if k < 3:
                toward_right[index, 0:48, k * LEAF : (k + 1) * LEAF] = generic
                toward_right[index, 48:96, k * LEAF : (k + 1) * LEAF] = entry
            else:
                far_right[index, :, (k - 3) * LEAF : (k - 2) * LEAF] = entry
        far_half[index, 0:5] = jnp.concatenate([0.5 * far[3:6], far[6:8]], axis=0)
        return count

    def prepare_four(group, count):
        for k in range(4):
            count = prepare_slot(4 * group + k, count)
        return count

    for extra in range(3):
        mine[kept + extra] = mine[0]
    item_count = lax.fori_loop(0, (kept + 3) // 4, prepare_four, 0)
    for extra in range(2):
        item_left[item_count + extra] = 0
        item_index[item_count + extra] = 0

    def state_forms(position):
        index = item_index[position]
        left = item_left[position]
        near_form[...] = jnp.dot(
            near_left[left, ROWS : 6 * ROWS, 0:48], near_right[index], preferred_element_type=F32
        )
        far_form[...] = jnp.dot(
            far_left[left, :, 0:48], far_right[index], preferred_element_type=F32
        )

    def space_forms(position):
        index = item_index[position]
        left = item_left[position]
        dist_form[...] = jnp.dot(
            near_left[left, 0:ROWS, 0:48], near_right[index], preferred_element_type=F32
        )
        for k in range(3):
            toward_form[k * ROWS : (k + 1) * ROWS, :] = jnp.dot(
                toward_left[left, k * ROWS : (k + 1) * ROWS, 0:96],
                toward_right[index, :, k * LEAF : (k + 1) * LEAF],
                preferred_element_type=F32,
            )

    def geometry():
        return face_geometry(
            dist_form[...], [toward_form[k * ROWS : (k + 1) * ROWS, :] for k in range(3)]
        )

    def keep_geometry(values):
        for k in range(4):
            geo_form[k * ROWS : (k + 1) * ROWS, :] = values[k]

    def flux_item(position, carry):
        left = item_left[position]
        index = item_index[position]
        coded = item_seat[position]
        other_seat = jnp.where(coded < 0, -1 - coded, coded)
        weight = jnp.where(coded < 0, 0.0, 1.0).astype(F32)
        fluxes = face_fluxes(
            [near_form[k * ROWS : (k + 1) * ROWS, :] for k in range(5)],
            [far_form[:, k * LEAF : (k + 1) * LEAF] for k in range(5)],
            [geo_form[k * ROWS : (k + 1) * ROWS, :] for k in range(3)],
            geo_form[3 * ROWS : 4 * ROWS, :],
            [near_plane[left, k] for k in range(5)],
            [far_half[index, k : k + 1, :] for k in range(5)],
        )
        following = geometry()
        keep_geometry(following)
        state_forms(position + 1)
        space_forms(position + 2)
        for k in range(5):
            row_sum[left, k] += fluxes[k]
            col_sum[other_seat, 8 * k : 8 * k + 8] += weight * sum(
                fluxes[k][8 * j : 8 * j + 8] for j in range(ROWS // 8)
            )
        return carry

    space_forms(0)
    keep_geometry(geometry())
    state_forms(0)
    space_forms(1)
    lax.fori_loop(0, item_count, flux_item, 0)

    def row_total(seat, carry):
        sums = {}
        for c in range(5):
            pieces = [row_sum[seat * splits + part, c] for part in range(splits)]
            turned = jnp.concatenate(pieces, axis=0).T
            sums[c] = jnp.sum(turned, axis=0, keepdims=True)
        row_rate[seat] = stack_rows(sums)
        return carry

    lax.fori_loop(0, length, row_total, 0)
    row_rate[length] = jnp.zeros((8, LEAF), F32)

    def rates(seat, less, leaf, column):
        total = stack_rows(
            {
                k: jnp.sum(col_sum[seat, 8 * k : 8 * k + 8], axis=0, keepdims=True)
                for k in range(5)
            }
        )
        if less is not None:
            total = total - less
        live = tile_of(leaf)[0:1] < 0.5 * AWAY
        scale = AREA_FLOOR * pay[rows_of(seat, 24), :][0:1]
        return lax.rem(column, width), jnp.where(live, total * scale, 0.0)

    def write_own(k, carry):
        column, value = rates(k, row_rate[k], width + k, base + k)
        for c in range(5):
            own_out[pl.ds(c * width + column, 1), :] = value[c : c + 1]
        return carry

    def write_upper(k, carry):
        column, value = rates(up + k, None, 2 * width + k, upper_base + k)
        for c in range(5):
            next_out[pl.ds(c * width + column, 1), :] = value[c : c + 1]
        return carry

    lax.fori_loop(0, length + 1, write_own, 0)
    lax.fori_loop(0, length + 2, write_upper, 0)


def shards(positions, velocity, density, pressure, counts, pair_list):
    width = counts.shape[0]
    slots = pair_list.shape[1]
    particles = width * LEAF
    sub_count = lax.axis_size("sub")
    leaf_sub = width // sub_count

    smem = pl.BlockSpec(memory_space=pltpu.SMEM)
    vmem = pl.BlockSpec(memory_space=pltpu.VMEM)
    lanes = -(-(slots + max(leaf_sub + 1, width)) // LEAF) * LEAF
    state, listed = pl.pallas_call(
        functools.partial(pack_kernel, width, leaf_sub),
        out_shape=[
            jax.ShapeDtypeStruct((8, particles), F32),
            jax.ShapeDtypeStruct((4, lanes), F32),
        ],
        in_specs=[smem, vmem, vmem, vmem, vmem, vmem, vmem],
        out_specs=[vmem, vmem],
        name="pack",
    )(
        counts,
        counts[None],
        positions,
        velocity,
        density[None],
        pressure[None],
        pair_list,
    )
    kept_state, kept_listed = lax.optimization_barrier(
        (jnp.where(state == state, state, 0.0), jnp.where(listed == listed, listed, 0.0))
    )
    lists = jnp.stack([shifted(listed, "slab", 1), kept_listed, shifted(listed, "slab", -1)])[None]
    lower = shifted(state, "slab", 1)
    upper = shifted(state, "slab", -1)
    beyond = shifted(state, "slab", -2)
    mask = 1
    while mask < sub_count:
        lists = jnp.concatenate([lists, swapped(lists, "sub", mask)], axis=0)
        mask *= 2
    rec = lists.astype(jnp.int32).reshape(-1)
    cap = -(-2 * leaf_sub // 4) * 4
    most = cap * CAND
    splits = LEAF // ROWS
    seats = 2 * upper_seat_of(cap)

    own_part, next_part = pl.pallas_call(
        functools.partial(step_kernel, width, sub_count, slots),
        out_shape=[jax.ShapeDtypeStruct((5 * width, LEAF), F32)] * 2,
        in_specs=[smem, vmem, vmem, vmem, vmem],
        out_specs=[vmem, vmem],
        scratch_shapes=[
            pltpu.SMEM((3 * sub_count * slots + 2 * UNROLL,), jnp.int32),
            pltpu.SMEM((most + 3,), jnp.int32),
            pltpu.SMEM((7 * width + 1,), jnp.int32),
            pltpu.SMEM((width,), jnp.int32),
        ]
        + [pltpu.SMEM((most * splits + 2,), jnp.int32)] * 3
        + [
            pltpu.SMEM((4 * width,), jnp.int32),
            pltpu.VMEM(((4 * width + 1) * 8, LEAF), F32),
            pltpu.VMEM(((4 * width + 1) * 32, LEAF), F32),
            pltpu.VMEM((seats * 24, LEAF), F32),
            pltpu.VMEM((seats * 64, LEAF), F32),
            pltpu.VMEM((cap * splits, 6 * ROWS, LEAF), BF16),
            pltpu.VMEM((cap * splits, ROWS, LEAF), BF16),
            pltpu.VMEM((cap * splits, 3 * ROWS, LEAF), BF16),
            pltpu.VMEM((cap * splits, 5, ROWS, LEAF), F32),
            pltpu.VMEM((most, 48, LEAF), BF16),
            pltpu.VMEM((most, 48, 5 * LEAF), BF16),
            pltpu.VMEM((most, 96, 3 * LEAF), BF16),
            pltpu.VMEM((most, 8, LEAF), F32),
            pltpu.VMEM((48, 5 * LEAF), BF16),
            pltpu.VMEM((UNROLL, LEAF, LEAF), F32),
            pltpu.VMEM((5 * ROWS, LEAF), F32),
            pltpu.VMEM((ROWS, 5 * LEAF), F32),
            pltpu.VMEM((3 * ROWS, LEAF), F32),
            pltpu.VMEM((ROWS, LEAF), F32),
            pltpu.VMEM((4 * ROWS, LEAF), F32),
            pltpu.VMEM((seats, 40, LEAF), F32),
            pltpu.VMEM((cap * splits, 5, ROWS, LEAF), F32),
            pltpu.VMEM((cap + 1, 8, LEAF), F32),
        ],
        compiler_params=pltpu.CompilerParams(vmem_limit_bytes=48 * 1024 * 1024),
        name="hydro_step",
    )(rec, lower, kept_state, upper, beyond)

    merged = own_part + shifted(next_part, "slab", 1)
    mask = 1
    while mask < sub_count:
        merged = merged + swapped(merged, "sub", mask)
        mask *= 2
    return merged.reshape(5, particles)


def solution(mesh):
    placed = (
        P(None, "slab"),
        P(None, "slab"),
        P("slab"),
        P("slab"),
        P("slab"),
        P(None, ("slab", "sub")),
    )
    return jax.shard_map(
        shards, mesh=mesh, in_specs=placed, out_specs=P(None, "slab"), check_vma=False
    )
```

```python
import functools
import math

import jax
import jax.numpy as jnp
from jax import lax
from jax.experimental import pallas as pl
from jax.experimental.pallas import tpu as pltpu
from jax.sharding import PartitionSpec as P

LEAF = 128
CAND = 5

GAMMA = 5.0 / 3.0
SUPPORT = 1.5
KERNEL_NORM = 21.0 / (2.0 * math.pi * SUPPORT**3)
MOMENT_REG = 0.05
AREA_FLOOR = 0.0001
AWAY = 64.0
UNROLL = 16
ROWS = 64
ROWS_LOG = 6
COST_LEAF, COST_SLOT, COST_PART = 17, 3, 5
F32 = jnp.float32
BF16 = jnp.bfloat16


def shifted(shard, axis, by):
    peers = lax.axis_size(axis)
    return lax.ppermute(shard, axis, [(i, (i + by) % peers) for i in range(peers)])


def swapped(shard, axis, mask):
    peers = lax.axis_size(axis)
    return lax.ppermute(shard, axis, [(i, i ^ mask) for i in range(peers)])


def reciprocal(value):
    return pl.reciprocal(value, approx=True)


def smoothing_of(dist_sq, scale):
    safe = jnp.maximum(dist_sq, 1e-12)
    radius = safe * lax.rsqrt(safe)
    inside = jnp.maximum(1.0 - radius, 0.0)
    square = inside * inside
    return (square * square) * (scale + (scale * 4.0) * radius)


def split_three(value):
    high = value.astype(BF16).astype(F32)
    rest = value - high
    middle = rest.astype(BF16).astype(F32)
    return high, middle, rest - middle


def stack_near(rows):
    high, middle, low = split_three(rows)
    return jnp.concatenate([high, high, high, middle, middle, low], axis=0).astype(BF16)


def stack_far(rows):
    high, middle, low = split_three(rows)
    return jnp.concatenate([high, middle, low, high, middle, high], axis=0).astype(BF16)


def bilinear(near_rows, far_rows):
    return lax.dot_general(
        stack_near(near_rows),
        stack_far(far_rows),
        (((0,), (0,)), ((), ())),
        preferred_element_type=F32,
    )


def moment_features(tile):
    row = lax.broadcasted_iota(jnp.int32, tile.shape, 0)
    by_x = tile * tile[0:1]
    by_y = jnp.where(row == 0, 1.0, tile * tile[1:2])
    by_z = tile * tile[2:3]
    whole = jnp.concatenate([tile, by_x, by_y, by_z], axis=0)
    high = whole.astype(BF16)
    low = (whole - high.astype(F32)).astype(BF16)
    both = jnp.concatenate([high, low], axis=0)
    return jnp.concatenate([both, both], axis=1)


def displacement(step_x, step_y, wrap):
    row = lax.broadcasted_iota(jnp.int32, (8, LEAF), 0)
    zero = jnp.zeros((8, LEAF), F32)
    out = jnp.where(row == 0, step_x, zero)
    out = jnp.where(row == 1, step_y, out)
    return jnp.where(row == 4, -wrap, out)


def finish_leaves(raw, tile):
    pos = [tile(k) for k in range(3)]
    live = pos[0] < 0.5 * AWAY
    total = raw(16)
    first = [raw(k) - pos[k] * total for k in range(3)]

    def second(left, right):
        lead = raw(8 + 8 * left + right)
        return lead - pos[left] * raw(right) - pos[right] * first[left]

    density = jnp.where(live, total, 1.0)
    inverse_density = 1.0 / density

    def scaled(value):
        return jnp.where(live, value * inverse_density, 0.0)

    exx = scaled(second(0, 0)) + MOMENT_REG
    exy = scaled(second(0, 1))
    exz = scaled(second(0, 2))
    eyy = scaled(second(1, 1)) + MOMENT_REG
    eyz = scaled(second(1, 2))
    ezz = scaled(second(2, 2)) + MOMENT_REG
    mxx = eyy * ezz - eyz * eyz
    mxy = exz * eyz - exy * ezz
    mxz = exy * eyz - exz * eyy
    myy = exx * ezz - exz * exz
    myz = exy * exz - exx * eyz
    mzz = exx * eyy - exy * exy
    scale = 1.0 / (exx * mxx + exy * mxy + exz * mxz)
    inverse = [entry * scale for entry in (mxx, mxy, mxz, myy, myz, mzz)]
    square = inverse_density * inverse_density
    rows = [density] + [entry * square for entry in inverse]
    for quantity in range(3, 8):
        value = tile(quantity)
        along = [
            scaled(
                raw(8 + 8 * k + quantity)
                - pos[k] * raw(quantity)
                - value * first[k]
            )
            for k in range(3)
        ]
        half = [0.5 * term for term in along]
        rows.append(inverse[0] * half[0] + inverse[1] * half[1] + inverse[2] * half[2])
        rows.append(inverse[1] * half[0] + inverse[3] * half[1] + inverse[4] * half[2])
        rows.append(inverse[2] * half[0] + inverse[4] * half[1] + inverse[5] * half[2])
    return rows


def dot3(left, right):
    return left[0] * right[0] + left[1] * right[1] + left[2] * right[2]


def apply_sym(matrix, vector):
    return [
        dot3((matrix[0], matrix[1], matrix[2]), vector),
        dot3((matrix[1], matrix[3], matrix[4]), vector),
        dot3((matrix[2], matrix[4], matrix[5]), vector),
    ]


def stack_rows(rows):
    row = lax.broadcasted_iota(jnp.int32, (8, LEAF), 0)
    out = jnp.zeros((8, LEAF), F32)
    for k, entry in rows.items():
        out = jnp.where(row == k, entry, out)
    return out


def near_coefficients(tile, pay):
    pos = [tile[k : k + 1] for k in range(3)]
    twice = [(-2.0 / SUPPORT**2) * entry for entry in pos]
    out = [
        {
            0: dot3(pos, pos) * (1.0 / SUPPORT**2),
            1: twice[0],
            2: twice[1],
            3: twice[2],
            7: 1.0 / SUPPORT**2,
        }
    ]
    matrix = [pay[1 + k : 2 + k] for k in range(6)]
    for line in ((0, 1, 2), (1, 3, 4), (2, 4, 5)):
        entries = [matrix[k] for k in line]
        out.append({0: -dot3(entries, pos), 1: entries[0], 2: entries[1], 3: entries[2]})
    for quantity in range(5):
        slope = [pay[7 + 3 * quantity + k : 8 + 3 * quantity + k] for k in range(3)]
        value = tile[3 + quantity : 4 + quantity]
        if quantity < 3:
            entry = {0: 0.5 * value - dot3(slope, pos), 4 + quantity: -0.5}
        else:
            entry = {0: value - dot3(slope, pos)}
        entry.update({1: slope[0], 2: slope[1], 3: slope[2]})
        out.append(entry)
    return [stack_rows(entry) for entry in out]


def far_coefficients(tile, pay):
    pos = [tile(k) for k in range(3)]
    out = []
    matrix = [pay[1 + k] for k in range(6)]
    for line in ((0, 1, 2), (1, 3, 4), (2, 4, 5)):
        entries = [matrix[k] for k in line]
        out.append({0: dot3(entries, pos), 1: -entries[0], 2: -entries[1], 3: -entries[2]})
    for quantity in range(5):
        slope = [pay[7 + 3 * quantity + k] for k in range(3)]
        value = tile(3 + quantity)
        if quantity < 3:
            entry = {0: 0.5 * value - dot3(slope, pos), 4 + quantity: -0.5}
        else:
            entry = {0: value - dot3(slope, pos)}
        entry.update({1: slope[0], 2: slope[1], 3: slope[2]})
        out.append(entry)
    return out


def limited(value, low, high):
    return jnp.minimum(jnp.maximum(value, low), high)


def face_geometry(dist_sq, toward):
    smooth = smoothing_of(dist_sq, KERNEL_NORM / AREA_FLOOR)
    length_sq = jnp.maximum(dot3(toward, toward), 1e-30)
    inverse_length = lax.rsqrt(length_sq)
    area = smooth * (length_sq * inverse_length)
    scale = jnp.minimum(inverse_length, smooth)
    return [entry * scale for entry in toward] + [area]


def face_fluxes(near_out, far_out, normal, area, near_plain, far_plain):
    left_vel, right_vel = [], []
    for k in range(3):
        high = jnp.abs(far_plain[k] - near_plain[k])
        low = -high
        left_vel.append(limited(near_out[k], low, high))
        right_vel.append(limited(far_out[k], low, high))
    face_vel = [near_plain[k] + far_plain[k] for k in range(3)]
    thermo = []
    for k in range(2):
        low = jnp.minimum(near_plain[3 + k], far_plain[3 + k])
        high = jnp.maximum(near_plain[3 + k], far_plain[3 + k])
        thermo.append(limited(near_out[3 + k], low, high))
        thermo.append(limited(far_out[3 + k], low, high))
    left_rho, right_rho, left_p, right_p = thermo
    left_u = dot3(left_vel, normal)
    right_u = dot3(right_vel, normal)
    left_gp = GAMMA * left_p
    right_gp = GAMMA * right_p
    left_c = left_gp * lax.rsqrt(left_gp * left_rho)
    right_c = right_gp * lax.rsqrt(right_gp * right_rho)
    slow = jnp.minimum(left_u - left_c, right_u - right_c)
    fast = jnp.maximum(left_u + left_c, right_u + right_c)
    left_m = left_rho * (slow - left_u)
    right_m = right_rho * (fast - right_u)
    contact = (right_p - left_p + left_m * left_u - right_m * right_u) * reciprocal(
        left_m - right_m
    )
    is_left = contact >= 0.0
    speed = jnp.where(is_left, jnp.minimum(slow, 0.0), jnp.maximum(fast, 0.0))
    rho = jnp.where(is_left, left_rho, right_rho) * area
    press = jnp.where(is_left, left_p, right_p) * area
    normal_speed = jnp.where(is_left, left_u, right_u)
    vel = [jnp.where(is_left, left_vel[k], right_vel[k]) + face_vel[k] for k in range(3)]
    lag = speed - normal_speed
    ratio = lag * reciprocal(speed - contact)
    through = ratio * contact
    gain = speed * ratio - speed
    push = (rho * lag) * gain
    mass = rho * through
    total_p = press + push
    mom = [mass * vel[k] + total_p * normal[k] for k in range(3)]
    energy = press * (through * (1.0 / (GAMMA - 1.0)) + normal_speed + gain) + push * contact
    energy = energy + (0.5 * mass) * dot3(vel, vel) + total_p * dot3(face_vel, normal)
    return [mass] + mom + [energy]


def pack_kernel(
    width,
    leaf_sub,
    counts,
    counts_row,
    positions,
    velocity,
    density,
    pressure,
    pair_list,
    state,
    listed,
):
    slab = lax.axis_index("slab")
    centre_x = slab.astype(F32) + 0.5
    row = lax.broadcasted_iota(jnp.int32, (3, LEAF), 0)
    lane = lax.broadcasted_iota(jnp.int32, (3, LEAF), 1)

    def one_leaf(column, carry):
        lanes = pl.ds(pl.multiple_of(column * LEAF, LEAF), LEAF)
        centre_y = column.astype(F32) + 0.5
        centre = jnp.where(row == 0, centre_x, jnp.where(row == 1, centre_y, 0.5))
        dead = (row == 0) & (lane >= counts[column])
        state[0:3, lanes] = jnp.where(dead, AWAY, positions[:, lanes] - centre)
        state[3:6, lanes] = velocity[:, lanes]
        state[6:7, lanes] = density[:, lanes]
        state[7:8, lanes] = pressure[:, lanes]
        return carry

    lax.fori_loop(0, width, one_leaf, 0, unroll=4)
    listed[...] = jnp.zeros(listed.shape, F32)
    slots = pair_list.shape[1]
    heads = pair_list[0:1, :]
    tails = pair_list[1:2, :]
    offsets = pair_list[2:3, :]
    occupied = heads >= 0
    head_col = heads - slab * width
    inside = (tails >= slab * width) & (tails < (slab + 1) * width)
    next_slab = lax.rem(slab + 1, lax.axis_size("slab"))
    tail_col = jnp.where(inside, tails - slab * width, tails - next_slab * width)
    outside = occupied & jnp.logical_not(inside)
    wraps = outside & (tails < heads)
    step_y = tail_col + offsets - head_col
    empty = 4 * width
    here = slice(0, slots)
    listed[0:1, here] = jnp.where(occupied, head_col, empty).astype(F32)
    listed[0:1, slots : slots + width] = counts_row[...].astype(F32)
    listed[1:2, here] = jnp.where(
        occupied, jnp.where(inside, tail_col, tail_col + width), empty
    ).astype(F32)
    listed[2:3, here] = jnp.where(occupied, step_y, 0).astype(F32)
    listed[3:4, here] = jnp.where(wraps, 1.0, 0.0)
    seats = head_col - lax.axis_index("sub") * leaf_sub
    behind = lax.broadcasted_iota(jnp.int32, (1, leaf_sub + 1), 1)
    shifts = lax.rem(5 * width * LEAF - offsets, width)
    shift = jnp.max(jnp.where(outside, shifts, 0), axis=1, keepdims=True).astype(F32)
    facts = jnp.where(behind == leaf_sub, shift, 0.0)
    for k in range(leaf_sub):
        found = jnp.where(occupied & (seats == k), 1.0, 0.0)
        facts = jnp.where(behind == k, jnp.sum(found, axis=1, keepdims=True), facts)
    listed[3:4, slots : slots + leaf_sub + 1] = facts


def upper_seat_of(cap):
    return -(-(cap + 2) // 8) * 8


def step_kernel(
    width,
    sub_count,
    slots,
    rec,
    lower_ref,
    own_ref,
    upper_ref,
    beyond_ref,
    own_out,
    next_out,
    order,
    mine,
    need,
    costs,
    item_left,
    item_index,
    item_seat,
    turned_leaf,
    local,
    raw,
    pay,
    far_coef,
    near_left,
    far_left,
    toward_left,
    near_plane,
    near_right,
    far_right,
    toward_right,
    far_half,
    spread,
    dist,
    near_form,
    far_form,
    toward_form,
    dist_form,
    geo_form,
    col_sum,
    row_sum,
    row_rate,
):
    whole = 4 * width
    leaf_sub = width // sub_count
    cap = -(-2 * leaf_sub // 4) * 4
    up = upper_seat_of(cap)
    stride = rec.shape[0] // (12 * sub_count)
    block = 4 * stride

    def count_of(column):
        return rec[block + slots + column]

    def slot_home(slot):
        return rec[slot]

    def slot_other(slot):
        return rec[slot + stride]

    def slot_step_y(slot):
        return rec[slot + 2 * stride].astype(F32)

    def slot_wrap(slot):
        return rec[slot + 3 * stride].astype(F32)

    def clear_need(entry, carry):
        need[entry] = 0
        return carry

    lax.fori_loop(0, 7 * width, clear_need, 0, unroll=16)
    need[7 * width] = 0

    me = lax.axis_index("sub")
    total_cost = jnp.int32(0)
    shift_w = jnp.int32(0)
    for group in range(sub_count):
        seats = jnp.bitwise_xor(me, group) * leaf_sub
        facts = (3 * group + 1) * block + 3 * stride + slots
        shift_w = jnp.maximum(shift_w, rec[facts + leaf_sub])
        for k in range(leaf_sub):
            parts = lax.shift_right_logical(count_of(seats + k) + (ROWS - 1), ROWS_LOG)
            cost = COST_LEAF + rec[facts + k] * (COST_SLOT + COST_PART * parts)
            costs[seats + k] = cost
            total_cost = total_cost + cost

    def deal(column, state):
        owner, length, before, first, mine_length = state
        cost = costs[column]
        middle = sub_count * (2 * before + cost)
        wish = (middle >= 2 * total_cost * (owner + 1)) | (length == cap)
        allowed = (owner < sub_count - 1) & (width - column <= (sub_count - 1 - owner) * cap)
        step = (wish & allowed).astype(jnp.int32)
        owner = owner + step
        length = (1 - step) * length + 1
        is_mine = (owner == me).astype(jnp.int32)
        first = jnp.where((is_mine > 0) & (mine_length == 0), column, first)
        return owner, length, before + cost, first, mine_length + is_mine

    zero = jnp.int32(0)
    _, _, _, base, length = lax.fori_loop(
        0, width, deal, (zero, zero, zero, zero, zero), unroll=4
    )
    upper_base = lax.rem(base + width - 1 + shift_w, width)

    def own_leaf(k):
        return width + lax.rem(base + k, width)

    def upper_leaf(k):
        return 2 * width + lax.rem(upper_base + k, width)

    def mark_own(k, carry):
        need[own_leaf(k)] = jnp.where(k < length, 3, 1)
        return carry

    def mark_upper(k, carry):
        need[upper_leaf(k)] = 1
        return carry

    lax.fori_loop(0, length + 1, mark_own, 0)
    lax.fori_loop(0, length + 2, mark_upper, 0)

    def collect_lower(k, carry):
        used, first = carry
        order[used] = first + k
        return used + (need[slot_other(first + k)] & 1), first

    def collect_own(k, carry):
        used, kept, first = carry
        slot = first + k
        flags = need[width + slot_home(slot)]
        order[used] = slot
        mine[kept] = slot
        used = used + ((flags | need[width + slot_other(slot)]) & 1)
        return used, kept + lax.shift_right_logical(flags, 1), first

    def collect_upper(k, carry):
        used, first = carry
        slot = first + k
        order[used] = slot
        flags = need[2 * width + slot_home(slot)] | need[2 * width + slot_other(slot)]
        return used + (flags & 1), first

    def touches(first, last, start, count):
        ahead = lax.rem(first - start + 4 * width, width) < count
        return ahead | (lax.rem(start - first + 4 * width, width) <= last - first)

    used, kept = zero, zero
    for group in range(sub_count):
        first = jnp.bitwise_xor(me, group) * leaf_sub
        slot = 3 * group * block
        moved = first + rec[slot + 3 * stride + slots + leaf_sub]
        used = lax.cond(
            touches(moved - 1, moved + leaf_sub, base, length + 1),
            lambda used, slot=slot: lax.fori_loop(
                0, slots, collect_lower, (used, slot), unroll=8
            )[0],
            lambda used: used,
            used,
        )
    from_own = used
    for group in range(sub_count):
        first = jnp.bitwise_xor(me, group) * leaf_sub
        slot = (3 * group + 1) * block
        used, kept = lax.cond(
            touches(first - 1, first + leaf_sub, base - 1, length + 2),
            lambda used, kept, slot=slot: lax.fori_loop(
                0, slots, collect_own, (used, kept, slot), unroll=8
            )[0:2],
            lambda used, kept: (used, kept),
            used,
            kept,
        )
    from_upper = used
    for group in range(sub_count):
        first = jnp.bitwise_xor(me, group) * leaf_sub
        slot = (3 * group + 2) * block
        used = lax.cond(
            touches(first, first + leaf_sub, upper_base, length + 2),
            lambda used, slot=slot: lax.fori_loop(
                0, slots, collect_upper, (used, slot), unroll=8
            )[0],
            lambda used: used,
            used,
        )
    for extra in range(2 * UNROLL):
        order[used + extra] = -1

    def rows_of(leaf, count):
        return pl.ds(pl.multiple_of(leaf * count, count), count)

    def load_leaf(column, carry):
        lanes = pl.ds(pl.multiple_of(column * LEAF, LEAF), LEAF)
        places = (
            column,
            width + lax.rem(column - base + width, width),
            2 * width + lax.rem(column - upper_base + width, width),
            3 * width + column,
        )
        for slab, ref in enumerate((lower_ref, own_ref, upper_ref, beyond_ref)):
            local[rows_of(places[slab], 8), :] = ref[:, lanes]
            turned_leaf[slab * width + column] = places[slab]
            raw[rows_of(slab * width + column, 32), :] = jnp.zeros((32, LEAF), F32)
        for k in range(5):
            own_out[pl.ds(k * width + column, 1), :] = jnp.zeros((1, LEAF), F32)
            next_out[pl.ds(k * width + column, 1), :] = jnp.zeros((1, LEAF), F32)
        return carry

    lax.fori_loop(0, width, load_leaf, 0)
    local[rows_of(whole, 8), :] = jnp.zeros((8, LEAF), F32)
    raw[rows_of(whole, 32), :] = jnp.zeros((32, LEAF), F32)

    def tile_of(leaf):
        return local[rows_of(leaf, 8), :]

    def slab_base(position):
        return jnp.where(position < from_own, 0, jnp.where(position < from_upper, width, 2 * width))

    def clear_rows(seat, carry):
        for part in range(LEAF // ROWS):
            for k in range(5):
                row_sum[seat * (LEAF // ROWS) + part, k] = jnp.zeros((ROWS, LEAF), F32)
        return carry

    lax.fori_loop(0, length, clear_rows, 0)

    def clear_cols(seat, carry):
        col_sum[seat] = jnp.zeros((40, LEAF), F32)
        return carry

    lax.fori_loop(0, length + 1, clear_cols, 0)
    lax.fori_loop(up, up + length + 2, clear_cols, 0)

    def slot_tiles(position):
        named = order[position]
        slot = jnp.maximum(named, 0)
        start = slab_base(position)
        other = slot_other(slot)
        shift = displacement(
            jnp.where(other >= width, 1.0, 0.0).astype(F32), slot_step_y(slot), slot_wrap(slot)
        )
        home = jnp.where(named < 0, whole, turned_leaf[jnp.where(named < 0, 0, start + slot_home(slot))])
        other = jnp.where(named < 0, whole, turned_leaf[jnp.where(named < 0, 0, start + other)])
        return home, other, tile_of(home), tile_of(other) + shift, shift

    def distances(group):
        row = lax.broadcasted_iota(jnp.int32, (8, LEAF), 0)
        for k in range(UNROLL):
            _, _, near, far, _ = slot_tiles(group * UNROLL + k)
            near_pos = [near[j : j + 1] for j in range(3)]
            far_pos = [far[j : j + 1] for j in range(3)]
            near_k = jnp.where(
                row < 3,
                near,
                jnp.where(row == 3, dot3(near_pos, near_pos), jnp.where(row == 4, 1.0, 0.0)),
            )
            far_k = jnp.where(
                row < 3,
                (-2.0 / SUPPORT**2) * far,
                jnp.where(
                    row == 4,
                    dot3(far_pos, far_pos) * (1.0 / SUPPORT**2),
                    jnp.where(row == 3, 1.0 / SUPPORT**2, 0.0),
                ),
            )
            dist[k] = bilinear(near_k, far_k)

    def moment_group(group, carry):
        parts = []
        for k in range(UNROLL):
            home, other, near, far, shift = slot_tiles(group * UNROLL + k)
            weight = jnp.where(home == other, 0.5, 1.0).astype(F32)
            smooth = smoothing_of(dist[k], KERNEL_NORM * weight)
            high = smooth.astype(BF16)
            low = (smooth - high.astype(F32)).astype(BF16)
            row_part = lax.dot_general(
                moment_features(far),
                jnp.concatenate([high, low], axis=1),
                (((1,), (1,)), ((), ())),
                preferred_element_type=F32,
            )
            col_part = lax.dot_general(
                moment_features(near - shift),
                jnp.concatenate([high, low], axis=0),
                (((1,), (0,)), ((), ())),
                preferred_element_type=F32,
            )
            parts.append((home, other, row_part, col_part))
        distances(group + 1)
        for home, other, row_part, col_part in parts:
            raw[rows_of(home, 32), :] += row_part[:32] + row_part[32:]
            raw[rows_of(other, 32), :] += col_part[:32] + col_part[32:]
        return carry

    distances(0)
    lax.fori_loop(0, (used + UNROLL - 1) // UNROLL, moment_group, 0)

    def finish(first_leaf, first_seat):
        def tile(k):
            return local[pl.ds(first_leaf * 8 + k, 8, stride=8), :]

        payload = finish_leaves(lambda k: raw[pl.ds(first_leaf * 32 + k, 8, stride=32), :], tile)
        for k, entry in enumerate(payload):
            pay[pl.ds(first_seat * 24 + k, 8, stride=24), :] = entry
        for k, entry in enumerate(far_coefficients(tile, payload)):
            for row in range(8):
                value = jnp.broadcast_to(jnp.asarray(entry.get(row, 0.0), F32), (8, LEAF))
                far_coef[pl.ds(first_seat * 64 + 8 * k + row, 8, stride=64), :] = value

    def finish_own(group, carry):
        finish(width + 8 * group, 8 * group)
        return carry

    def finish_upper(group, carry):
        finish(2 * width + 8 * group, up + 8 * group)
        return carry

    lax.fori_loop(0, (length + 8) // 8, finish_own, 0)
    lax.fori_loop(0, (length + 9) // 8, finish_upper, 0)

    splits = LEAF // ROWS

    picked = lax.broadcasted_iota(jnp.int32, (48, LEAF), 0)
    for k in range(5):
        chosen = (picked == 3 + k) | (picked == 27 + k) | (picked == 43 + k)
        spread[:, k * LEAF : (k + 1) * LEAF] = jnp.where(chosen, 0.5 if k < 3 else 1.0, 0.0).astype(
            BF16
        )

    def turn_home(seat):
        tile = tile_of(width + seat)
        payload = pay[rows_of(seat, 24), :]
        generic = {0: 1.0}
        generic.update({1 + k: tile[k : k + 1] for k in range(6)})
        generic = stack_near(stack_rows(generic))
        coefficients = [stack_near(entry) for entry in near_coefficients(tile, payload)]
        planes = jnp.dot(stack_near(tile).T, spread[...], preferred_element_type=F32)
        turned_far = generic.T
        turned_near = [coefficients[k].T for k in (0, 4, 5, 6, 7, 8)]
        turned_toward = [
            jnp.concatenate([coefficients[1 + k], generic], axis=0).T for k in range(3)
        ]
        for part in range(splits):
            rows = slice(part * ROWS, (part + 1) * ROWS)
            place = seat * splits + part
            for k in range(6):
                near_left[place, k * ROWS : (k + 1) * ROWS, 0:48] = turned_near[k][rows]
            for k in range(3):
                toward_left[place, k * ROWS : (k + 1) * ROWS, 0:96] = turned_toward[k][rows]
            far_left[place, :, 0:48] = turned_far[rows]
            for k in range(5):
                near_plane[place, k] = planes[rows, k * LEAF : (k + 1) * LEAF]

    def turn_four(group, carry):
        for k in range(4):
            turn_home(4 * group + k)
        return carry

    lax.fori_loop(0, (length + 3) // 4, turn_four, 0)

    def prepare_slot(index, count):
        slot = mine[index]
        valid = (index < kept).astype(jnp.int32)
        column = slot_home(slot)
        away = slot_other(slot)
        is_upper = away >= width
        other = width + away
        step_x = jnp.where(is_upper, 1.0, 0.0).astype(F32)
        step_y = slot_step_y(slot)
        wrap = slot_wrap(slot)
        other_seat = jnp.where(
            is_upper,
            up + lax.rem(away - upper_base, width),
            lax.rem(away + width - base, width),
        )
        for part in range(splits):
            item_left[count] = (column - base) * splits + part
            item_index[count] = index
            item_seat[count] = jnp.where(column == away, -1 - other_seat, other_seat)
            count = count + valid * (count_of(column) > part * ROWS).astype(jnp.int32)

        far = tile_of(turned_leaf[other]) + displacement(step_x, step_y, wrap)
        row = lax.broadcasted_iota(jnp.int32, (8, LEAF), 0)
        pos = [far[k : k + 1] for k in range(3)]
        generic = {0: 1.0, 7: dot3(pos, pos)}
        generic.update({1 + k: far[k : k + 1] for k in range(6)})
        generic = stack_far(stack_rows(generic))
        near_right[index] = generic
        for k in range(8):
            entry = far_coef[pl.ds(pl.multiple_of(other_seat * 64 + 8 * k, 8), 8), :]
            change = entry[1:2] * step_x + entry[2:3] * step_y
            if k == 4:
                change = change + 0.5 * wrap
            entry = stack_far(jnp.where(row == 0, entry - change, entry))
            if k < 3:
                toward_right[index, 0:48, k * LEAF : (k + 1) * LEAF] = generic
                toward_right[index, 48:96, k * LEAF : (k + 1) * LEAF] = entry
            else:
                far_right[index, :, (k - 3) * LEAF : (k - 2) * LEAF] = entry
        far_half[index, 0:5] = jnp.concatenate([0.5 * far[3:6], far[6:8]], axis=0)
        return count

    def prepare_four(group, count):
        for k in range(4):
            count = prepare_slot(4 * group + k, count)
        return count

    for extra in range(3):
        mine[kept + extra] = mine[0]
    item_count = lax.fori_loop(0, (kept + 3) // 4, prepare_four, 0)
    for extra in range(2):
        item_left[item_count + extra] = 0
        item_index[item_count + extra] = 0

    def state_forms(position):
        index = item_index[position]
        left = item_left[position]
        near_form[...] = jnp.dot(
            near_left[left, ROWS : 6 * ROWS, 0:48], near_right[index], preferred_element_type=F32
        )
        far_form[...] = jnp.dot(
            far_left[left, :, 0:48], far_right[index], preferred_element_type=F32
        )

    def space_forms(position):
        index = item_index[position]
        left = item_left[position]
        dist_form[...] = jnp.dot(
            near_left[left, 0:ROWS, 0:48], near_right[index], preferred_element_type=F32
        )
        for k in range(3):
            toward_form[k * ROWS : (k + 1) * ROWS, :] = jnp.dot(
                toward_left[left, k * ROWS : (k + 1) * ROWS, 0:96],
                toward_right[index, :, k * LEAF : (k + 1) * LEAF],
                preferred_element_type=F32,
            )

    def geometry():
        return face_geometry(
            dist_form[...], [toward_form[k * ROWS : (k + 1) * ROWS, :] for k in range(3)]
        )

    def keep_geometry(values):
        for k in range(4):
            geo_form[k * ROWS : (k + 1) * ROWS, :] = values[k]

    def flux_item(position, carry):
        left = item_left[position]
        index = item_index[position]
        coded = item_seat[position]
        other_seat = jnp.where(coded < 0, -1 - coded, coded)
        weight = jnp.where(coded < 0, 0.0, 1.0).astype(F32)
        fluxes = face_fluxes(
            [near_form[k * ROWS : (k + 1) * ROWS, :] for k in range(5)],
            [far_form[:, k * LEAF : (k + 1) * LEAF] for k in range(5)],
            [geo_form[k * ROWS : (k + 1) * ROWS, :] for k in range(3)],
            geo_form[3 * ROWS : 4 * ROWS, :],
            [near_plane[left, k] for k in range(5)],
            [far_half[index, k : k + 1, :] for k in range(5)],
        )
        following = geometry()
        keep_geometry(following)
        state_forms(position + 1)
        space_forms(position + 2)
        for k in range(5):
            row_sum[left, k] += fluxes[k]
            col_sum[other_seat, 8 * k : 8 * k + 8] += weight * sum(
                fluxes[k][8 * j : 8 * j + 8] for j in range(ROWS // 8)
            )
        return carry

    space_forms(0)
    keep_geometry(geometry())
    state_forms(0)
    space_forms(1)
    lax.fori_loop(0, item_count, flux_item, 0)

    def row_total(seat):
        sums = {}
        for c in range(5):
            pieces = [row_sum[seat * splits + part, c] for part in range(splits)]
            turned = jnp.concatenate(pieces, axis=0).T
            sums[c] = jnp.sum(turned, axis=0, keepdims=True)
        row_rate[seat] = stack_rows(sums)

    def total_two(pair, carry):
        row_total(2 * pair)
        row_total(2 * pair + 1)
        return carry

    lax.fori_loop(0, (length + 1) // 2, total_two, 0)
    row_rate[length] = jnp.zeros((8, LEAF), F32)

    def rates(seat, less, leaf, column):
        total = stack_rows(
            {
                k: jnp.sum(col_sum[seat, 8 * k : 8 * k + 8], axis=0, keepdims=True)
                for k in range(5)
            }
        )
        if less is not None:
            total = total - less
        live = tile_of(leaf)[0:1] < 0.5 * AWAY
        scale = AREA_FLOOR * pay[rows_of(seat, 24), :][0:1]
        return lax.rem(column, width), jnp.where(live, total * scale, 0.0)

    def write_own(k, carry):
        column, value = rates(k, row_rate[k], width + k, base + k)
        for c in range(5):
            own_out[pl.ds(c * width + column, 1), :] = value[c : c + 1]
        return carry

    def write_upper(k, carry):
        column, value = rates(up + k, None, 2 * width + k, upper_base + k)
        for c in range(5):
            next_out[pl.ds(c * width + column, 1), :] = value[c : c + 1]
        return carry

    lax.fori_loop(0, length + 1, write_own, 0)
    lax.fori_loop(0, length + 2, write_upper, 0)


def shards(positions, velocity, density, pressure, counts, pair_list):
    width = counts.shape[0]
    slots = pair_list.shape[1]
    particles = width * LEAF
    sub_count = lax.axis_size("sub")
    leaf_sub = width // sub_count

    smem = pl.BlockSpec(memory_space=pltpu.SMEM)
    vmem = pl.BlockSpec(memory_space=pltpu.VMEM)
    lanes = -(-(slots + max(leaf_sub + 1, width)) // LEAF) * LEAF
    state, listed = pl.pallas_call(
        functools.partial(pack_kernel, width, leaf_sub),
        out_shape=[
            jax.ShapeDtypeStruct((8, particles), F32),
            jax.ShapeDtypeStruct((4, lanes), F32),
        ],
        in_specs=[smem, vmem, vmem, vmem, vmem, vmem, vmem],
        out_specs=[vmem, vmem],
        name="pack",
    )(
        counts,
        counts[None],
        positions,
        velocity,
        density[None],
        pressure[None],
        pair_list,
    )
    kept_state, kept_listed = lax.optimization_barrier(
        (jnp.where(state == state, state, 0.0), jnp.where(listed == listed, listed, 0.0))
    )
    lists = jnp.stack([shifted(listed, "slab", 1), kept_listed, shifted(listed, "slab", -1)])[None]
    lower = shifted(state, "slab", 1)
    upper = shifted(state, "slab", -1)
    beyond = shifted(state, "slab", -2)
    mask = 1
    while mask < sub_count:
        lists = jnp.concatenate([lists, swapped(lists, "sub", mask)], axis=0)
        mask *= 2
    rec = lists.astype(jnp.int32).reshape(-1)
    cap = -(-2 * leaf_sub // 4) * 4
    most = cap * CAND
    splits = LEAF // ROWS
    seats = 2 * upper_seat_of(cap)

    own_part, next_part = pl.pallas_call(
        functools.partial(step_kernel, width, sub_count, slots),
        out_shape=[jax.ShapeDtypeStruct((5 * width, LEAF), F32)] * 2,
        in_specs=[smem, vmem, vmem, vmem, vmem],
        out_specs=[vmem, vmem],
        scratch_shapes=[
            pltpu.SMEM((3 * sub_count * slots + 2 * UNROLL,), jnp.int32),
            pltpu.SMEM((most + 3,), jnp.int32),
            pltpu.SMEM((7 * width + 1,), jnp.int32),
            pltpu.SMEM((width,), jnp.int32),
        ]
        + [pltpu.SMEM((most * splits + 2,), jnp.int32)] * 3
        + [
            pltpu.SMEM((4 * width,), jnp.int32),
            pltpu.VMEM(((4 * width + 1) * 8, LEAF), F32),
            pltpu.VMEM(((4 * width + 1) * 32, LEAF), F32),
            pltpu.VMEM((seats * 24, LEAF), F32),
            pltpu.VMEM((seats * 64, LEAF), F32),
            pltpu.VMEM((cap * splits, 6 * ROWS, LEAF), BF16),
            pltpu.VMEM((cap * splits, ROWS, LEAF), BF16),
            pltpu.VMEM((cap * splits, 3 * ROWS, LEAF), BF16),
            pltpu.VMEM((cap * splits, 5, ROWS, LEAF), F32),
            pltpu.VMEM((most, 48, LEAF), BF16),
            pltpu.VMEM((most, 48, 5 * LEAF), BF16),
            pltpu.VMEM((most, 96, 3 * LEAF), BF16),
            pltpu.VMEM((most, 8, LEAF), F32),
            pltpu.VMEM((48, 5 * LEAF), BF16),
            pltpu.VMEM((UNROLL, LEAF, LEAF), F32),
            pltpu.VMEM((5 * ROWS, LEAF), F32),
            pltpu.VMEM((ROWS, 5 * LEAF), F32),
            pltpu.VMEM((3 * ROWS, LEAF), F32),
            pltpu.VMEM((ROWS, LEAF), F32),
            pltpu.VMEM((4 * ROWS, LEAF), F32),
            pltpu.VMEM((seats, 40, LEAF), F32),
            pltpu.VMEM((cap * splits, 5, ROWS, LEAF), F32),
            pltpu.VMEM((cap + 1, 8, LEAF), F32),
        ],
        compiler_params=pltpu.CompilerParams(vmem_limit_bytes=48 * 1024 * 1024),
        name="hydro_step",
    )(rec, lower, kept_state, upper, beyond)

    merged = own_part + shifted(next_part, "slab", 1)
    mask = 1
    while mask < sub_count:
        merged = merged + swapped(merged, "sub", mask)
        mask *= 2
    return merged.reshape(5, particles)


def solution(mesh):
    placed = (
        P(None, "slab"),
        P(None, "slab"),
        P("slab"),
        P("slab"),
        P("slab"),
        P(None, ("slab", "sub")),
    )
    return jax.shard_map(
        shards, mesh=mesh, in_specs=placed, out_specs=P(None, "slab"), check_vma=False
    )
```

```python
import functools
import math

import jax
import jax.numpy as jnp
from jax import lax
from jax.experimental import pallas as pl
from jax.experimental.pallas import tpu as pltpu
from jax.sharding import PartitionSpec as P

LEAF = 128
CAND = 5

GAMMA = 5.0 / 3.0
SUPPORT = 1.5
KERNEL_NORM = 21.0 / (2.0 * math.pi * SUPPORT**3)
MOMENT_REG = 0.05
AREA_FLOOR = 0.0001
AWAY = 64.0
UNROLL = 16
ROWS = 64
ROWS_LOG = 6
COST_LEAF, COST_SLOT, COST_PART = 17, 3, 5
F32 = jnp.float32
BF16 = jnp.bfloat16


def shifted(shard, axis, by):
    peers = lax.axis_size(axis)
    return lax.ppermute(shard, axis, [(i, (i + by) % peers) for i in range(peers)])


def swapped(shard, axis, mask):
    peers = lax.axis_size(axis)
    return lax.ppermute(shard, axis, [(i, i ^ mask) for i in range(peers)])


def reciprocal(value):
    return pl.reciprocal(value, approx=True)


def smoothing_of(dist_sq, scale):
    safe = jnp.maximum(dist_sq, 1e-12)
    radius = safe * lax.rsqrt(safe)
    inside = jnp.maximum(1.0 - radius, 0.0)
    square = inside * inside
    return (square * square) * (scale + (scale * 4.0) * radius)


def split_three(value):
    high = value.astype(BF16).astype(F32)
    rest = value - high
    middle = rest.astype(BF16).astype(F32)
    return high, middle, rest - middle


def stack_near(rows):
    high, middle, low = split_three(rows)
    return jnp.concatenate([high, high, high, middle, middle, low], axis=0).astype(BF16)


def stack_far(rows):
    high, middle, low = split_three(rows)
    return jnp.concatenate([high, middle, low, high, middle, high], axis=0).astype(BF16)


def bilinear(near_rows, far_rows):
    return lax.dot_general(
        stack_near(near_rows),
        stack_far(far_rows),
        (((0,), (0,)), ((), ())),
        preferred_element_type=F32,
    )


def moment_features(tile):
    row = lax.broadcasted_iota(jnp.int32, tile.shape, 0)
    by_x = tile * tile[0:1]
    by_y = jnp.where(row == 0, 1.0, tile * tile[1:2])
    by_z = tile * tile[2:3]
    whole = jnp.concatenate([tile, by_x, by_y, by_z], axis=0)
    high = whole.astype(BF16)
    low = (whole - high.astype(F32)).astype(BF16)
    both = jnp.concatenate([high, low], axis=0)
    return jnp.concatenate([both, both], axis=1)


def displacement(step_x, step_y, wrap):
    row = lax.broadcasted_iota(jnp.int32, (8, LEAF), 0)
    zero = jnp.zeros((8, LEAF), F32)
    out = jnp.where(row == 0, step_x, zero)
    out = jnp.where(row == 1, step_y, out)
    return jnp.where(row == 4, -wrap, out)


def finish_leaves(raw, tile):
    pos = [tile(k) for k in range(3)]
    live = pos[0] < 0.5 * AWAY
    total = raw(16)
    first = [raw(k) - pos[k] * total for k in range(3)]

    def second(left, right):
        lead = raw(8 + 8 * left + right)
        return lead - pos[left] * raw(right) - pos[right] * first[left]

    density = jnp.where(live, total, 1.0)
    inverse_density = 1.0 / density

    def scaled(value):
        return jnp.where(live, value * inverse_density, 0.0)

    exx = scaled(second(0, 0)) + MOMENT_REG
    exy = scaled(second(0, 1))
    exz = scaled(second(0, 2))
    eyy = scaled(second(1, 1)) + MOMENT_REG
    eyz = scaled(second(1, 2))
    ezz = scaled(second(2, 2)) + MOMENT_REG
    mxx = eyy * ezz - eyz * eyz
    mxy = exz * eyz - exy * ezz
    mxz = exy * eyz - exz * eyy
    myy = exx * ezz - exz * exz
    myz = exy * exz - exx * eyz
    mzz = exx * eyy - exy * exy
    scale = 1.0 / (exx * mxx + exy * mxy + exz * mxz)
    inverse = [entry * scale for entry in (mxx, mxy, mxz, myy, myz, mzz)]
    square = inverse_density * inverse_density
    rows = [density] + [entry * square for entry in inverse]
    for quantity in range(3, 8):
        value = tile(quantity)
        along = [
            scaled(
                raw(8 + 8 * k + quantity)
                - pos[k] * raw(quantity)
                - value * first[k]
            )
            for k in range(3)
        ]
        half = [0.5 * term for term in along]
        rows.append(inverse[0] * half[0] + inverse[1] * half[1] + inverse[2] * half[2])
        rows.append(inverse[1] * half[0] + inverse[3] * half[1] + inverse[4] * half[2])
        rows.append(inverse[2] * half[0] + inverse[4] * half[1] + inverse[5] * half[2])
    return rows


def dot3(left, right):
    return left[0] * right[0] + left[1] * right[1] + left[2] * right[2]


def apply_sym(matrix, vector):
    return [
        dot3((matrix[0], matrix[1], matrix[2]), vector),
        dot3((matrix[1], matrix[3], matrix[4]), vector),
        dot3((matrix[2], matrix[4], matrix[5]), vector),
    ]


def stack_rows(rows):
    row = lax.broadcasted_iota(jnp.int32, (8, LEAF), 0)
    out = jnp.zeros((8, LEAF), F32)
    for k, entry in rows.items():
        out = jnp.where(row == k, entry, out)
    return out


def near_coefficients(tile, pay):
    pos = [tile[k : k + 1] for k in range(3)]
    twice = [(-2.0 / SUPPORT**2) * entry for entry in pos]
    out = [
        {
            0: dot3(pos, pos) * (1.0 / SUPPORT**2),
            1: twice[0],
            2: twice[1],
            3: twice[2],
            7: 1.0 / SUPPORT**2,
        }
    ]
    matrix = [pay[1 + k : 2 + k] for k in range(6)]
    for line in ((0, 1, 2), (1, 3, 4), (2, 4, 5)):
        entries = [matrix[k] for k in line]
        out.append({0: -dot3(entries, pos), 1: entries[0], 2: entries[1], 3: entries[2]})
    for quantity in range(5):
        slope = [pay[7 + 3 * quantity + k : 8 + 3 * quantity + k] for k in range(3)]
        value = tile[3 + quantity : 4 + quantity]
        if quantity < 3:
            entry = {0: 0.5 * value - dot3(slope, pos), 4 + quantity: -0.5}
        else:
            entry = {0: value - dot3(slope, pos)}
        entry.update({1: slope[0], 2: slope[1], 3: slope[2]})
        out.append(entry)
    return [stack_rows(entry) for entry in out]


def far_coefficients(tile, pay):
    pos = [tile(k) for k in range(3)]
    out = []
    matrix = [pay[1 + k] for k in range(6)]
    for line in ((0, 1, 2), (1, 3, 4), (2, 4, 5)):
        entries = [matrix[k] for k in line]
        out.append({0: dot3(entries, pos), 1: -entries[0], 2: -entries[1], 3: -entries[2]})
    for quantity in range(5):
        slope = [pay[7 + 3 * quantity + k] for k in range(3)]
        value = tile(3 + quantity)
        if quantity < 3:
            entry = {0: 0.5 * value - dot3(slope, pos), 4 + quantity: -0.5}
        else:
            entry = {0: value - dot3(slope, pos)}
        entry.update({1: slope[0], 2: slope[1], 3: slope[2]})
        out.append(entry)
    return out


def limited(value, low, high):
    return jnp.minimum(jnp.maximum(value, low), high)


def face_geometry(dist_sq, toward):
    smooth = smoothing_of(dist_sq, KERNEL_NORM / AREA_FLOOR)
    length_sq = jnp.maximum(dot3(toward, toward), 1e-30)
    inverse_length = lax.rsqrt(length_sq)
    area = smooth * (length_sq * inverse_length)
    scale = jnp.minimum(inverse_length, smooth)
    return [entry * scale for entry in toward] + [area]


def face_fluxes(near_out, far_out, normal, area, near_plain, far_plain):
    left_vel, right_vel = [], []
    for k in range(3):
        high = jnp.abs(far_plain[k] - near_plain[k])
        low = -high
        left_vel.append(limited(near_out[k], low, high))
        right_vel.append(limited(far_out[k], low, high))
    face_vel = [near_plain[k] + far_plain[k] for k in range(3)]
    thermo = []
    for k in range(2):
        low = jnp.minimum(near_plain[3 + k], far_plain[3 + k])
        high = jnp.maximum(near_plain[3 + k], far_plain[3 + k])
        thermo.append(limited(near_out[3 + k], low, high))
        thermo.append(limited(far_out[3 + k], low, high))
    left_rho, right_rho, left_p, right_p = thermo
    left_u = dot3(left_vel, normal)
    right_u = dot3(right_vel, normal)
    left_gp = GAMMA * left_p
    right_gp = GAMMA * right_p
    left_c = left_gp * lax.rsqrt(left_gp * left_rho)
    right_c = right_gp * lax.rsqrt(right_gp * right_rho)
    slow = jnp.minimum(left_u - left_c, right_u - right_c)
    fast = jnp.maximum(left_u + left_c, right_u + right_c)
    left_m = left_rho * (slow - left_u)
    right_m = right_rho * (fast - right_u)
    contact = (right_p - left_p + left_m * left_u - right_m * right_u) * reciprocal(
        left_m - right_m
    )
    is_left = contact >= 0.0
    speed = jnp.where(is_left, jnp.minimum(slow, 0.0), jnp.maximum(fast, 0.0))
    rho = jnp.where(is_left, left_rho, right_rho) * area
    press = jnp.where(is_left, left_p, right_p) * area
    normal_speed = jnp.where(is_left, left_u, right_u)
    vel = [jnp.where(is_left, left_vel[k], right_vel[k]) + face_vel[k] for k in range(3)]
    lag = speed - normal_speed
    ratio = lag * reciprocal(speed - contact)
    through = ratio * contact
    gain = speed * ratio - speed
    push = (rho * lag) * gain
    mass = rho * through
    total_p = press + push
    mom = [mass * vel[k] + total_p * normal[k] for k in range(3)]
    energy = press * (through * (1.0 / (GAMMA - 1.0)) + normal_speed + gain) + push * contact
    energy = energy + (0.5 * mass) * dot3(vel, vel) + total_p * dot3(face_vel, normal)
    return [mass] + mom + [energy]


def pack_kernel(
    width,
    leaf_sub,
    counts,
    counts_row,
    positions,
    velocity,
    density,
    pressure,
    pair_list,
    state,
    listed,
):
    slab = lax.axis_index("slab")
    centre_x = slab.astype(F32) + 0.5
    row = lax.broadcasted_iota(jnp.int32, (3, LEAF), 0)
    lane = lax.broadcasted_iota(jnp.int32, (3, LEAF), 1)

    def one_leaf(column, carry):
        lanes = pl.ds(pl.multiple_of(column * LEAF, LEAF), LEAF)
        centre_y = column.astype(F32) + 0.5
        centre = jnp.where(row == 0, centre_x, jnp.where(row == 1, centre_y, 0.5))
        dead = (row == 0) & (lane >= counts[column])
        state[0:3, lanes] = jnp.where(dead, AWAY, positions[:, lanes] - centre)
        state[3:6, lanes] = velocity[:, lanes]
        state[6:7, lanes] = density[:, lanes]
        state[7:8, lanes] = pressure[:, lanes]
        return carry

    lax.fori_loop(0, width, one_leaf, 0, unroll=4)
    listed[...] = jnp.zeros(listed.shape, F32)
    slots = pair_list.shape[1]
    heads = pair_list[0:1, :]
    tails = pair_list[1:2, :]
    offsets = pair_list[2:3, :]
    occupied = heads >= 0
    head_col = heads - slab * width
    inside = (tails >= slab * width) & (tails < (slab + 1) * width)
    next_slab = lax.rem(slab + 1, lax.axis_size("slab"))
    tail_col = jnp.where(inside, tails - slab * width, tails - next_slab * width)
    outside = occupied & jnp.logical_not(inside)
    wraps = outside & (tails < heads)
    step_y = tail_col + offsets - head_col
    empty = 4 * width
    here = slice(0, slots)
    listed[0:1, here] = jnp.where(occupied, head_col, empty).astype(F32)
    listed[0:1, slots : slots + width] = counts_row[...].astype(F32)
    listed[1:2, here] = jnp.where(
        occupied, jnp.where(inside, tail_col, tail_col + width), empty
    ).astype(F32)
    listed[2:3, here] = jnp.where(occupied, step_y, 0).astype(F32)
    listed[3:4, here] = jnp.where(wraps, 1.0, 0.0)
    seats = head_col - lax.axis_index("sub") * leaf_sub
    behind = lax.broadcasted_iota(jnp.int32, (1, leaf_sub + 1), 1)
    shifts = lax.rem(5 * width * LEAF - offsets, width)
    shift = jnp.max(jnp.where(outside, shifts, 0), axis=1, keepdims=True).astype(F32)
    facts = jnp.where(behind == leaf_sub, shift, 0.0)
    for k in range(leaf_sub):
        found = jnp.where(occupied & (seats == k), 1.0, 0.0)
        facts = jnp.where(behind == k, jnp.sum(found, axis=1, keepdims=True), facts)
    listed[3:4, slots : slots + leaf_sub + 1] = facts


def upper_seat_of(cap):
    return -(-(cap + 2) // 8) * 8


def step_kernel(
    width,
    sub_count,
    slots,
    rec,
    lower_ref,
    own_ref,
    upper_ref,
    beyond_ref,
    own_out,
    next_out,
    order,
    mine,
    need,
    costs,
    item_left,
    item_index,
    item_seat,
    turned_leaf,
    local,
    raw,
    pay,
    far_coef,
    near_left,
    far_left,
    toward_left,
    near_plane,
    near_right,
    far_right,
    toward_right,
    far_half,
    spread,
    dist,
    near_form,
    far_form,
    toward_form,
    dist_form,
    geo_form,
    col_sum,
    row_sum,
    row_rate,
):
    whole = 4 * width
    leaf_sub = width // sub_count
    cap = -(-2 * leaf_sub // 4) * 4
    up = upper_seat_of(cap)
    stride = rec.shape[0] // (12 * sub_count)
    block = 4 * stride

    def count_of(column):
        return rec[block + slots + column]

    def slot_home(slot):
        return rec[slot]

    def slot_other(slot):
        return rec[slot + stride]

    def slot_step_y(slot):
        return rec[slot + 2 * stride].astype(F32)

    def slot_wrap(slot):
        return rec[slot + 3 * stride].astype(F32)

    def clear_need(entry, carry):
        need[entry] = 0
        return carry

    lax.fori_loop(0, 7 * width, clear_need, 0, unroll=16)
    need[7 * width] = 0

    me = lax.axis_index("sub")
    total_cost = jnp.int32(0)
    shift_w = jnp.int32(0)
    for group in range(sub_count):
        seats = jnp.bitwise_xor(me, group) * leaf_sub
        facts = (3 * group + 1) * block + 3 * stride + slots
        shift_w = jnp.maximum(shift_w, rec[facts + leaf_sub])
        for k in range(leaf_sub):
            parts = lax.shift_right_logical(count_of(seats + k) + (ROWS - 1), ROWS_LOG)
            cost = COST_LEAF + rec[facts + k] * (COST_SLOT + COST_PART * parts)
            costs[seats + k] = cost
            total_cost = total_cost + cost

    def deal(column, state):
        owner, length, before, first, mine_length = state
        cost = costs[column]
        middle = sub_count * (2 * before + cost)
        wish = (middle >= 2 * total_cost * (owner + 1)) | (length == cap)
        allowed = (owner < sub_count - 1) & (width - column <= (sub_count - 1 - owner) * cap)
        step = (wish & allowed).astype(jnp.int32)
        owner = owner + step
        length = (1 - step) * length + 1
        is_mine = (owner == me).astype(jnp.int32)
        first = jnp.where((is_mine > 0) & (mine_length == 0), column, first)
        return owner, length, before + cost, first, mine_length + is_mine

    zero = jnp.int32(0)
    _, _, _, base, length = lax.fori_loop(
        0, width, deal, (zero, zero, zero, zero, zero), unroll=4
    )
    upper_base = lax.rem(base + width - 1 + shift_w, width)

    def own_leaf(k):
        return width + lax.rem(base + k, width)

    def upper_leaf(k):
        return 2 * width + lax.rem(upper_base + k, width)

    def mark_own(k, carry):
        need[own_leaf(k)] = jnp.where(k < length, 3, 1)
        return carry

    def mark_upper(k, carry):
        need[upper_leaf(k)] = 1
        return carry

    lax.fori_loop(0, length + 1, mark_own, 0)
    lax.fori_loop(0, length + 2, mark_upper, 0)

    def collect_lower(k, carry):
        used, first = carry
        order[used] = first + k
        return used + (need[slot_other(first + k)] & 1), first

    def collect_own(k, carry):
        used, kept, first = carry
        slot = first + k
        flags = need[width + slot_home(slot)]
        order[used] = slot
        mine[kept] = slot
        used = used + ((flags | need[width + slot_other(slot)]) & 1)
        return used, kept + lax.shift_right_logical(flags, 1), first

    def collect_upper(k, carry):
        used, first = carry
        slot = first + k
        order[used] = slot
        flags = need[2 * width + slot_home(slot)] | need[2 * width + slot_other(slot)]
        return used + (flags & 1), first

    def touches(first, last, start, count):
        ahead = lax.rem(first - start + 4 * width, width) < count
        return ahead | (lax.rem(start - first + 4 * width, width) <= last - first)

    used, kept = zero, zero
    for group in range(sub_count):
        first = jnp.bitwise_xor(me, group) * leaf_sub
        slot = 3 * group * block
        moved = first + rec[slot + 3 * stride + slots + leaf_sub]
        used = lax.cond(
            touches(moved - 1, moved + leaf_sub, base, length + 1),
            lambda used, slot=slot: lax.fori_loop(
                0, slots, collect_lower, (used, slot), unroll=8
            )[0],
            lambda used: used,
            used,
        )
    from_own = used
    for group in range(sub_count):
        first = jnp.bitwise_xor(me, group) * leaf_sub
        slot = (3 * group + 1) * block
        used, kept = lax.cond(
            touches(first - 1, first + leaf_sub, base - 1, length + 2),
            lambda used, kept, slot=slot: lax.fori_loop(
                0, slots, collect_own, (used, kept, slot), unroll=8
            )[0:2],
            lambda used, kept: (used, kept),
            used,
            kept,
        )
    from_upper = used
    for group in range(sub_count):
        first = jnp.bitwise_xor(me, group) * leaf_sub
        slot = (3 * group + 2) * block
        used = lax.cond(
            touches(first, first + leaf_sub, upper_base, length + 2),
            lambda used, slot=slot: lax.fori_loop(
                0, slots, collect_upper, (used, slot), unroll=8
            )[0],
            lambda used: used,
            used,
        )
    for extra in range(2 * UNROLL):
        order[used + extra] = -1

    def rows_of(leaf, count):
        return pl.ds(pl.multiple_of(leaf * count, count), count)

    def load_leaf(column, carry):
        lanes = pl.ds(pl.multiple_of(column * LEAF, LEAF), LEAF)
        places = (
            column,
            width + lax.rem(column - base + width, width),
            2 * width + lax.rem(column - upper_base + width, width),
            3 * width + column,
        )
        for slab, ref in enumerate((lower_ref, own_ref, upper_ref, beyond_ref)):
            local[rows_of(places[slab], 8), :] = ref[:, lanes]
            turned_leaf[slab * width + column] = places[slab]
            raw[rows_of(slab * width + column, 32), :] = jnp.zeros((32, LEAF), F32)
        for k in range(5):
            own_out[pl.ds(k * width + column, 1), :] = jnp.zeros((1, LEAF), F32)
            next_out[pl.ds(k * width + column, 1), :] = jnp.zeros((1, LEAF), F32)
        return carry

    lax.fori_loop(0, width, load_leaf, 0)
    local[rows_of(whole, 8), :] = jnp.zeros((8, LEAF), F32)
    raw[rows_of(whole, 32), :] = jnp.zeros((32, LEAF), F32)

    def tile_of(leaf):
        return local[rows_of(leaf, 8), :]

    def slab_base(position):
        return jnp.where(position < from_own, 0, jnp.where(position < from_upper, width, 2 * width))

    def clear_rows(seat, carry):
        for part in range(LEAF // ROWS):
            for k in range(5):
                row_sum[seat * (LEAF // ROWS) + part, k] = jnp.zeros((ROWS, LEAF), F32)
        return carry

    lax.fori_loop(0, length, clear_rows, 0)

    def clear_cols(seat, carry):
        col_sum[seat] = jnp.zeros((40, LEAF), F32)
        return carry

    lax.fori_loop(0, length + 1, clear_cols, 0)
    lax.fori_loop(up, up + length + 2, clear_cols, 0)

    def slot_tiles(position):
        named = order[position]
        slot = jnp.maximum(named, 0)
        start = slab_base(position)
        other = slot_other(slot)
        shift = displacement(
            jnp.where(other >= width, 1.0, 0.0).astype(F32), slot_step_y(slot), slot_wrap(slot)
        )
        home = jnp.where(named < 0, whole, turned_leaf[jnp.where(named < 0, 0, start + slot_home(slot))])
        other = jnp.where(named < 0, whole, turned_leaf[jnp.where(named < 0, 0, start + other)])
        return home, other, tile_of(home), tile_of(other) + shift, shift

    def distances(group):
        row = lax.broadcasted_iota(jnp.int32, (8, LEAF), 0)
        for k in range(UNROLL):
            _, _, near, far, _ = slot_tiles(group * UNROLL + k)
            near_pos = [near[j : j + 1] for j in range(3)]
            far_pos = [far[j : j + 1] for j in range(3)]
            near_k = jnp.where(
                row < 3,
                near,
                jnp.where(row == 3, dot3(near_pos, near_pos), jnp.where(row == 4, 1.0, 0.0)),
            )
            far_k = jnp.where(
                row < 3,
                (-2.0 / SUPPORT**2) * far,
                jnp.where(
                    row == 4,
                    dot3(far_pos, far_pos) * (1.0 / SUPPORT**2),
                    jnp.where(row == 3, 1.0 / SUPPORT**2, 0.0),
                ),
            )
            dist[k] = bilinear(near_k, far_k)

    def moment_group(group, carry):
        parts = []
        for k in range(UNROLL):
            home, other, near, far, shift = slot_tiles(group * UNROLL + k)
            weight = jnp.where(home == other, 0.5, 1.0).astype(F32)
            smooth = smoothing_of(dist[k], KERNEL_NORM * weight)
            high = smooth.astype(BF16)
            low = (smooth - high.astype(F32)).astype(BF16)
            row_part = lax.dot_general(
                moment_features(far),
                jnp.concatenate([high, low], axis=1),
                (((1,), (1,)), ((), ())),
                preferred_element_type=F32,
            )
            col_part = lax.dot_general(
                moment_features(near - shift),
                jnp.concatenate([high, low], axis=0),
                (((1,), (0,)), ((), ())),
                preferred_element_type=F32,
            )
            parts.append((home, other, row_part, col_part))
        distances(group + 1)
        for home, other, row_part, col_part in parts:
            raw[rows_of(home, 32), :] += row_part[:32] + row_part[32:]
            raw[rows_of(other, 32), :] += col_part[:32] + col_part[32:]
        return carry

    distances(0)
    lax.fori_loop(0, (used + UNROLL - 1) // UNROLL, moment_group, 0)

    def finish(first_leaf, first_seat):
        def tile(k):
            return local[pl.ds(first_leaf * 8 + k, 8, stride=8), :]

        payload = finish_leaves(lambda k: raw[pl.ds(first_leaf * 32 + k, 8, stride=32), :], tile)
        for k, entry in enumerate(payload):
            pay[pl.ds(first_seat * 24 + k, 8, stride=24), :] = entry
        for k, entry in enumerate(far_coefficients(tile, payload)):
            for row in range(8):
                value = jnp.broadcast_to(jnp.asarray(entry.get(row, 0.0), F32), (8, LEAF))
                far_coef[pl.ds(first_seat * 64 + 8 * k + row, 8, stride=64), :] = value

    def finish_own(group, carry):
        finish(width + 8 * group, 8 * group)
        return carry

    def finish_upper(group, carry):
        finish(2 * width + 8 * group, up + 8 * group)
        return carry

    lax.fori_loop(0, (length + 8) // 8, finish_own, 0)
    lax.fori_loop(0, (length + 9) // 8, finish_upper, 0)

    splits = LEAF // ROWS

    picked = lax.broadcasted_iota(jnp.int32, (48, LEAF), 0)
    for k in range(5):
        chosen = (picked == 3 + k) | (picked == 27 + k) | (picked == 43 + k)
        spread[:, k * LEAF : (k + 1) * LEAF] = jnp.where(chosen, 0.5 if k < 3 else 1.0, 0.0).astype(
            BF16
        )

    def turn_home(seat):
        tile = tile_of(width + seat)
        payload = pay[rows_of(seat, 24), :]
        generic = {0: 1.0}
        generic.update({1 + k: tile[k : k + 1] for k in range(6)})
        generic = stack_near(stack_rows(generic))
        coefficients = [stack_near(entry) for entry in near_coefficients(tile, payload)]
        planes = jnp.dot(stack_near(tile).T, spread[...], preferred_element_type=F32)
        turned_far = generic.T
        turned_near = [coefficients[k].T for k in (0, 4, 5, 6, 7, 8)]
        turned_toward = [
            jnp.concatenate([coefficients[1 + k], generic], axis=0).T for k in range(3)
        ]
        for part in range(splits):
            rows = slice(part * ROWS, (part + 1) * ROWS)
            place = seat * splits + part
            for k in range(6):
                near_left[place, k * ROWS : (k + 1) * ROWS, 0:48] = turned_near[k][rows]
            for k in range(3):
                toward_left[place, k * ROWS : (k + 1) * ROWS, 0:96] = turned_toward[k][rows]
            far_left[place, :, 0:48] = turned_far[rows]
            for k in range(5):
                near_plane[place, k] = planes[rows, k * LEAF : (k + 1) * LEAF]

    def turn_four(group, carry):
        for k in range(4):
            turn_home(4 * group + k)
        return carry

    lax.fori_loop(0, (length + 3) // 4, turn_four, 0)

    def prepare_slot(index, count):
        slot = mine[index]
        valid = (index < kept).astype(jnp.int32)
        column = slot_home(slot)
        away = slot_other(slot)
        is_upper = away >= width
        other = width + away
        step_x = jnp.where(is_upper, 1.0, 0.0).astype(F32)
        step_y = slot_step_y(slot)
        wrap = slot_wrap(slot)
        other_seat = jnp.where(
            is_upper,
            up + lax.rem(away - upper_base, width),
            lax.rem(away + width - base, width),
        )
        for part in range(splits):
            item_left[count] = (column - base) * splits + part
            item_index[count] = index
            item_seat[count] = jnp.where(column == away, -1 - other_seat, other_seat)
            count = count + valid * (count_of(column) > part * ROWS).astype(jnp.int32)

        far = tile_of(turned_leaf[other]) + displacement(step_x, step_y, wrap)
        row = lax.broadcasted_iota(jnp.int32, (8, LEAF), 0)
        pos = [far[k : k + 1] for k in range(3)]
        generic = {0: 1.0, 7: dot3(pos, pos)}
        generic.update({1 + k: far[k : k + 1] for k in range(6)})
        generic = stack_far(stack_rows(generic))
        near_right[index] = generic
        for k in range(8):
            entry = far_coef[pl.ds(pl.multiple_of(other_seat * 64 + 8 * k, 8), 8), :]
            change = entry[1:2] * step_x + entry[2:3] * step_y
            if k == 4:
                change = change + 0.5 * wrap
            entry = stack_far(jnp.where(row == 0, entry - change, entry))
            if k < 3:
                toward_right[index, 0:48, k * LEAF : (k + 1) * LEAF] = generic
                toward_right[index, 48:96, k * LEAF : (k + 1) * LEAF] = entry
            else:
                far_right[index, :, (k - 3) * LEAF : (k - 2) * LEAF] = entry
        far_half[index, 0:5] = jnp.concatenate([0.5 * far[3:6], far[6:8]], axis=0)
        return count

    def prepare_four(group, count):
        for k in range(4):
            count = prepare_slot(4 * group + k, count)
        return count

    for extra in range(3):
        mine[kept + extra] = mine[0]
    item_count = lax.fori_loop(0, (kept + 3) // 4, prepare_four, 0)
    for extra in range(2):
        item_left[item_count + extra] = 0
        item_index[item_count + extra] = 0

    def state_forms(position):
        index = item_index[position]
        left = item_left[position]
        near_form[...] = jnp.dot(
            near_left[left, ROWS : 6 * ROWS, 0:48], near_right[index], preferred_element_type=F32
        )
        far_form[...] = jnp.dot(
            far_left[left, :, 0:48], far_right[index], preferred_element_type=F32
        )

    def space_forms(position):
        index = item_index[position]
        left = item_left[position]
        dist_form[...] = jnp.dot(
            near_left[left, 0:ROWS, 0:48], near_right[index], preferred_element_type=F32
        )
        for k in range(3):
            toward_form[k * ROWS : (k + 1) * ROWS, :] = jnp.dot(
                toward_left[left, k * ROWS : (k + 1) * ROWS, 0:96],
                toward_right[index, :, k * LEAF : (k + 1) * LEAF],
                preferred_element_type=F32,
            )

    def geometry():
        return face_geometry(
            dist_form[...], [toward_form[k * ROWS : (k + 1) * ROWS, :] for k in range(3)]
        )

    def keep_geometry(values):
        for k in range(4):
            geo_form[k * ROWS : (k + 1) * ROWS, :] = values[k]

    def flux_item(position, carry):
        left = item_left[position]
        index = item_index[position]
        coded = item_seat[position]
        other_seat = jnp.where(coded < 0, -1 - coded, coded)
        weight = jnp.where(coded < 0, 0.0, 1.0).astype(F32)
        fluxes = face_fluxes(
            [near_form[k * ROWS : (k + 1) * ROWS, :] for k in range(5)],
            [far_form[:, k * LEAF : (k + 1) * LEAF] for k in range(5)],
            [geo_form[k * ROWS : (k + 1) * ROWS, :] for k in range(3)],
            geo_form[3 * ROWS : 4 * ROWS, :],
            [near_plane[left, k] for k in range(5)],
            [far_half[index, k : k + 1, :] for k in range(5)],
        )
        following = geometry()
        keep_geometry(following)
        state_forms(position + 1)
        space_forms(position + 2)
        for k in range(5):
            row_sum[left, k] += fluxes[k]
            col_sum[other_seat, 8 * k : 8 * k + 8] += weight * sum(
                fluxes[k][8 * j : 8 * j + 8] for j in range(ROWS // 8)
            )
        return carry

    space_forms(0)
    keep_geometry(geometry())
    state_forms(0)
    space_forms(1)
    lax.fori_loop(0, item_count, flux_item, 0)

    def row_total(seat):
        sums = {}
        for c in range(5):
            pieces = [row_sum[seat * splits + part, c] for part in range(splits)]
            turned = jnp.concatenate(pieces, axis=0).T
            sums[c] = jnp.sum(turned, axis=0, keepdims=True)
        row_rate[seat] = stack_rows(sums)

    def total_four(group, carry):
        for k in range(4):
            row_total(4 * group + k)
        return carry

    lax.fori_loop(0, (length + 3) // 4, total_four, 0)
    row_rate[length] = jnp.zeros((8, LEAF), F32)

    def rates(seat, less, leaf, column):
        total = stack_rows(
            {
                k: jnp.sum(col_sum[seat, 8 * k : 8 * k + 8], axis=0, keepdims=True)
                for k in range(5)
            }
        )
        if less is not None:
            total = total - less
        live = tile_of(leaf)[0:1] < 0.5 * AWAY
        scale = AREA_FLOOR * pay[rows_of(seat, 24), :][0:1]
        return lax.rem(column, width), jnp.where(live, total * scale, 0.0)

    def write_own(k, carry):
        column, value = rates(k, row_rate[k], width + k, base + k)
        for c in range(5):
            own_out[pl.ds(c * width + column, 1), :] = value[c : c + 1]
        return carry

    def write_upper(k, carry):
        column, value = rates(up + k, None, 2 * width + k, upper_base + k)
        for c in range(5):
            next_out[pl.ds(c * width + column, 1), :] = value[c : c + 1]
        return carry

    lax.fori_loop(0, length + 1, write_own, 0)
    lax.fori_loop(0, length + 2, write_upper, 0)


def shards(positions, velocity, density, pressure, counts, pair_list):
    width = counts.shape[0]
    slots = pair_list.shape[1]
    particles = width * LEAF
    sub_count = lax.axis_size("sub")
    leaf_sub = width // sub_count

    smem = pl.BlockSpec(memory_space=pltpu.SMEM)
    vmem = pl.BlockSpec(memory_space=pltpu.VMEM)
    lanes = -(-(slots + max(leaf_sub + 1, width)) // LEAF) * LEAF
    state, listed = pl.pallas_call(
        functools.partial(pack_kernel, width, leaf_sub),
        out_shape=[
            jax.ShapeDtypeStruct((8, particles), F32),
            jax.ShapeDtypeStruct((4, lanes), F32),
        ],
        in_specs=[smem, vmem, vmem, vmem, vmem, vmem, vmem],
        out_specs=[vmem, vmem],
        name="pack",
    )(
        counts,
        counts[None],
        positions,
        velocity,
        density[None],
        pressure[None],
        pair_list,
    )
    kept_state, kept_listed = lax.optimization_barrier(
        (jnp.where(state == state, state, 0.0), jnp.where(listed == listed, listed, 0.0))
    )
    lists = jnp.stack([shifted(listed, "slab", 1), kept_listed, shifted(listed, "slab", -1)])[None]
    lower = shifted(state, "slab", 1)
    upper = shifted(state, "slab", -1)
    beyond = shifted(state, "slab", -2)
    mask = 1
    while mask < sub_count:
        lists = jnp.concatenate([lists, swapped(lists, "sub", mask)], axis=0)
        mask *= 2
    rec = lists.astype(jnp.int32).reshape(-1)
    cap = -(-2 * leaf_sub // 4) * 4
    most = cap * CAND
    splits = LEAF // ROWS
    seats = 2 * upper_seat_of(cap)

    own_part, next_part = pl.pallas_call(
        functools.partial(step_kernel, width, sub_count, slots),
        out_shape=[jax.ShapeDtypeStruct((5 * width, LEAF), F32)] * 2,
        in_specs=[smem, vmem, vmem, vmem, vmem],
        out_specs=[vmem, vmem],
        scratch_shapes=[
            pltpu.SMEM((3 * sub_count * slots + 2 * UNROLL,), jnp.int32),
            pltpu.SMEM((most + 3,), jnp.int32),
            pltpu.SMEM((7 * width + 1,), jnp.int32),
            pltpu.SMEM((width,), jnp.int32),
        ]
        + [pltpu.SMEM((most * splits + 2,), jnp.int32)] * 3
        + [
            pltpu.SMEM((4 * width,), jnp.int32),
            pltpu.VMEM(((4 * width + 1) * 8, LEAF), F32),
            pltpu.VMEM(((4 * width + 1) * 32, LEAF), F32),
            pltpu.VMEM((seats * 24, LEAF), F32),
            pltpu.VMEM((seats * 64, LEAF), F32),
            pltpu.VMEM((cap * splits, 6 * ROWS, LEAF), BF16),
            pltpu.VMEM((cap * splits, ROWS, LEAF), BF16),
            pltpu.VMEM((cap * splits, 3 * ROWS, LEAF), BF16),
            pltpu.VMEM((cap * splits, 5, ROWS, LEAF), F32),
            pltpu.VMEM((most, 48, LEAF), BF16),
            pltpu.VMEM((most, 48, 5 * LEAF), BF16),
            pltpu.VMEM((most, 96, 3 * LEAF), BF16),
            pltpu.VMEM((most, 8, LEAF), F32),
            pltpu.VMEM((48, 5 * LEAF), BF16),
            pltpu.VMEM((UNROLL, LEAF, LEAF), F32),
            pltpu.VMEM((5 * ROWS, LEAF), F32),
            pltpu.VMEM((ROWS, 5 * LEAF), F32),
            pltpu.VMEM((3 * ROWS, LEAF), F32),
            pltpu.VMEM((ROWS, LEAF), F32),
            pltpu.VMEM((4 * ROWS, LEAF), F32),
            pltpu.VMEM((seats, 40, LEAF), F32),
            pltpu.VMEM((cap * splits, 5, ROWS, LEAF), F32),
            pltpu.VMEM((cap + 1, 8, LEAF), F32),
        ],
        compiler_params=pltpu.CompilerParams(vmem_limit_bytes=48 * 1024 * 1024),
        name="hydro_step",
    )(rec, lower, kept_state, upper, beyond)

    merged = own_part + shifted(next_part, "slab", 1)
    mask = 1
    while mask < sub_count:
        merged = merged + swapped(merged, "sub", mask)
        mask *= 2
    return merged.reshape(5, particles)


def solution(mesh):
    placed = (
        P(None, "slab"),
        P(None, "slab"),
        P("slab"),
        P("slab"),
        P("slab"),
        P(None, ("slab", "sub")),
    )
    return jax.shard_map(
        shards, mesh=mesh, in_specs=placed, out_specs=P(None, "slab"), check_vma=False
    )
```
